128 devices in a mesh: section: 8 (over x_hi, y), ctx: 16 (over z, x_lo, core).
Axes of the slice: x: 4 (x_hi: 2, x_lo: 2; x = x_hi * 2 + x_lo), y: 4, z: 4, core: 2. Of those that a mesh axis runs over, the one named last changes fastest.
Arguments:
- down_in: bfloat16 [8, 2048, 4096], P('section', 'ctx')
- up_in: bfloat16 [8, 2048, 4096], P('section', 'ctx')
- down_cot: bfloat16 [8, 2048, 4096], P('section', 'ctx'), may hold values from -6 to 6
- up_cot: bfloat16 [8, 2048, 4096], P('section', 'ctx'), may hold values from -6 to 6
- kv_weight: bfloat16 [2, 8, 4096, 1024], P(None, 'section'), as said below
- norm_gain: float32 [2, 8, 4096], P(None, 'section'), as said below
- span_ids: int32 [16], replicated, may hold values from 0 to 15, each once
Outputs:
- down_out: bfloat16 [8, 2048, 4096], P('section', 'ctx')
- up_out: bfloat16 [8, 2048, 4096], P('section', 'ctx')
- down_grad: bfloat16 [8, 2048, 4096], P('section', 'ctx')
- up_grad: bfloat16 [8, 2048, 4096], P('section', 'ctx')
- kv_grad: float32 [8, 4096, 1024], P('section', 'ctx')
- gain_grad: float32 [8, 4096], P('section', 'ctx')
The draws below stay inside these ranges and needn't reach their ends.
Inputs may be any that keep to these rules, and one draw needn't show every extreme that they name: kv_weight[1, s] equals kv_weight[0, 7 - s]: copy 1 is the layer of the mirrored section. norm_gain[1, s] equals norm_gain[0, 7 - s]; all entries are positive.
All inputs are finite; a program needn't handle non-finite values.
Results may differ from the reference program's by a relative error of at most 0.027.
Values may be sent and summed in bfloat16 or wider, within the bound.
A program may use at most 192 MiB of HBM per device.

```python
import jax
import jax.numpy as jnp
from jax import lax

D = 4096
HEAD = 128
KV_HEADS = 4
TOK_DEV = 128
SECTIONS = 8
SPANS = 16
TOKENS = 2048
KVW = 1024
N_CTX = 16


def draw_down_in(key, part):
    key = jax.random.fold_in(key, 5)
    values = jnp.clip(jax.random.normal(key, (SECTIONS, TOKENS, D), jnp.float32), -6.0, 6.0)
    return values.astype(jnp.bfloat16)


def draw_up_in(key, part):
    key = jax.random.fold_in(key, 7)
    values = jnp.clip(jax.random.normal(key, (SECTIONS, TOKENS, D), jnp.float32), -6.0, 6.0)
    return values.astype(jnp.bfloat16)


def draw_kv_weight(key, part):
    key = jax.random.fold_in(key, 11)
    base = jax.random.normal(key, (SECTIONS, D, KVW), jnp.float32) * D ** (-0.5)
    return jnp.stack([base, base[::-1]]).astype(jnp.bfloat16)


def draw_norm_gain(key, part):
    key = jax.random.fold_in(key, 23)
    base = 1.0 + 0.25 * jnp.clip(jax.random.normal(key, (SECTIONS, D), jnp.float32), -2.4, 2.4)
    return jnp.stack([base, base[::-1]]).astype(jnp.float32)


def levels(own_key, shape, cuts, low, top_value):
    level, own = 1.0, jax.random.fold_in(own_key, 6)
    for dim, blocks in cuts:
        steps = jnp.exp(jax.random.uniform(jax.random.fold_in(own, dim), (blocks,), jnp.float32, low / len(cuts), top_value / len(cuts)))
        level = level * jnp.repeat(steps, shape[dim] // blocks).reshape([-1 if axis == dim else 1 for axis in range(len(shape))])
    return level


def gaussian(rng, dims, scale, most, cuts=(), held_as=jnp.bfloat16):
    array = jax.random.normal(rng, dims, jnp.float32) * scale
    if len(cuts) > 0:
        array = levels(rng, dims, cuts, -0.22, 0.18) * array
    return jnp.clip(array, min=-most, max=most).astype(held_as)


def setup_inputs(seed: int = 0) -> dict:
    key_of = jax.random.split(jax.random.key(seed), 8)
    return {
        "down_in": draw_down_in(jax.random.fold_in(key_of[7], 71), 0),
        "up_in": draw_up_in(jax.random.fold_in(key_of[7], 71), 0),
        "down_cot": gaussian(key_of[2], (SECTIONS, TOKENS, D), 1.0, 6.0, ((0, 8), (1, 16))),
        "up_cot": gaussian(key_of[3], (SECTIONS, TOKENS, D), 1.0, 6.0, ((0, 8), (1, 16))),
        "kv_weight": draw_kv_weight(jax.random.fold_in(key_of[7], 71), 0),
        "norm_gain": draw_norm_gain(jax.random.fold_in(key_of[7], 71), 0),
        "span_ids": jax.random.permutation(key_of[6], SPANS).astype(jnp.int32),
    }


EPS = 1e-05

def rounded(value):
    return lax.optimization_barrier(value.astype(jnp.bfloat16)).astype(jnp.float32)

def positions(span_ids):
    steps = jnp.arange(TOK_DEV, dtype=jnp.int32)
    return (span_ids.astype(jnp.int32)[:, None] * TOK_DEV + steps[None, :]).reshape(-1).astype(jnp.int32)

def layer_pass(x, cot, gain, weight, span_ids):
    group = D // (KV_HEADS * HEAD)
    half = KVW // 2
    scale = HEAD ** (-0.5)
    xf = x.astype(jnp.float32)
    recip = lax.rsqrt(lax.optimization_barrier(jnp.mean(xf * xf, -1, keepdims=True)) + EPS)
    normed = xf * recip
    act = (normed * gain[None, :]).astype(jnp.bfloat16)
    kv = jnp.dot(act, weight, preferred_element_type=jnp.float32).astype(jnp.bfloat16)
    keys = kv[:, :half].reshape(TOKENS, KV_HEADS, HEAD).astype(jnp.float32)
    vals = kv[:, half:].reshape(TOKENS, KV_HEADS, HEAD).astype(jnp.float32)
    key_pos = positions(span_ids)
    dyf = cot.astype(jnp.float32)

    def query_block(dkv_sum, span):
        start = (span * TOK_DEV).astype(jnp.int32)
        query = lax.dynamic_slice_in_dim(act, start, TOK_DEV, 0).astype(jnp.float32)
        query = query.reshape(TOK_DEV, KV_HEADS, group, HEAD)
        query_pos = lax.dynamic_slice_in_dim(key_pos, start, TOK_DEV, 0)
        visible = key_pos[None, :] <= query_pos[:, None]
        scores = jnp.einsum('tkgd,nkd->kgtn', query, keys) * scale
        top = lax.optimization_barrier(jnp.max(jnp.where(visible, scores, -1e+30), -1, keepdims=True))
        expo = jnp.where(visible, jnp.exp(scores - top), 0.0)
        total = lax.optimization_barrier(jnp.sum(expo, -1, keepdims=True))
        mixed = jnp.einsum('kgtn,nkd->tkgd', rounded(expo), vals) / jnp.transpose(total, (2, 0, 1, 3))
        lse = top + jnp.log(total)
        dout = lax.dynamic_slice_in_dim(dyf, start, TOK_DEV, 0).reshape(TOK_DEV, KV_HEADS, group, HEAD)
        delta = jnp.transpose(lax.optimization_barrier(jnp.sum(dout * mixed, -1)), (1, 2, 0))
        prob = jnp.where(visible, jnp.exp(scores - lse), 0.0)
        dprob = jnp.einsum('tkgd,nkd->kgtn', dout, vals)
        dscore = rounded(prob * (dprob - delta[..., None]) * scale)
        dquery = jnp.einsum('kgtn,nkd->tkgd', dscore, keys)
        dkey = jnp.einsum('kgtn,tkgd->nkd', dscore, query)
        dval = jnp.einsum('kgtn,tkgd->nkd', rounded(prob), dout)
        part = jnp.concatenate([dkey.reshape(TOKENS, half), dval.reshape(TOKENS, half)], 1)
        return (dkv_sum + rounded(part), (mixed.reshape(TOK_DEV, D), dquery.reshape(TOK_DEV, D)))
    dkv_sum, (mixed_all, dquery_all) = lax.scan(query_block, jnp.zeros((TOKENS, KVW), jnp.float32), jnp.arange(N_CTX, dtype=jnp.int32))
    mixed_all = mixed_all.reshape(TOKENS, D)
    dquery_all = dquery_all.reshape(TOKENS, D)
    out = (xf + mixed_all).astype(jnp.bfloat16)
    dkv_b = dkv_sum.astype(jnp.bfloat16)
    dact = dquery_all + lax.dot_general(dkv_b, weight, (((1,), (1,)), ((), ())), preferred_element_type=jnp.float32)

    def span_grads(carry, pieces):
        act_c, dkv_c, dact_c, normed_c = pieces
        wpart = lax.dot_general(act_c, dkv_c, (((0,), (0,)), ((), ())), preferred_element_type=jnp.float32)
        gpart = lax.optimization_barrier(jnp.sum(dact_c * normed_c, 0))
        return ((carry[0] + rounded(wpart), carry[1] + rounded(gpart)), None)
    (dweight, dgain), _ = lax.scan(span_grads, (jnp.zeros((D, KVW), jnp.float32), jnp.zeros((D,), jnp.float32)), (act.reshape(N_CTX, TOK_DEV, D), dkv_b.reshape(N_CTX, TOK_DEV, KVW), dact.reshape(N_CTX, TOK_DEV, D), normed.reshape(N_CTX, TOK_DEV, D)))
    dnormed = dact * gain[None, :]
    dx = (dyf + recip * (dnormed - normed * lax.optimization_barrier(jnp.mean(dnormed * normed, -1, keepdims=True)))).astype(jnp.bfloat16)
    return (out, dx, dweight, dgain)

def reference(down_in, up_in, down_cot, up_cot, kv_weight, norm_gain, span_ids):
    ydown, yup, gdown, gup, wdown, wup, adown, aup = ([], [], [], [], [], [], [], [])
    for section in range(SECTIONS):
        out, dx, dweight, dgain = layer_pass(down_in[section], down_cot[section], norm_gain[0, section], kv_weight[0, section], span_ids)
        ydown.append(out)
        gdown.append(dx)
        wdown.append(dweight)
        adown.append(dgain)
        out, dx, dweight, dgain = layer_pass(up_in[section], up_cot[section], norm_gain[1, section], kv_weight[1, section], span_ids)
        yup.append(out)
        gup.append(dx)
        wup.append(dweight)
        aup.append(dgain)
    down_out = jnp.stack([ydown[(section - 1) % SECTIONS] for section in range(SECTIONS)])
    up_out = jnp.stack([yup[(section + 1) % SECTIONS] for section in range(SECTIONS)])
    kv_grad = jnp.stack([wdown[section] + wup[SECTIONS - 1 - section] for section in range(SECTIONS)])
    gain_grad = jnp.stack([adown[section] + aup[SECTIONS - 1 - section] for section in range(SECTIONS)])
    return (down_out, up_out, jnp.stack(gdown), jnp.stack(gup), kv_grad, gain_grad)
```

```python
import functools

import jax
import jax.numpy as jnp
from jax import lax
from jax.experimental import pallas as pl
from jax.experimental.pallas import tpu as pltpu
from jax.sharding import PartitionSpec as P

LOG2E = 1.4426950408889634
NT = (((1,), (1,)), ((), ()))
TN = (((0,), (0,)), ((), ()))
F32 = jnp.float32
BF = jnp.bfloat16


def stack_heads(block):
    return jnp.concatenate([block[:, j * 128:(j + 1) * 128] for j in range(8)], 0)


def spread_heads(rows):
    return jnp.concatenate([rows[j * 128:(j + 1) * 128] for j in range(8)], 1)


def attention_kernel(kf, kb, bvar, tq_ref, inv_ref, q_ref, dy_ref, kv_hbm, mixed_ref, dq_ref, terms_ref,
                     kv_s, dk_s, dv_s, sems):
    nq = q_ref.shape[0]
    head = pl.program_id(0)
    spans = kv_hbm.shape[0]
    scale = 128 ** -0.5
    c = scale * LOG2E

    @pl.when(head == 0)
    def _():
        copies = [pltpu.make_async_copy(kv_hbm.at[inv_ref[t]], kv_s.at[pl.ds(t * 128, 128)], sems.at[t])
                  for t in range(spans)]
        for cp in copies:
            cp.start()
        for cp in copies:
            cp.wait()

    dk_s[...] = jnp.zeros_like(dk_s)
    dv_s[...] = jnp.zeros_like(dv_s)
    kcol = pl.multiple_of(head * 256, 256)
    vcol = pl.multiple_of(head * 256 + 128, 128)

    def span(qi, _):
        t = tq_ref[qi]
        q = stack_heads(q_ref[qi])
        dy = stack_heads(dy_ref[qi])
        rows = q.shape[0]

        def fwd(b, carry, masked):
            m, l, acc = carry
            at = pl.multiple_of(b * kf, kf)
            k = kv_s[pl.ds(at, kf), pl.ds(kcol, 128)]
            v = kv_s[pl.ds(at, kf), pl.ds(vcol, 128)]
            s = lax.dot_general(q, k, NT, preferred_element_type=F32) * c
            if masked:
                kpos = at + lax.broadcasted_iota(jnp.int32, (128, kf), 1)
                qpos = t * 128 + lax.broadcasted_iota(jnp.int32, (128, kf), 0)
                s = jnp.where((kpos <= qpos)[None], s.reshape(8, 128, kf), -1e30).reshape(rows, kf)
            m_new = jnp.maximum(m, jnp.max(s, 1, keepdims=True))
            e = jnp.exp2(s - m_new)
            fade = jnp.exp2(m - m_new)
            l = l * fade + jnp.sum(e, 1, keepdims=True)
            acc = acc * fade + lax.dot_general(e.astype(BF), v, (((1,), (0,)), ((), ())), preferred_element_type=F32)
            return m_new, l, acc

        nf = (t * 128) // kf
        carry = (jnp.full((rows, 1), -1e30, F32), jnp.zeros((rows, 1), F32), jnp.zeros((rows, 128), F32))
        carry = lax.fori_loop(0, nf, lambda b, cr: fwd(b, cr, False), carry)
        m, l, acc = fwd(nf, carry, True)
        mixed = acc / l
        mixed_ref[qi] = spread_heads(mixed).astype(mixed_ref.dtype)
        lse = m + jnp.log2(l)
        delta = jnp.sum(dy.astype(F32) * mixed, 1, keepdims=True)
        lse_r = jnp.transpose(jnp.broadcast_to(lse, (rows, 128)))[0:1]
        delta_r = jnp.transpose(jnp.broadcast_to(delta, (rows, 128)))[0:1]

        def bwd(b, dq, masked):
            at = pl.multiple_of(b * kb, kb)
            k = kv_s[pl.ds(at, kb), pl.ds(kcol, 128)]
            v = kv_s[pl.ds(at, kb), pl.ds(vcol, 128)]
            s = lax.dot_general(k, q, NT, preferred_element_type=F32) * c
            p = jnp.exp2(s - lse_r)
            if masked:
                kpos = at + lax.broadcasted_iota(jnp.int32, (kb, 128), 0)
                qpos = t * 128 + lax.broadcasted_iota(jnp.int32, (kb, 128), 1)
                vis = kpos <= qpos
                p = jnp.concatenate([jnp.where(vis, p[:, j * 128:(j + 1) * 128], 0.0) for j in range(8)], 1)
            dp = lax.dot_general(v, dy, NT, preferred_element_type=F32)
            ds = (p * (dp - delta_r)).astype(BF)
            dv_s[pl.ds(at, kb)] += jnp.dot(p.astype(BF), dy, preferred_element_type=F32)
            dk_s[pl.ds(at, kb)] += jnp.dot(ds, q, preferred_element_type=F32)
            if bvar == 0:
                return dq + lax.dot_general(ds, k, TN, preferred_element_type=F32)
            return dq + lax.dot_general(k, ds, TN, preferred_element_type=F32)

        nb = (t * 128) // kb
        dq = jnp.zeros((rows, 128) if bvar == 0 else (128, rows), F32)
        dq = lax.fori_loop(0, nb, lambda b, cr: bwd(b, cr, False), dq)
        dq = bwd(nb, dq, True)
        if bvar != 0:
            dq = jnp.transpose(dq)
        dq_ref[qi] = spread_heads(dq * scale).astype(dq_ref.dtype)
        return 0

    lax.fori_loop(0, nq, span, 0)
    for t in range(spans):
        at = pl.ds(pl.multiple_of(inv_ref[t] * 128, 128), 128)
        terms_ref[at, 0:128] = (dk_s[t * 128:(t + 1) * 128] * scale).astype(BF)
        terms_ref[at, 128:256] = dv_s[t * 128:(t + 1) * 128].astype(BF)


def attention(q, dy, kv, tq, inv, kf=512, kb=256, bvar=0, vmem=50 << 20):
    nq, tok, width = q.shape
    nh = width // 1024
    spans = kv.shape[0]
    smem = pl.BlockSpec(memory_space=pltpu.SMEM)
    qspec = pl.BlockSpec((nq, tok, 1024), lambda h: (0, 0, h))
    flops = 2 * 7 * nq * nh * 1024 * spans * 128 * 128
    return pl.pallas_call(
        functools.partial(attention_kernel, kf, kb, bvar),
        grid=(nh,),
        in_specs=[smem, smem, qspec, qspec, pl.BlockSpec(memory_space=pl.ANY)],
        out_specs=[qspec, qspec, pl.BlockSpec((spans * 128, 256), lambda h: (0, h))],
        out_shape=[jax.ShapeDtypeStruct(q.shape, BF), jax.ShapeDtypeStruct(q.shape, BF),
                   jax.ShapeDtypeStruct((spans * 128, nh * 256), BF)],
        scratch_shapes=[pltpu.VMEM((spans * 128, nh * 256), BF), pltpu.VMEM((spans * 128, 128), F32),
                        pltpu.VMEM((spans * 128, 128), F32), pltpu.SemaphoreType.DMA((spans,))],
        compiler_params=pltpu.CompilerParams(vmem_limit_bytes=vmem),
        cost_estimate=pl.CostEstimate(flops=flops, bytes_accessed=16 << 20, transcendentals=0),
        name="attention",
    )(tq, inv, q, dy, kv)


MESH_ID = pl.DeviceIdType.MESH
EPS = 1e-05
DOWN, UP = 0, 1
OWN, PAIR = 0, 1
UNITS = [(UP, OWN), (UP, PAIR), (DOWN, OWN), (DOWN, PAIR)]


class Place:
    def __init__(self):
        self.me = lax.axis_index("ctx")
        self.core = self.me % 2
        self.chip = self.me // 2
        beside = self.chip % 2
        self.partner = self.me + 1 - 2 * self.core
        self.across = self.me + 2 - 4 * beside
        self.above = (self.me + 4) % 16
        self.below = (self.me + 12) % 16
        self.chip_x = self.chip + 1 - 2 * beside

    def greet(self, barrier):
        for dev in (self.partner, self.across, self.above, self.below):
            pl.semaphore_signal(barrier, inc=1, device_id={"ctx": dev}, device_id_type=MESH_ID)
        pl.semaphore_wait(barrier, 4)

    def span(self, chip, kind):
        return 2 * chip + (self.core if kind == OWN else 1 - self.core)

    def up(self, chip, by):
        return (chip + 2 * by) % 8


class Wires:
    def __init__(self, send_sem, recv_sem):
        self.send_sem, self.recv_sem, self.started = send_sem, recv_sem, []

    def copy(self, index, src, dst, dev):
        return pltpu.make_async_remote_copy(
            src_ref=src, dst_ref=dst, send_sem=self.send_sem.at[index], recv_sem=self.recv_sem.at[index],
            device_id={"ctx": dev}, device_id_type=MESH_ID)

    def send(self, index, src, dst, dev):
        copy = self.copy(index, src, dst, dev)
        copy.start()
        self.started.append(copy)

    def arrive(self, index, ref, dev):
        self.copy(index, ref, ref, dev).wait_recv()

    def finish(self):
        for copy in self.started:
            copy.wait_send()


X, ZM, ZP, XZM, XZP, AN, XA = range(7)


def gather_first(place, wires, base, unit, src, slot):
    kind = unit[1]
    at = base + 7 * UNITS.index(unit)
    here = slot(unit, place.chip)
    wires.send(at + X, src, here, place.across)
    wires.send(at + ZM, src, here, place.above)
    wires.send(at + ZP, src, here, place.below)


def gather_second(place, wires, base, unit, slot, landed):
    kind = unit[1]
    at = base + 7 * UNITS.index(unit)
    cx = slot(unit, place.chip_x)
    wires.arrive(at + X, cx, place.across)
    wires.send(at + XZM, cx, cx, place.above)
    wires.send(at + XZP, cx, cx, place.below)
    landed(unit, place.chip_x)
    lo, hi = slot(unit, place.up(place.chip, 3)), slot(unit, place.up(place.chip, 1))
    wires.arrive(at + ZM, lo, place.below)
    if kind == OWN:
        wires.send(at + AN, lo, lo, place.above)
    wires.arrive(at + ZP, hi, place.above)
    if kind == PAIR:
        wires.send(at + AN, hi, hi, place.below)
    landed(unit, place.up(place.chip, 3))
    landed(unit, place.up(place.chip, 1))


def gather_third(place, wires, base, unit, slot, landed):
    at = base + 7 * UNITS.index(unit)
    far = slot(unit, place.up(place.chip, 2))
    wires.arrive(at + AN, far, place.below if unit[1] == OWN else place.above)
    wires.send(at + XA, far, far, place.across)
    landed(unit, place.up(place.chip, 2))
    for kind, by, dev in ((XZM, 3, place.below), (XZP, 1, place.above)):
        chip = place.up(place.chip_x, by)
        wires.arrive(at + kind, slot(unit, chip), dev)
        landed(unit, chip)


def gather_last(place, wires, base, unit, slot, landed):
    at = base + 7 * UNITS.index(unit)
    chip = place.up(place.chip_x, 2)
    wires.arrive(at + XA, slot(unit, chip), place.across)
    landed(unit, chip)


def nothing(unit, chip):
    pass


def spread_kernel(act_d, act_u, cot_d, cot_u, kv_d, kv_u, q_d, q_u, dy_d, dy_u, all_d, all_u,
                  send_sem, recv_sem, local_sem):
    place = Place()
    wires = Wires(send_sem, recv_sem)
    place.greet(pltpu.get_barrier_semaphore())
    all_kv, kv = (all_d, all_u), (kv_d, kv_u)
    tok = act_d.shape[0]
    mine = lambda width: pl.ds(pl.multiple_of(place.core * width, width), width)
    other = lambda width: pl.ds(pl.multiple_of((1 - place.core) * width, width), width)
    slot = lambda unit, chip: all_kv[unit[0]].at[place.span(chip, unit[1])]
    local = []

    def keep(src, dst):
        copy = pltpu.make_async_copy(src, dst, local_sem.at[len(local)])
        copy.start()
        local.append(copy)

    for layer in (UP, DOWN):
        wires.send(28 + layer, kv[layer].at[:, other(512)], all_kv[layer].at[place.me], place.partner)
    for layer in (UP, DOWN):
        gather_first(place, wires, 0, (layer, OWN), kv[layer].at[:, mine(512)], slot)
        keep(kv[layer].at[:, mine(512)], all_kv[layer].at[place.me])
    at = 30
    for src, dst in ((act_u, q_u), (cot_u, dy_u), (act_d, q_d), (cot_d, dy_d)):
        wires.send(at, src.at[:, other(2048)], dst.at[place.core], place.partner)
        keep(src.at[:, mine(2048)], dst.at[place.core])
        at += 1
    for layer in (UP, DOWN):
        wires.arrive(28 + layer, all_kv[layer].at[place.partner], place.partner)
        gather_first(place, wires, 0, (layer, PAIR), slot((layer, PAIR), place.chip), slot)
    for unit in UNITS:
        gather_second(place, wires, 0, unit, slot, nothing)
    for unit in UNITS:
        gather_third(place, wires, 0, unit, slot, nothing)
    for unit in UNITS:
        gather_last(place, wires, 0, unit, slot, nothing)
    at = 30
    for dst in (q_u, dy_u, q_d, dy_d):
        wires.arrive(at, dst.at[1 - place.core], place.partner)
        at += 1
    for copy in local:
        copy.wait()
    wires.finish()


def spread(act_d, act_u, cot_d, cot_u, kv_d, kv_u):
    half = jax.ShapeDtypeStruct((2, 128, 2048), BF)
    whole = jax.ShapeDtypeStruct((16, 128, 512), BF)
    hbm = pl.BlockSpec(memory_space=pl.ANY)
    return pl.pallas_call(
        spread_kernel,
        in_specs=[hbm] * 6,
        out_specs=[hbm] * 6,
        out_shape=[half] * 4 + [whole] * 2,
        scratch_shapes=[pltpu.SemaphoreType.DMA((34,)), pltpu.SemaphoreType.DMA((34,)), pltpu.SemaphoreType.DMA((6,))],
        compiler_params=pltpu.CompilerParams(collective_id=1, has_side_effects=True),
        name="spread",
    )(act_d, act_u, cot_d, cot_u, kv_d, kv_u)


R0, RA, RB, R1, RU, RD, RX = range(7)


def reduce_kernel(terms_d, terms_u, mix_d, mix_u, dq_d, dq_u, mixed_d, mixed_u, dquery_d, dquery_u, all_d, all_u,
                  slots, stage, total, send_sem, recv_sem, local_sem):
    place = Place()
    wires = Wires(send_sem, recv_sem)
    place.greet(pltpu.get_barrier_semaphore())
    terms, all_kv = (terms_d, terms_u), (all_d, all_u)
    mine = pl.ds(pl.multiple_of(place.core * 512, 512), 512)
    wide = pl.ds(pl.multiple_of(place.core * 2048, 2048), 2048)
    chip, chip_x = place.chip, place.chip_x
    local = []

    def term(unit, at):
        return terms[unit[0]].at[pl.ds(pl.multiple_of(place.span(at, unit[1]) * 128, 128), 128)]

    def plus(*refs):
        value = refs[0][...].astype(F32)
        for ref in refs[1:]:
            value = value + ref[...].astype(F32)
        return value.astype(BF)

    for n, unit in enumerate(UNITS):
        at = 7 * n
        wires.send(at + R0, term(unit, place.up(chip_x, 2)), slots.at[at + R0], place.across)
        wires.send(at + RA, term(unit, place.up(chip_x, 1)), slots.at[at + RA], place.above)
        wires.send(at + RB, term(unit, place.up(chip_x, 3)), slots.at[at + RB], place.below)
        if unit[1] == OWN:
            wires.send(at + RD, term(unit, place.up(chip, 1)), slots.at[at + RD], place.above)
        else:
            wires.send(at + RU, term(unit, place.up(chip, 3)), slots.at[at + RU], place.below)
    index = 56 + 32
    for src, dst in ((mix_u, mixed_u), (mix_d, mixed_d), (dq_u, dquery_u), (dq_d, dquery_d)):
        wires.send(index, src.at[1 - place.core], dst.at[:, wide], place.partner)
        copy = pltpu.make_async_copy(src.at[place.core], dst.at[:, wide], local_sem.at[len(local)])
        copy.start()
        local.append(copy)
        index += 1
    for n, unit in enumerate(UNITS):
        at = 7 * n
        wires.arrive(at + R0, slots.at[at + R0], place.across)
        stage[3 * n] = plus(slots.at[at + R0], term(unit, place.up(chip, 2)))
        wires.send(at + R1, stage.at[3 * n], slots.at[at + R1], place.below if unit[1] == OWN else place.above)
    for n, unit in enumerate(UNITS):
        at = 7 * n
        wires.arrive(at + RA, slots.at[at + RA], place.below)
        wires.arrive(at + RB, slots.at[at + RB], place.above)
        stage[3 * n + 1] = plus(slots.at[at + RA], slots.at[at + RB], term(unit, chip_x))
        wires.send(at + RX, stage.at[3 * n + 1], slots.at[at + RX], place.across)
        if unit[1] == OWN:
            wires.arrive(at + R1, slots.at[at + R1], place.above)
            stage[3 * n + 2] = plus(slots.at[at + R1], term(unit, place.up(chip, 3)))
            wires.send(at + RU, stage.at[3 * n + 2], slots.at[at + RU], place.below)
        else:
            wires.arrive(at + R1, slots.at[at + R1], place.below)
            stage[3 * n + 2] = plus(slots.at[at + R1], term(unit, place.up(chip, 1)))
            wires.send(at + RD, stage.at[3 * n + 2], slots.at[at + RD], place.above)

    slot = lambda unit, at: all_kv[unit[0]].at[place.span(at, unit[1]), :, mine]
    passed = [0]

    def hand_over(unit, at):
        ref = slot(unit, at)
        wires.send(56 + passed[0], ref, ref, place.partner)
        passed[0] += 1

    order = []

    def landed(unit, at):
        order.append((unit, at))
        hand_over(unit, at)

    for n, unit in enumerate(UNITS):
        at = 7 * n
        wires.arrive(at + RX, slots.at[at + RX], place.across)
        wires.arrive(at + RU, slots.at[at + RU], place.above)
        wires.arrive(at + RD, slots.at[at + RD], place.below)
        total[n] = plus(slots.at[at + RX], slots.at[at + RU], slots.at[at + RD], term(unit, chip))
        gather_first(place, wires, 28, unit, total.at[n], slot)
        copy = pltpu.make_async_copy(total.at[n], slot(unit, chip), local_sem.at[len(local)])
        copy.start()
        local.append(copy)
        wires.send(56 + passed[0], total.at[n], slot(unit, chip), place.partner)
        order.append((unit, chip))
        passed[0] += 1
    for unit in UNITS:
        gather_second(place, wires, 28, unit, slot, landed)
    for unit in UNITS:
        gather_third(place, wires, 28, unit, slot, landed)
    for unit in UNITS:
        gather_last(place, wires, 28, unit, slot, landed)
    theirs = pl.ds(pl.multiple_of((1 - place.core) * 512, 512), 512)
    for n, (unit, at) in enumerate(order):
        span = place.span(at, 1 - unit[1])
        wires.arrive(56 + n, all_kv[unit[0]].at[span, :, theirs], place.partner)
    index = 56 + 32
    others = pl.ds(pl.multiple_of((1 - place.core) * 2048, 2048), 2048)
    for dst in (mixed_u, mixed_d, dquery_u, dquery_d):
        wires.arrive(index, dst.at[:, others], place.partner)
        index += 1
    for copy in local:
        copy.wait()
    wires.finish()


def reduce_terms(terms_d, terms_u, mix_d, mix_u, dq_d, dq_u):
    hbm = pl.BlockSpec(memory_space=pl.ANY)
    vmem = pl.BlockSpec(memory_space=pltpu.VMEM)
    row = jax.ShapeDtypeStruct((128, 4096), BF)
    whole = jax.ShapeDtypeStruct((16, 128, 1024), BF)
    return pl.pallas_call(
        reduce_kernel,
        in_specs=[vmem] * 2 + [hbm] * 4,
        out_specs=[hbm] * 6,
        out_shape=[row] * 4 + [whole] * 2,
        scratch_shapes=[pltpu.VMEM((28, 128, 512), BF), pltpu.VMEM((12, 128, 512), BF), pltpu.VMEM((4, 128, 512), BF),
                        pltpu.SemaphoreType.DMA((92,)), pltpu.SemaphoreType.DMA((92,)), pltpu.SemaphoreType.DMA((8,))],
        compiler_params=pltpu.CompilerParams(collective_id=2, has_side_effects=True, vmem_limit_bytes=32 << 20),
        name="reduce_terms",
    )(terms_d, terms_u, mix_d, mix_u, dq_d, dq_u)


def mirror_kernel(wu_ref, g_ref, w_out, gd_out, gu_out, parts, mine, send_sem, recv_sem, local_sem):
    me = lax.axis_index("ctx")
    section = lax.axis_index("section")
    barrier = pltpu.get_barrier_semaphore()
    pl.semaphore_signal(barrier, inc=1, device_id={"section": 7 - section}, device_id_type=MESH_ID)
    for step in range(1, 16):
        pl.semaphore_signal(barrier, inc=1, device_id={"ctx": (me + step) % 16}, device_id_type=MESH_ID)
    pl.semaphore_wait(barrier, 16)
    far = pltpu.make_async_remote_copy(src_ref=wu_ref, dst_ref=w_out, send_sem=send_sem.at[0], recv_sem=recv_sem.at[0],
                                       device_id={"section": 7 - section}, device_id_type=MESH_ID)
    far.start()
    copies = []
    for step in range(1, 16):
        to = (me + step) % 16
        copy = pltpu.make_async_remote_copy(
            src_ref=g_ref.at[to], dst_ref=parts.at[step], send_sem=send_sem.at[step], recv_sem=recv_sem.at[step],
            device_id={"ctx": to}, device_id_type=MESH_ID)
        copy.start()
        copies.append(copy)
    value = g_ref[me]
    for step in range(1, 16):
        copies[step - 1].wait_recv()
        value = value + parts[step]
    mine[...] = value
    gd_out[...] = value
    last = pltpu.make_async_remote_copy(src_ref=mine, dst_ref=gu_out, send_sem=send_sem.at[16], recv_sem=recv_sem.at[16],
                                        device_id={"section": 7 - section}, device_id_type=MESH_ID)
    last.start()
    for copy in copies:
        copy.wait_send()
    last.wait()
    far.wait()


def mirror(wu, gains):
    hbm = pl.BlockSpec(memory_space=pl.ANY)
    vmem = pl.BlockSpec(memory_space=pltpu.VMEM)
    small = jax.ShapeDtypeStruct((8, 256), F32)
    return pl.pallas_call(
        mirror_kernel,
        in_specs=[hbm, vmem],
        out_specs=[hbm, vmem, vmem],
        out_shape=[jax.ShapeDtypeStruct(wu.shape, BF), small, small],
        scratch_shapes=[pltpu.VMEM((16, 8, 256), F32), pltpu.VMEM((8, 256), F32),
                        pltpu.SemaphoreType.DMA((17,)), pltpu.SemaphoreType.DMA((17,)), pltpu.SemaphoreType.DMA((1,))],
        compiler_params=pltpu.CompilerParams(collective_id=3, has_side_effects=True),
        name="mirror",
    )(wu, gains)


def by_head(kv):
    return kv.reshape(-1, 2, 4, 128).transpose(0, 2, 1, 3).reshape(-1, 1024)


def by_kind(kv):
    return kv.reshape(-1, 4, 2, 128).transpose(0, 2, 1, 3).reshape(-1, 1024)


def prepare(x, gain, weight):
    xf = x.astype(F32)
    recip = lax.rsqrt(jnp.mean(xf * xf, -1, keepdims=True) + EPS)
    normed = xf * recip
    act = (normed * gain[None, :]).astype(BF)
    kv = jnp.dot(act, weight, preferred_element_type=F32).astype(BF)
    return recip, act, by_head(kv)


def complete(x, recip, cot, gain, weight, dquery, dkv):
    normed = x.astype(F32) * recip
    dact = dquery.astype(F32) + lax.dot_general(by_kind(dkv), weight, NT, preferred_element_type=F32)
    gpart = jnp.sum(dact * normed, 0)
    dnormed = dact * gain[None, :]
    dx = cot.astype(F32) + recip * (dnormed - normed * jnp.mean(dnormed * normed, -1, keepdims=True))
    return dx.astype(BF), gpart


def weight_grad(features, dkv):
    return lax.dot_general(features, dkv, TN, preferred_element_type=F32)


def shifted(array, by):
    size = lax.axis_size("section")
    return lax.ppermute(array, "section", [(i, (i + by) % size) for i in range(size)])


def per_device(down_in, up_in, down_cot, up_cot, kv_weight, norm_gain, span_ids):
    own = lax.axis_index("ctx")
    x_d, x_u, cot_d, cot_u = down_in[0], up_in[0], down_cot[0], up_cot[0]
    gain_d, gain_u = norm_gain[0, 0], norm_gain[1, 0]
    weight_d, weight_u = kv_weight[0, 0], kv_weight[1, 0]
    recip_u, act_u, kv_u = prepare(x_u, gain_u, weight_u)
    recip_d, act_d, kv_d = prepare(x_d, gain_d, weight_d)
    q_d, q_u, dy_d, dy_u, all_d, all_u = spread(act_d, act_u, cot_d, cot_u, kv_d, kv_u)
    features = jnp.stack([act_d, act_u]).reshape(2, 128, 16, 256).transpose(2, 0, 1, 3)
    features = lax.all_to_all(features, "ctx", 0, 0, tiled=False)
    features = features.transpose(1, 0, 2, 3).reshape(2, 2048, 256)
    times = lax.dynamic_slice_in_dim(span_ids, own // 2 * 2, 2, 0)
    inverse = jnp.argsort(span_ids).astype(jnp.int32)
    mix_u, dq_u, terms_u = attention(q_u, dy_u, all_u, times, inverse)
    mix_d, dq_d, terms_d = attention(q_d, dy_d, all_d, times, inverse)
    mixed_d, mixed_u, dquery_d, dquery_u, dkv_d, dkv_u = reduce_terms(terms_d, terms_u, mix_d, mix_u, dq_d, dq_u)
    y_down = (x_d.astype(F32) + mixed_d.astype(F32)).astype(BF)
    y_up = (x_u.astype(F32) + mixed_u.astype(F32)).astype(BF)
    down_out = shifted(y_down, 1)
    up_out = shifted(y_up, -1)
    wgrad_u = weight_grad(features[1], dkv_u.reshape(2048, 1024)).astype(BF)
    own_dkv = lambda dkv: lax.dynamic_index_in_dim(dkv, own, 0, False)
    grad_u, gpart_u = complete(x_u, recip_u, cot_u, gain_u, weight_u, dquery_u, own_dkv(dkv_u))
    grad_d, gpart_d = complete(x_d, recip_d, cot_d, gain_d, weight_d, dquery_d, own_dkv(dkv_d))
    gains = jnp.stack([gpart_d, gpart_u] + [jnp.zeros_like(gpart_d)] * 6).reshape(8, 16, 256).transpose(1, 0, 2)
    mirror_w, gain_here, gain_there = mirror(wgrad_u, gains)
    wgrad_d = weight_grad(features[0], dkv_d.reshape(2048, 1024))
    kv_grad = by_kind(wgrad_d + mirror_w.astype(F32))[None]
    gain_grad = (gain_here[0] + gain_there[1])[None]
    return (down_out[None], up_out[None], grad_d[None], grad_u[None], kv_grad, gain_grad)


def solution(mesh):
    row = P("section", "ctx", None)
    in_specs = (row, row, row, row, P(None, "section", None, None), P(None, "section", None), P())
    out_specs = (row, row, row, row, row, P("section", "ctx"))
    return jax.shard_map(per_device, mesh=mesh, in_specs=in_specs, out_specs=out_specs, check_vma=False)
```

```python
import functools

import jax
import jax.numpy as jnp
from jax import lax
from jax.experimental import pallas as pl
from jax.experimental.pallas import tpu as pltpu
from jax.sharding import PartitionSpec as P

LOG2E = 1.4426950408889634
NT = (((1,), (1,)), ((), ()))
TN = (((0,), (0,)), ((), ()))
F32 = jnp.float32
BF = jnp.bfloat16


def stack_heads(block):
    return jnp.concatenate([block[:, j * 128:(j + 1) * 128] for j in range(8)], 0)


def spread_heads(rows):
    return jnp.concatenate([rows[j * 128:(j + 1) * 128] for j in range(8)], 1)


def attention_kernel(first, kf, kb, tq_ref, inv_ref, q_ref, dy_ref, x_ref, kv_hbm, y_ref, dq_ref, terms_ref,
                     kv_s, dk_s, dv_s, sems):
    nq = q_ref.shape[0]
    head = pl.program_id(0)
    spans = kv_hbm.shape[0]
    scale = 128 ** -0.5
    c = scale * LOG2E

    @pl.when(head == 0)
    def _():
        copies = [pltpu.make_async_copy(kv_hbm.at[inv_ref[t], :, pl.ds(first * 256, kv_s.shape[1])], kv_s.at[pl.ds(t * 128, 128)], sems.at[t])
                  for t in range(spans)]
        for cp in copies:
            cp.start()
        for cp in copies:
            cp.wait()

    dk_s[...] = jnp.zeros_like(dk_s)
    dv_s[...] = jnp.zeros_like(dv_s)
    kcol = pl.multiple_of(head * 256, 256)
    vcol = pl.multiple_of(head * 256 + 128, 128)

    def span(qi, _):
        t = tq_ref[qi]
        q = stack_heads(q_ref[qi])
        dy = stack_heads(dy_ref[qi])
        rows = q.shape[0]

        def fwd(b, carry, masked):
            m, l, acc = carry
            at = pl.multiple_of(b * kf, kf)
            k = kv_s[pl.ds(at, kf), pl.ds(kcol, 128)]
            v = kv_s[pl.ds(at, kf), pl.ds(vcol, 128)]
            s = lax.dot_general(q, k, NT, preferred_element_type=F32) * c
            if masked:
                kpos = at + lax.broadcasted_iota(jnp.int32, (128, kf), 1)
                qpos = t * 128 + lax.broadcasted_iota(jnp.int32, (128, kf), 0)
                s = jnp.where((kpos <= qpos)[None], s.reshape(8, 128, kf), -1e30).reshape(rows, kf)
            m_new = jnp.maximum(m, jnp.max(s, 1, keepdims=True))
            e = jnp.exp2(s - m_new)
            fade = jnp.exp2(m - m_new)
            l = l * fade + jnp.sum(e, 1, keepdims=True)
            acc = acc * fade + lax.dot_general(e.astype(BF), v, (((1,), (0,)), ((), ())), preferred_element_type=F32)
            return m_new, l, acc

        nf = (t * 128) // kf
        carry = (jnp.full((rows, 1), -1e30, F32), jnp.zeros((rows, 1), F32), jnp.zeros((rows, 128), F32))
        carry = lax.fori_loop(0, nf, lambda b, cr: fwd(b, cr, False), carry)
        m, l, acc = fwd(nf, carry, True)
        mixed = acc / l
        y_ref[qi] = (x_ref[qi].astype(F32) + spread_heads(mixed)).astype(y_ref.dtype)
        lse = m + jnp.log2(l)
        delta = jnp.sum(dy.astype(F32) * mixed, 1, keepdims=True)
        lse_r = jnp.transpose(jnp.broadcast_to(lse, (rows, 128)))[0:1]
        delta_r = jnp.transpose(jnp.broadcast_to(delta, (rows, 128)))[0:1]

        def bwd(b, dq, masked):
            at = pl.multiple_of(b * kb, kb)
            k = kv_s[pl.ds(at, kb), pl.ds(kcol, 128)]
            v = kv_s[pl.ds(at, kb), pl.ds(vcol, 128)]
            s = lax.dot_general(k, q, NT, preferred_element_type=F32) * c
            p = jnp.exp2(s - lse_r)
            if masked:
                kpos = at + lax.broadcasted_iota(jnp.int32, (kb, 128), 0)
                qpos = t * 128 + lax.broadcasted_iota(jnp.int32, (kb, 128), 1)
                vis = kpos <= qpos
                p = jnp.concatenate([jnp.where(vis, p[:, j * 128:(j + 1) * 128], 0.0) for j in range(8)], 1)
            dp = lax.dot_general(v, dy, NT, preferred_element_type=F32)
            ds = (p * (dp - delta_r)).astype(BF)
            dv_s[pl.ds(at, kb)] += jnp.dot(p.astype(BF), dy, preferred_element_type=F32)
            dk_s[pl.ds(at, kb)] += jnp.dot(ds, q, preferred_element_type=F32)
            return dq + lax.dot_general(ds, k, TN, preferred_element_type=F32)

        nb = (t * 128) // kb
        dq = jnp.zeros((rows, 128), F32)
        dq = lax.fori_loop(0, nb, lambda b, cr: bwd(b, cr, False), dq)
        dq = bwd(nb, dq, True)
        dq_ref[qi] = spread_heads(dq * scale).astype(dq_ref.dtype)
        return 0

    lax.fori_loop(0, nq, span, 0)
    for t in range(spans):
        at = pl.ds(pl.multiple_of(inv_ref[t] * 128, 128), 128)
        terms_ref[at, 0:128] = (dk_s[t * 128:(t + 1) * 128] * scale).astype(BF)
        terms_ref[at, 128:256] = dv_s[t * 128:(t + 1) * 128].astype(BF)


def attention(q, dy, x, kv, tq, inv, first, count, kf=1024, kb=512):
    nq, tok, _ = q.shape
    spans = kv.shape[0]
    smem = pl.BlockSpec(memory_space=pltpu.SMEM)
    qspec = pl.BlockSpec((nq, tok, 1024), lambda h: (0, 0, first + h))
    ospec = pl.BlockSpec((nq, tok, 1024), lambda h: (0, 0, h))
    flops = 2 * 7 * nq * count * 1024 * spans * 128 * 128
    rows = jax.ShapeDtypeStruct((nq, tok, count * 1024), BF)
    return pl.pallas_call(
        functools.partial(attention_kernel, first, kf, kb),
        grid=(count,),
        in_specs=[smem, smem, qspec, qspec, qspec, pl.BlockSpec(memory_space=pl.ANY)],
        out_specs=[ospec, ospec, pl.BlockSpec((spans * 128, 256), lambda h: (0, h))],
        out_shape=[rows, rows, jax.ShapeDtypeStruct((spans * 128, count * 256), BF)],
        scratch_shapes=[pltpu.VMEM((spans * 128, count * 256), BF), pltpu.VMEM((spans * 128, 128), F32),
                        pltpu.VMEM((spans * 128, 128), F32), pltpu.SemaphoreType.DMA((spans,))],
        compiler_params=pltpu.CompilerParams(vmem_limit_bytes=50 << 20),
        cost_estimate=pl.CostEstimate(flops=flops, bytes_accessed=16 << 20, transcendentals=0),
        name="attention",
    )(tq, inv, q, dy, x, kv)


MESH_ID = pl.DeviceIdType.MESH
EPS = 1e-05
DOWN, UP = 0, 1
OWN, PAIR = 0, 1
UNITS = [(0, OWN), (0, PAIR), (1, OWN), (1, PAIR)]


class Place:
    def __init__(self):
        self.me = lax.axis_index("ctx")
        self.core = self.me % 2
        self.chip = self.me // 2
        beside = self.chip % 2
        self.partner = self.me + 1 - 2 * self.core
        self.across = self.me + 2 - 4 * beside
        self.above = (self.me + 4) % 16
        self.below = (self.me + 12) % 16
        self.chip_x = self.chip + 1 - 2 * beside

    def greet(self, barrier):
        for dev in (self.partner, self.across, self.above, self.below):
            pl.semaphore_signal(barrier, inc=1, device_id={"ctx": dev}, device_id_type=MESH_ID)
        pl.semaphore_wait(barrier, 4)

    def span(self, chip, kind):
        return 2 * chip + (self.core if kind == OWN else 1 - self.core)

    def up(self, chip, by):
        return (chip + 2 * by) % 8


class Wires:
    def __init__(self, send_sem, recv_sem):
        self.send_sem, self.recv_sem, self.started = send_sem, recv_sem, []

    def copy(self, index, src, dst, dev):
        return pltpu.make_async_remote_copy(
            src_ref=src, dst_ref=dst, send_sem=self.send_sem.at[index], recv_sem=self.recv_sem.at[index],
            device_id={"ctx": dev}, device_id_type=MESH_ID)

    def send(self, index, src, dst, dev):
        copy = self.copy(index, src, dst, dev)
        copy.start()
        self.started.append(copy)

    def arrive(self, index, ref, dev):
        self.copy(index, ref, ref, dev).wait_recv()

    def finish(self):
        for copy in self.started:
            copy.wait_send()


X, ZM, ZP, XZM, XZP, AN, XA = range(7)


def gather_first(place, wires, base, unit, src, slot):
    kind = unit[1]
    at = base + 7 * UNITS.index(unit)
    here = slot(unit, place.chip)
    wires.send(at + X, src, here, place.across)
    wires.send(at + ZM, src, here, place.above)
    wires.send(at + ZP, src, here, place.below)


def gather_second(place, wires, base, unit, slot, landed):
    kind = unit[1]
    at = base + 7 * UNITS.index(unit)
    cx = slot(unit, place.chip_x)
    wires.arrive(at + X, cx, place.across)
    wires.send(at + XZM, cx, cx, place.above)
    wires.send(at + XZP, cx, cx, place.below)
    landed(unit, place.chip_x)
    lo, hi = slot(unit, place.up(place.chip, 3)), slot(unit, place.up(place.chip, 1))
    wires.arrive(at + ZM, lo, place.below)
    if kind == OWN:
        wires.send(at + AN, lo, lo, place.above)
    wires.arrive(at + ZP, hi, place.above)
    if kind == PAIR:
        wires.send(at + AN, hi, hi, place.below)
    landed(unit, place.up(place.chip, 3))
    landed(unit, place.up(place.chip, 1))


def gather_third(place, wires, base, unit, slot, landed):
    at = base + 7 * UNITS.index(unit)
    far = slot(unit, place.up(place.chip, 2))
    wires.arrive(at + AN, far, place.below if unit[1] == OWN else place.above)
    wires.send(at + XA, far, far, place.across)
    landed(unit, place.up(place.chip, 2))
    for kind, by, dev in ((XZM, 3, place.below), (XZP, 1, place.above)):
        chip = place.up(place.chip_x, by)
        wires.arrive(at + kind, slot(unit, chip), dev)
        landed(unit, chip)


def gather_last(place, wires, base, unit, slot, landed):
    at = base + 7 * UNITS.index(unit)
    chip = place.up(place.chip_x, 2)
    wires.arrive(at + XA, slot(unit, chip), place.across)
    landed(unit, chip)


def nothing(unit, chip):
    pass


def spread_kernel(act_d, act_u, cot_d, cot_u, x_d, x_u, kv_d, kv_u,
                  q_d, q_u, dy_d, dy_u, xh_d, xh_u, pair_d, all_u, send_sem, recv_sem, local_sem):
    place = Place()
    wires = Wires(send_sem, recv_sem)
    place.greet(pltpu.get_barrier_semaphore())
    mine = lambda width: pl.ds(pl.multiple_of(place.core * width, width), width)
    other = lambda width: pl.ds(pl.multiple_of((1 - place.core) * width, width), width)
    slot = lambda unit, chip: all_u.at[place.span(chip, unit[1]), :, pl.ds(unit[0] * 256, 256)]
    part = lambda head: pl.ds(pl.multiple_of(place.core * 512 + head * 256, 256), 256)
    local = []

    def keep(src, dst):
        copy = pltpu.make_async_copy(src, dst, local_sem.at[len(local)])
        copy.start()
        local.append(copy)

    wires.send(28, kv_u.at[:, other(512)], all_u.at[place.me], place.partner)
    for head in range(2):
        gather_first(place, wires, 0, (head, OWN), kv_u.at[:, part(head)], slot)
    keep(kv_u.at[:, mine(512)], all_u.at[place.me])
    wires.arrive(28, all_u.at[place.partner], place.partner)
    for head in range(2):
        gather_first(place, wires, 0, (head, PAIR), slot((head, PAIR), place.chip), slot)
    wires.send(29, kv_d.at[:, other(512)], pair_d.at[place.core], place.partner)
    keep(kv_d.at[:, mine(512)], pair_d.at[place.core])
    halves = ((act_u, q_u), (cot_u, dy_u), (x_u, xh_u), (act_d, q_d), (cot_d, dy_d), (x_d, xh_d))
    for n, (src, dst) in enumerate(halves):
        wires.send(30 + n, src.at[:, other(2048)], dst.at[place.core], place.partner)
        keep(src.at[:, mine(2048)], dst.at[place.core])
    for unit in UNITS:
        gather_second(place, wires, 0, unit, slot, nothing)
    for unit in UNITS:
        gather_third(place, wires, 0, unit, slot, nothing)
    for unit in UNITS:
        gather_last(place, wires, 0, unit, slot, nothing)
    wires.arrive(29, pair_d.at[1 - place.core], place.partner)
    for n, (src, dst) in enumerate(halves):
        wires.arrive(30 + n, dst.at[1 - place.core], place.partner)
    for copy in local:
        copy.wait()
    wires.finish()


def spread(*operands):
    half = jax.ShapeDtypeStruct((2, 128, 2048), BF)
    hbm = pl.BlockSpec(memory_space=pl.ANY)
    return pl.pallas_call(
        spread_kernel,
        in_specs=[hbm] * 8,
        out_specs=[hbm] * 8,
        out_shape=[half] * 6 + [jax.ShapeDtypeStruct((2, 128, 512), BF), jax.ShapeDtypeStruct((16, 128, 512), BF)],
        scratch_shapes=[pltpu.SemaphoreType.DMA((36,)), pltpu.SemaphoreType.DMA((36,)), pltpu.SemaphoreType.DMA((8,))],
        compiler_params=pltpu.CompilerParams(collective_id=1, has_side_effects=True),
        name="spread",
    )(*operands)


R0, RA, RB, R1, RU, RD, RX = range(7)


def reduce_kernel(terms_0, terms_1, y_0, y_1, dq_0, dq_1, wgrad_u, down_out, dquery, all_kv, mirror_w,
                  slots, stage, total, send_sem, recv_sem, local_sem):
    place = Place()
    wires = Wires(send_sem, recv_sem)
    section = lax.axis_index("section")
    after, before, mirrored = (section + 1) % 8, (section + 7) % 8, 7 - section
    barrier = pltpu.get_barrier_semaphore()
    for there in (after, before):
        for dev in (place.me, place.partner):
            pl.semaphore_signal(barrier, inc=1, device_id={"section": there, "ctx": dev}, device_id_type=MESH_ID)
    pl.semaphore_signal(barrier, inc=1, device_id={"section": mirrored}, device_id_type=MESH_ID)
    for dev in (place.partner, place.across, place.above, place.below):
        pl.semaphore_signal(barrier, inc=1, device_id={"ctx": dev}, device_id_type=MESH_ID)
    pl.semaphore_wait(barrier, 9)
    terms = (terms_0, terms_1)
    part = lambda core, head, width: pl.ds(pl.multiple_of(core * 2 * width + head * width, width), width)
    chip, chip_x = place.chip, place.chip_x
    local = []

    def term(unit, at):
        return terms[unit[0]].at[pl.ds(pl.multiple_of(place.span(at, unit[1]) * 128, 128), 128)]

    def plus(*refs):
        value = refs[0][...].astype(F32)
        for ref in refs[1:]:
            value = value + ref[...].astype(F32)
        return value.astype(BF)

    for n, unit in enumerate(UNITS):
        at = 7 * n
        wires.send(at + R0, term(unit, place.up(chip_x, 2)), slots.at[at + R0], place.across)
        wires.send(at + RA, term(unit, place.up(chip_x, 1)), slots.at[at + RA], place.above)
        wires.send(at + RB, term(unit, place.up(chip_x, 3)), slots.at[at + RB], place.below)
        if unit[1] == OWN:
            wires.send(at + RD, term(unit, place.up(chip, 1)), slots.at[at + RD], place.above)
        else:
            wires.send(at + RU, term(unit, place.up(chip, 3)), slots.at[at + RU], place.below)
    index = 56 + 32
    far = []

    def far_send(src, dst, dev):
        copy = pltpu.make_async_remote_copy(
            src_ref=src, dst_ref=dst, send_sem=send_sem.at[index + len(far)], recv_sem=recv_sem.at[index + len(far)],
            device_id=dev, device_id_type=MESH_ID)
        copy.start()
        far.append(copy)

    for head, (y, dq) in enumerate(((y_0, dq_0), (y_1, dq_1))):
        here = part(place.core, head, 1024)
        far_send(dq.at[1 - place.core], dquery.at[:, here], {"ctx": place.partner})
        far_send(y.at[place.core], down_out.at[:, here], {"section": after})
        far_send(y.at[1 - place.core], down_out.at[:, here], {"section": after, "ctx": place.partner})
        copy = pltpu.make_async_copy(dq.at[place.core], dquery.at[:, here], local_sem.at[len(local)])
        copy.start()
        local.append(copy)
    far_send(wgrad_u, mirror_w, {"section": mirrored})
    for n, unit in enumerate(UNITS):
        at = 7 * n
        wires.arrive(at + R0, slots.at[at + R0], place.across)
        stage[3 * n] = plus(slots.at[at + R0], term(unit, place.up(chip, 2)))
        wires.send(at + R1, stage.at[3 * n], slots.at[at + R1], place.below if unit[1] == OWN else place.above)
    for n, unit in enumerate(UNITS):
        at = 7 * n
        wires.arrive(at + RA, slots.at[at + RA], place.below)
        wires.arrive(at + RB, slots.at[at + RB], place.above)
        stage[3 * n + 1] = plus(slots.at[at + RA], slots.at[at + RB], term(unit, chip_x))
        wires.send(at + RX, stage.at[3 * n + 1], slots.at[at + RX], place.across)
        if unit[1] == OWN:
            wires.arrive(at + R1, slots.at[at + R1], place.above)
            stage[3 * n + 2] = plus(slots.at[at + R1], term(unit, place.up(chip, 3)))
            wires.send(at + RU, stage.at[3 * n + 2], slots.at[at + RU], place.below)
        else:
            wires.arrive(at + R1, slots.at[at + R1], place.below)
            stage[3 * n + 2] = plus(slots.at[at + R1], term(unit, place.up(chip, 1)))
            wires.send(at + RD, stage.at[3 * n + 2], slots.at[at + RD], place.above)

    slot = lambda unit, at: all_kv.at[place.span(at, unit[1]), :, part(place.core, unit[0], 256)]
    passed = [0]

    def hand_over(unit, at):
        ref = slot(unit, at)
        wires.send(56 + passed[0], ref, ref, place.partner)
        passed[0] += 1

    order = []

    def landed(unit, at):
        order.append((unit, at))
        hand_over(unit, at)

    for n, unit in enumerate(UNITS):
        at = 7 * n
        wires.arrive(at + RX, slots.at[at + RX], place.across)
        wires.arrive(at + RU, slots.at[at + RU], place.above)
        wires.arrive(at + RD, slots.at[at + RD], place.below)
        total[n] = plus(slots.at[at + RX], slots.at[at + RU], slots.at[at + RD], term(unit, chip))
        gather_first(place, wires, 28, unit, total.at[n], slot)
        copy = pltpu.make_async_copy(total.at[n], slot(unit, chip), local_sem.at[len(local)])
        copy.start()
        local.append(copy)
        wires.send(56 + passed[0], total.at[n], slot(unit, chip), place.partner)
        order.append((unit, chip))
        passed[0] += 1
    for unit in UNITS:
        gather_second(place, wires, 28, unit, slot, landed)
    for unit in UNITS:
        gather_third(place, wires, 28, unit, slot, landed)
    for unit in UNITS:
        gather_last(place, wires, 28, unit, slot, landed)
    for n, (unit, at) in enumerate(order):
        ref = all_kv.at[place.span(at, 1 - unit[1]), :, part(1 - place.core, unit[0], 256)]
        wires.arrive(56 + n, ref, place.partner)
    for copy in far:
        copy.wait()
    for copy in local:
        copy.wait()
    wires.finish()


def reduce_terms(*operands):
    hbm = pl.BlockSpec(memory_space=pl.ANY)
    vmem = pl.BlockSpec(memory_space=pltpu.VMEM)
    row = jax.ShapeDtypeStruct((128, 4096), BF)
    return pl.pallas_call(
        reduce_kernel,
        in_specs=[vmem] * 2 + [hbm] * 5,
        out_specs=[hbm] * 4,
        out_shape=[row] * 2 + [jax.ShapeDtypeStruct((16, 128, 1024), BF), jax.ShapeDtypeStruct((256, 1024), BF)],
        scratch_shapes=[pltpu.VMEM((28, 128, 256), BF), pltpu.VMEM((12, 128, 256), BF), pltpu.VMEM((4, 128, 256), BF),
                        pltpu.SemaphoreType.DMA((95,)), pltpu.SemaphoreType.DMA((95,)), pltpu.SemaphoreType.DMA((6,))],
        compiler_params=pltpu.CompilerParams(collective_id=2, has_side_effects=True, vmem_limit_bytes=32 << 20),
        name="reduce_terms",
    )(*operands)


def gains_kernel(g_ref, gd_out, gu_out, parts, mine, send_sem, recv_sem):
    me = lax.axis_index("ctx")
    section = lax.axis_index("section")
    barrier = pltpu.get_barrier_semaphore()
    pl.semaphore_signal(barrier, inc=1, device_id={"section": 7 - section}, device_id_type=MESH_ID)
    for step in range(1, 16):
        pl.semaphore_signal(barrier, inc=1, device_id={"ctx": (me + step) % 16}, device_id_type=MESH_ID)
    pl.semaphore_wait(barrier, 16)
    copies = []
    for step in range(1, 16):
        to = (me + step) % 16
        copy = pltpu.make_async_remote_copy(
            src_ref=g_ref.at[to], dst_ref=parts.at[step], send_sem=send_sem.at[step], recv_sem=recv_sem.at[step],
            device_id={"ctx": to}, device_id_type=MESH_ID)
        copy.start()
        copies.append(copy)
    value = g_ref[me]
    for step in range(1, 16):
        copies[step - 1].wait_recv()
        value = value + parts[step]
    mine[...] = value
    gd_out[...] = value
    last = pltpu.make_async_remote_copy(src_ref=mine, dst_ref=gu_out, send_sem=send_sem.at[0], recv_sem=recv_sem.at[0],
                                        device_id={"section": 7 - section}, device_id_type=MESH_ID)
    last.start()
    for copy in copies:
        copy.wait_send()
    last.wait()


def sum_gains(gains):
    vmem = pl.BlockSpec(memory_space=pltpu.VMEM)
    small = jax.ShapeDtypeStruct((8, 256), F32)
    return pl.pallas_call(
        gains_kernel,
        in_specs=[vmem],
        out_specs=[vmem, vmem],
        out_shape=[small, small],
        scratch_shapes=[pltpu.VMEM((16, 8, 256), F32), pltpu.VMEM((8, 256), F32),
                        pltpu.SemaphoreType.DMA((16,)), pltpu.SemaphoreType.DMA((16,))],
        compiler_params=pltpu.CompilerParams(collective_id=3, has_side_effects=True),
        name="sum_gains",
    )(gains)


def by_head(kv):
    return kv.reshape(-1, 2, 4, 128).transpose(0, 2, 1, 3).reshape(-1, 1024)


def by_kind(kv):
    return kv.reshape(-1, 4, 2, 128).transpose(0, 2, 1, 3).reshape(-1, 1024)


def prepare(x, gain, weight):
    xf = x.astype(F32)
    recip = lax.rsqrt(jnp.mean(xf * xf, -1, keepdims=True) + EPS)
    normed = xf * recip
    act = (normed * gain[None, :]).astype(BF)
    kv = jnp.dot(act, weight, preferred_element_type=F32).astype(BF)
    return recip, act, by_head(kv)


def complete(x, recip, cot, gain, weight, dquery, dkv):
    normed = x.astype(F32) * recip
    dact = dquery.astype(F32) + lax.dot_general(by_kind(dkv), weight, NT, preferred_element_type=F32)
    gpart = jnp.sum(dact * normed, 0)
    dnormed = dact * gain[None, :]
    dx = cot.astype(F32) + recip * (dnormed - normed * jnp.mean(dnormed * normed, -1, keepdims=True))
    return dx.astype(BF), gpart


def exchanged(array):
    return lax.ppermute(array, "ctx", [(i, i ^ 1) for i in range(lax.axis_size("ctx"))])


def halves_joined(core, mine, other):
    return jnp.where(core == 0, jnp.concatenate([mine, other], 1), jnp.concatenate([other, mine], 1))


def relayed(halves, core, by):
    sections, spans = lax.axis_size("section"), lax.axis_size("ctx")
    to = lambda flip: [(s * spans + i, (s + by) % sections * spans + (i ^ flip)) for s in range(sections) for i in range(spans)]
    pick = lambda which: lax.dynamic_index_in_dim(halves, which, 0, False)
    mine = lax.ppermute(pick(core), ("section", "ctx"), to(0))
    other = lax.ppermute(pick(1 - core), ("section", "ctx"), to(1))
    return halves_joined(core, mine, other)


def per_device(down_in, up_in, down_cot, up_cot, kv_weight, norm_gain, span_ids):
    own = lax.axis_index("ctx")
    core = own % 2
    x_d, x_u, cot_d, cot_u = down_in[0], up_in[0], down_cot[0], up_cot[0]
    gain_d, gain_u = norm_gain[0, 0], norm_gain[1, 0]
    weight_d, weight_u = kv_weight[0, 0], kv_weight[1, 0]
    same_core = [[i for i in range(16) if i % 2 == c] for c in range(2)]
    times = lax.dynamic_slice_in_dim(span_ids, own // 2 * 2, 2, 0)
    inverse = jnp.argsort(span_ids).astype(jnp.int32)
    recip_u, act_u, kv_u = prepare(x_u, gain_u, weight_u)
    recip_d, act_d, kv_d = prepare(x_d, gain_d, weight_d)
    q_d, q_u, dy_d, dy_u, xh_d, xh_u, pair_d, all_u = spread(act_d, act_u, cot_d, cot_u, x_d, x_u, kv_d, kv_u)
    all_d = lax.all_gather(pair_d.reshape(256, 512), "ctx", axis=0, axis_index_groups=same_core).reshape(16, 128, 512)
    act_d, act_u, _ = lax.optimization_barrier((act_d, act_u, pair_d))
    features = jnp.stack([act_d, act_u]).reshape(2, 128, 16, 256).transpose(2, 0, 1, 3)
    features = lax.all_to_all(features, "ctx", 0, 0, tiled=False)
    yh_u, dq_u, terms_u = attention(q_u, dy_u, xh_u, all_u, times, inverse, 0, 2)
    got_u = lax.all_to_all(terms_u.reshape(8, 256, 512), "ctx", 0, 0, axis_index_groups=same_core, tiled=False)
    up_out = relayed(yh_u, core, -1)
    dq_there = exchanged(lax.dynamic_index_in_dim(dq_u, 1 - core, 0, False))
    yh_d0, dq_d0, terms_d0 = attention(q_d, dy_d, xh_d, all_d, times, inverse, 0, 1)
    got_u, all_d, terms_d0 = lax.optimization_barrier((got_u, all_d, terms_d0))
    pair_u = jnp.sum(got_u.astype(F32), 0).astype(BF)
    dkv_u = lax.all_gather(pair_u, "ctx", axis=0)
    yh_d1, dq_d1, terms_d1 = attention(q_d, dy_d, xh_d, all_d, times, inverse, 1, 1)
    dkv_u, terms_d1 = lax.optimization_barrier((dkv_u, terms_d1))
    dkv_u = dkv_u.reshape(8, 2, 256, 512)
    wgrad_u = jnp.einsum("ctf,ckth->fkh", features[:, 1].reshape(8, 256, 256), dkv_u, preferred_element_type=F32)
    wgrad_u = wgrad_u.reshape(256, 1024).astype(BF)
    down_out, dquery_d, dkv_d, mirror_w = reduce_terms(terms_d0, terms_d1, yh_d0, yh_d1, dq_d0, dq_d1, wgrad_u)
    dquery_u = halves_joined(core, lax.dynamic_index_in_dim(dq_u, core, 0, False), dq_there)
    own_u = lax.dynamic_index_in_dim(dkv_u, own // 2, 0, False)
    own_u = lax.dynamic_slice_in_dim(own_u, core * 128, 128, 1).transpose(1, 0, 2).reshape(128, 1024)
    own_d = lax.dynamic_index_in_dim(dkv_d, own, 0, False)
    grad_u, gpart_u = complete(x_u, recip_u, cot_u, gain_u, weight_u, dquery_u, own_u)
    grad_d, gpart_d = complete(x_d, recip_d, cot_d, gain_d, weight_d, dquery_d, own_d)
    gains = jnp.stack([gpart_d, gpart_u] + [jnp.zeros_like(gpart_d)] * 6).reshape(8, 16, 256).transpose(1, 0, 2)
    gain_here, gain_there = sum_gains(gains)
    wgrad_d = lax.dot_general(features[:, 0].reshape(2048, 256), dkv_d.reshape(2048, 1024), TN, preferred_element_type=F32)
    kv_grad = by_kind(wgrad_d + mirror_w.astype(F32))[None]
    gain_grad = (gain_here[0] + gain_there[1])[None]
    return (down_out[None], up_out[None], grad_d[None], grad_u[None], kv_grad, gain_grad)


def solution(mesh):
    row = P("section", "ctx", None)
    in_specs = (row, row, row, row, P(None, "section", None, None), P(None, "section", None), P())
    out_specs = (row, row, row, row, row, P("section", "ctx"))
    return jax.shard_map(per_device, mesh=mesh, in_specs=in_specs, out_specs=out_specs, check_vma=False)
```

```python
import functools

import jax
import jax.numpy as jnp
from jax import lax
from jax.experimental import pallas as pl
from jax.experimental.pallas import tpu as pltpu
from jax.sharding import PartitionSpec as P

LOG2E = 1.4426950408889634
NT = (((1,), (1,)), ((), ()))
TN = (((0,), (0,)), ((), ()))
F32 = jnp.float32
BF = jnp.bfloat16


def stack_heads(block):
    return jnp.concatenate([block[:, j * 128:(j + 1) * 128] for j in range(8)], 0)


def spread_heads(rows):
    return jnp.concatenate([rows[j * 128:(j + 1) * 128] for j in range(8)], 1)


def attention_kernel(kf, kb, tq_ref, inv_ref, q_own, q_got, dy_own, dy_got, x_own, x_got, kv_hbm,
                     y_own, y_got, dq_own, dq_got, terms_ref, kv_s, dk_s, dv_s, sems):
    head = pl.program_id(0)
    spans = kv_hbm.shape[0]
    scale = 128 ** -0.5
    c = scale * LOG2E

    @pl.when(head == 0)
    def _():
        copies = [pltpu.make_async_copy(kv_hbm.at[inv_ref[t]], kv_s.at[pl.ds(t * 128, 128)], sems.at[t])
                  for t in range(spans)]
        for cp in copies:
            cp.start()
        for cp in copies:
            cp.wait()

    dk_s[...] = jnp.zeros_like(dk_s)
    dv_s[...] = jnp.zeros_like(dv_s)
    kcol = pl.multiple_of(head * 256, 256)
    vcol = pl.multiple_of(head * 256 + 128, 128)

    def span(qi, q_ref, dy_ref, x_ref, y_ref, dq_ref):
        t = tq_ref[qi]
        q = stack_heads(q_ref[...])
        dy = stack_heads(dy_ref[...])
        rows = q.shape[0]

        def fwd(b, carry, masked):
            m, l, acc = carry
            at = pl.multiple_of(b * kf, kf)
            k = kv_s[pl.ds(at, kf), pl.ds(kcol, 128)]
            v = kv_s[pl.ds(at, kf), pl.ds(vcol, 128)]
            s = lax.dot_general(q, k, NT, preferred_element_type=F32) * c
            if masked:
                kpos = at + lax.broadcasted_iota(jnp.int32, (128, kf), 1)
                qpos = t * 128 + lax.broadcasted_iota(jnp.int32, (128, kf), 0)
                s = jnp.where((kpos <= qpos)[None], s.reshape(8, 128, kf), -1e30).reshape(rows, kf)
            m_new = jnp.maximum(m, jnp.max(s, 1, keepdims=True))
            e = jnp.exp2(s - m_new)
            fade = jnp.exp2(m - m_new)
            l = l * fade + jnp.sum(e, 1, keepdims=True)
            acc = acc * fade + lax.dot_general(e.astype(BF), v, (((1,), (0,)), ((), ())), preferred_element_type=F32)
            return m_new, l, acc

        nf = (t * 128) // kf
        carry = (jnp.full((rows, 1), -1e30, F32), jnp.zeros((rows, 1), F32), jnp.zeros((rows, 128), F32))
        carry = lax.fori_loop(0, nf, lambda b, cr: fwd(b, cr, False), carry)
        m, l, acc = fwd(nf, carry, True)
        mixed = acc / l
        y_ref[...] = (x_ref[...].astype(F32) + spread_heads(mixed)).astype(y_ref.dtype)
        lse = m + jnp.log2(l)
        delta = jnp.sum(dy.astype(F32) * mixed, 1, keepdims=True)
        lse_r = jnp.transpose(jnp.broadcast_to(lse, (rows, 128)))[0:1]
        delta_r = jnp.transpose(jnp.broadcast_to(delta, (rows, 128)))[0:1]

        def bwd(b, dq, masked):
            at = pl.multiple_of(b * kb, kb)
            k = kv_s[pl.ds(at, kb), pl.ds(kcol, 128)]
            v = kv_s[pl.ds(at, kb), pl.ds(vcol, 128)]
            s = lax.dot_general(k, q, NT, preferred_element_type=F32) * c
            p = jnp.exp2(s - lse_r)
            if masked:
                kpos = at + lax.broadcasted_iota(jnp.int32, (kb, 128), 0)
                qpos = t * 128 + lax.broadcasted_iota(jnp.int32, (kb, 128), 1)
                vis = kpos <= qpos
                p = jnp.concatenate([jnp.where(vis, p[:, j * 128:(j + 1) * 128], 0.0) for j in range(8)], 1)
            dp = lax.dot_general(v, dy, NT, preferred_element_type=F32)
            ds = (p * (dp - delta_r)).astype(BF)
            dv_s[pl.ds(at, kb)] += jnp.dot(p.astype(BF), dy, preferred_element_type=F32)
            dk_s[pl.ds(at, kb)] += jnp.dot(ds, q, preferred_element_type=F32)
            return dq + lax.dot_general(ds, k, TN, preferred_element_type=F32)

        nb = (t * 128) // kb
        dq = jnp.zeros((rows, 128), F32)
        dq = lax.fori_loop(0, nb, lambda b, cr: bwd(b, cr, False), dq)
        dq = bwd(nb, dq, True)
        dq_ref[...] = spread_heads(dq * scale).astype(dq_ref.dtype)

    span(0, q_own, dy_own, x_own, y_own, dq_own)
    span(1, q_got, dy_got, x_got, y_got, dq_got)
    for t in range(spans):
        at = pl.ds(pl.multiple_of(inv_ref[t] * 128, 128), 128)
        terms_ref[at, 0:128] = (dk_s[t * 128:(t + 1) * 128] * scale).astype(BF)
        terms_ref[at, 128:256] = dv_s[t * 128:(t + 1) * 128].astype(BF)


def attention(q, dy, x, kv, tq, inv, kf=1024, kb=512):
    spans = kv.shape[0]
    count = kv.shape[2] // 256
    own = pl.BlockSpec((128, 1024), lambda h, tq, inv: (0, tq[2] * count + h))
    got = pl.BlockSpec((128, 1024), lambda h, tq, inv: (0, h))
    flops = 2 * 7 * 2 * count * 1024 * spans * 128 * 128
    rows = jax.ShapeDtypeStruct((128, count * 1024), BF)
    return pl.pallas_call(
        functools.partial(attention_kernel, kf, kb),
        grid_spec=pltpu.PrefetchScalarGridSpec(
            num_scalar_prefetch=2,
            grid=(count,),
            in_specs=[own, got] * 3 + [pl.BlockSpec(memory_space=pl.ANY)],
            out_specs=[got] * 4 + [pl.BlockSpec((spans * 128, 256), lambda h, tq, inv: (0, h))],
            scratch_shapes=[pltpu.VMEM((spans * 128, count * 256), BF), pltpu.VMEM((spans * 128, 128), F32),
                            pltpu.VMEM((spans * 128, 128), F32), pltpu.SemaphoreType.DMA((spans,))],
        ),
        out_shape=[rows] * 4 + [jax.ShapeDtypeStruct((spans * 128, count * 256), BF)],
        compiler_params=pltpu.CompilerParams(vmem_limit_bytes=50 << 20),
        cost_estimate=pl.CostEstimate(flops=flops, bytes_accessed=16 << 20, transcendentals=0),
        name="attention",
    )(tq, inv, *q, *dy, *x, kv)


MESH_ID = pl.DeviceIdType.MESH
EPS = 1e-05
DOWN, UP = 0, 1
OWN, PAIR = 0, 1
UNITS = [(UP, OWN), (UP, PAIR), (DOWN, OWN), (DOWN, PAIR)]


class Place:
    def __init__(self):
        self.me = lax.axis_index("ctx")
        self.core = self.me % 2
        self.chip = self.me // 2
        beside = self.chip % 2
        self.partner = self.me + 1 - 2 * self.core
        self.across = self.me + 2 - 4 * beside
        self.above = (self.me + 4) % 16
        self.below = (self.me + 12) % 16
        self.chip_x = self.chip + 1 - 2 * beside

    def greet(self, barrier):
        for dev in (self.partner, self.across, self.above, self.below):
            pl.semaphore_signal(barrier, inc=1, device_id={"ctx": dev}, device_id_type=MESH_ID)
        pl.semaphore_wait(barrier, 4)

    def span(self, chip, kind):
        return 2 * chip + (self.core if kind == OWN else 1 - self.core)

    def up(self, chip, by):
        return (chip + 2 * by) % 8


class Wires:
    def __init__(self, send_sem, recv_sem):
        self.send_sem, self.recv_sem, self.started = send_sem, recv_sem, []

    def copy(self, index, src, dst, dev):
        return pltpu.make_async_remote_copy(
            src_ref=src, dst_ref=dst, send_sem=self.send_sem.at[index], recv_sem=self.recv_sem.at[index],
            device_id={"ctx": dev}, device_id_type=MESH_ID)

    def send(self, index, src, dst, dev):
        copy = self.copy(index, src, dst, dev)
        copy.start()
        self.started.append(copy)

    def arrive(self, index, ref, dev):
        self.copy(index, ref, ref, dev).wait_recv()

    def finish(self):
        for copy in self.started:
            copy.wait_send()


X, ZM, ZP, XZM, XZP, AN, XA = range(7)


def gather_first(place, wires, base, unit, src, slot):
    kind = unit[1]
    at = base + 7 * UNITS.index(unit)
    here = slot(unit, place.chip)
    wires.send(at + X, src, here, place.across)
    wires.send(at + ZM, src, here, place.above)
    wires.send(at + ZP, src, here, place.below)


def gather_second(place, wires, base, unit, slot, landed):
    kind = unit[1]
    at = base + 7 * UNITS.index(unit)
    cx = slot(unit, place.chip_x)
    wires.arrive(at + X, cx, place.across)
    wires.send(at + XZM, cx, cx, place.above)
    wires.send(at + XZP, cx, cx, place.below)
    landed(unit, place.chip_x)
    lo, hi = slot(unit, place.up(place.chip, 3)), slot(unit, place.up(place.chip, 1))
    wires.arrive(at + ZM, lo, place.below)
    if kind == OWN:
        wires.send(at + AN, lo, lo, place.above)
    wires.arrive(at + ZP, hi, place.above)
    if kind == PAIR:
        wires.send(at + AN, hi, hi, place.below)
    landed(unit, place.up(place.chip, 3))
    landed(unit, place.up(place.chip, 1))


def gather_third(place, wires, base, unit, slot, landed):
    at = base + 7 * UNITS.index(unit)
    far = slot(unit, place.up(place.chip, 2))
    wires.arrive(at + AN, far, place.below if unit[1] == OWN else place.above)
    wires.send(at + XA, far, far, place.across)
    landed(unit, place.up(place.chip, 2))
    for kind, by, dev in ((XZM, 3, place.below), (XZP, 1, place.above)):
        chip = place.up(place.chip_x, by)
        wires.arrive(at + kind, slot(unit, chip), dev)
        landed(unit, chip)


def gather_last(place, wires, base, unit, slot, landed):
    at = base + 7 * UNITS.index(unit)
    chip = place.up(place.chip_x, 2)
    wires.arrive(at + XA, slot(unit, chip), place.across)
    landed(unit, chip)


def nothing(unit, chip):
    pass


def spread_kernel(act_d, act_u, cot_d, cot_u, x_d, x_u, kv_d, kv_u,
                  q_d, q_u, dy_d, dy_u, xh_d, xh_u, all_d, all_u, send_sem, recv_sem, local_sem):
    place = Place()
    wires = Wires(send_sem, recv_sem)
    place.greet(pltpu.get_barrier_semaphore())
    all_kv, kv = (all_d, all_u), (kv_d, kv_u)
    mine = pl.ds(pl.multiple_of(place.core * 512, 512), 512)
    other = lambda width: pl.ds(pl.multiple_of((1 - place.core) * width, width), width)
    slot = lambda unit, chip: all_kv[unit[0]].at[place.span(chip, unit[1])]
    local = []
    for layer in (UP, DOWN):
        wires.send(28 + layer, kv[layer].at[:, other(512)], all_kv[layer].at[place.me], place.partner)
    for layer in (UP, DOWN):
        gather_first(place, wires, 0, (layer, OWN), kv[layer].at[:, mine], slot)
        copy = pltpu.make_async_copy(kv[layer].at[:, mine], all_kv[layer].at[place.me], local_sem.at[layer])
        copy.start()
        local.append(copy)
    for layer in (UP, DOWN):
        wires.arrive(28 + layer, all_kv[layer].at[place.partner], place.partner)
        gather_first(place, wires, 0, (layer, PAIR), slot((layer, PAIR), place.chip), slot)
    halves = ((act_u, q_u), (cot_u, dy_u), (x_u, xh_u), (act_d, q_d), (cot_d, dy_d), (x_d, xh_d))
    for n, (src, dst) in enumerate(halves):
        wires.send(30 + n, src.at[:, other(2048)], dst, place.partner)
    for unit in UNITS:
        gather_second(place, wires, 0, unit, slot, nothing)
    for unit in UNITS:
        gather_third(place, wires, 0, unit, slot, nothing)
    for unit in UNITS:
        gather_last(place, wires, 0, unit, slot, nothing)
    for n, (src, dst) in enumerate(halves):
        wires.arrive(30 + n, dst, place.partner)
    for copy in local:
        copy.wait()
    wires.finish()


def spread(*operands):
    half = jax.ShapeDtypeStruct((128, 2048), BF)
    hbm = pl.BlockSpec(memory_space=pl.ANY)
    return pl.pallas_call(
        spread_kernel,
        in_specs=[hbm] * 6 + [pl.BlockSpec(memory_space=pltpu.VMEM)] * 2,
        out_specs=[hbm] * 8,
        out_shape=[half] * 6 + [jax.ShapeDtypeStruct((16, 128, 512), BF)] * 2,
        scratch_shapes=[pltpu.SemaphoreType.DMA((36,)), pltpu.SemaphoreType.DMA((36,)), pltpu.SemaphoreType.DMA((2,))],
        compiler_params=pltpu.CompilerParams(collective_id=1, has_side_effects=True),
        name="spread",
    )(*operands)


R0, RA, RB, R1, RU, RD, RX = range(7)


def reduce_kernel(terms_d, terms_u, yo_d, yg_d, yo_u, yg_u, dqg_d, dqg_u, down_out, up_out, dq_d, dq_u, all_d, all_u,
                  slots, stage, total, send_sem, recv_sem, local_sem):
    place = Place()
    wires = Wires(send_sem, recv_sem)
    section = lax.axis_index("section")
    after, before = (section + 1) % 8, (section + 7) % 8
    barrier = pltpu.get_barrier_semaphore()
    for there in (after, before):
        for dev in (place.me, place.partner):
            pl.semaphore_signal(barrier, inc=1, device_id={"section": there, "ctx": dev}, device_id_type=MESH_ID)
    for dev in (place.partner, place.across, place.above, place.below):
        pl.semaphore_signal(barrier, inc=1, device_id={"ctx": dev}, device_id_type=MESH_ID)
    pl.semaphore_wait(barrier, 8)
    terms, all_kv = (terms_d, terms_u), (all_d, all_u)
    mine = pl.ds(pl.multiple_of(place.core * 512, 512), 512)
    wide = pl.ds(pl.multiple_of(place.core * 2048, 2048), 2048)
    chip, chip_x = place.chip, place.chip_x
    local = []

    def term(unit, at):
        return terms[unit[0]].at[pl.ds(pl.multiple_of(place.span(at, unit[1]) * 128, 128), 128)]

    def plus(*refs):
        value = refs[0][...].astype(F32)
        for ref in refs[1:]:
            value = value + ref[...].astype(F32)
        return value.astype(BF)

    for n, unit in enumerate(UNITS):
        at = 7 * n
        wires.send(at + R0, term(unit, place.up(chip_x, 2)), slots.at[at + R0], place.across)
        wires.send(at + RA, term(unit, place.up(chip_x, 1)), slots.at[at + RA], place.above)
        wires.send(at + RB, term(unit, place.up(chip_x, 3)), slots.at[at + RB], place.below)
        if unit[1] == OWN:
            wires.send(at + RD, term(unit, place.up(chip, 1)), slots.at[at + RD], place.above)
        else:
            wires.send(at + RU, term(unit, place.up(chip, 3)), slots.at[at + RU], place.below)
    index = 56 + 32
    far = []

    def far_send(src, dst, dev):
        copy = pltpu.make_async_remote_copy(
            src_ref=src, dst_ref=dst, send_sem=send_sem.at[index + len(far)], recv_sem=recv_sem.at[index + len(far)],
            device_id=dev, device_id_type=MESH_ID)
        copy.start()
        far.append(copy)

    far_send(dqg_u, dq_u, {"ctx": place.partner})
    far_send(dqg_d, dq_d, {"ctx": place.partner})
    for there, mine_y, other_y, out in ((before, yo_u, yg_u, up_out), (after, yo_d, yg_d, down_out)):
        far_send(mine_y, out.at[:, wide], {"section": there})
        far_send(other_y, out.at[:, wide], {"section": there, "ctx": place.partner})
    for n, unit in enumerate(UNITS):
        at = 7 * n
        wires.arrive(at + R0, slots.at[at + R0], place.across)
        stage[3 * n] = plus(slots.at[at + R0], term(unit, place.up(chip, 2)))
        wires.send(at + R1, stage.at[3 * n], slots.at[at + R1], place.below if unit[1] == OWN else place.above)
    for n, unit in enumerate(UNITS):
        at = 7 * n
        wires.arrive(at + RA, slots.at[at + RA], place.below)
        wires.arrive(at + RB, slots.at[at + RB], place.above)
        stage[3 * n + 1] = plus(slots.at[at + RA], slots.at[at + RB], term(unit, chip_x))
        wires.send(at + RX, stage.at[3 * n + 1], slots.at[at + RX], place.across)
        if unit[1] == OWN:
            wires.arrive(at + R1, slots.at[at + R1], place.above)
            stage[3 * n + 2] = plus(slots.at[at + R1], term(unit, place.up(chip, 3)))
            wires.send(at + RU, stage.at[3 * n + 2], slots.at[at + RU], place.below)
        else:
            wires.arrive(at + R1, slots.at[at + R1], place.below)
            stage[3 * n + 2] = plus(slots.at[at + R1], term(unit, place.up(chip, 1)))
            wires.send(at + RD, stage.at[3 * n + 2], slots.at[at + RD], place.above)

    slot = lambda unit, at: all_kv[unit[0]].at[place.span(at, unit[1]), :, mine]
    passed = [0]

    def hand_over(unit, at):
        ref = slot(unit, at)
        wires.send(56 + passed[0], ref, ref, place.partner)
        passed[0] += 1

    order = []

    def landed(unit, at):
        order.append((unit, at))
        hand_over(unit, at)

    for n, unit in enumerate(UNITS):
        at = 7 * n
        wires.arrive(at + RX, slots.at[at + RX], place.across)
        wires.arrive(at + RU, slots.at[at + RU], place.above)
        wires.arrive(at + RD, slots.at[at + RD], place.below)
        total[n] = plus(slots.at[at + RX], slots.at[at + RU], slots.at[at + RD], term(unit, chip))
        gather_first(place, wires, 28, unit, total.at[n], slot)
        copy = pltpu.make_async_copy(total.at[n], slot(unit, chip), local_sem.at[len(local)])
        copy.start()
        local.append(copy)
        wires.send(56 + passed[0], total.at[n], slot(unit, chip), place.partner)
        order.append((unit, chip))
        passed[0] += 1
    for unit in UNITS:
        gather_second(place, wires, 28, unit, slot, landed)
    for unit in UNITS:
        gather_third(place, wires, 28, unit, slot, landed)
    for unit in UNITS:
        gather_last(place, wires, 28, unit, slot, landed)
    theirs = pl.ds(pl.multiple_of((1 - place.core) * 512, 512), 512)
    for n, (unit, at) in enumerate(order):
        span = place.span(at, 1 - unit[1])
        wires.arrive(56 + n, all_kv[unit[0]].at[span, :, theirs], place.partner)
    for copy in far:
        copy.wait_send()
    wires.arrive(index, dq_u, place.partner)
    wires.arrive(index + 1, dq_d, place.partner)
    for n, (out, there) in enumerate(((up_out, after), (down_out, before))):
        for flip, dev in ((0, place.me), (1, place.partner)):
            half = pl.ds(pl.multiple_of((place.core + flip * (1 - 2 * place.core)) * 2048, 2048), 2048)
            pltpu.make_async_remote_copy(
                src_ref=out.at[:, half], dst_ref=out.at[:, half], send_sem=send_sem.at[index + 2 + 2 * n + flip],
                recv_sem=recv_sem.at[index + 2 + 2 * n + flip], device_id={"section": there, "ctx": dev},
                device_id_type=MESH_ID).wait_recv()
    for copy in local:
        copy.wait()
    wires.finish()


def reduce_terms(*operands):
    hbm = pl.BlockSpec(memory_space=pl.ANY)
    vmem = pl.BlockSpec(memory_space=pltpu.VMEM)
    row = jax.ShapeDtypeStruct((128, 4096), BF)
    half = jax.ShapeDtypeStruct((128, 2048), BF)
    whole = jax.ShapeDtypeStruct((16, 128, 1024), BF)
    return pl.pallas_call(
        reduce_kernel,
        in_specs=[vmem] * 2 + [hbm] * 6,
        out_specs=[hbm] * 6,
        out_shape=[row] * 2 + [half] * 2 + [whole] * 2,
        scratch_shapes=[pltpu.VMEM((28, 128, 512), BF), pltpu.VMEM((12, 128, 512), BF), pltpu.VMEM((4, 128, 512), BF),
                        pltpu.SemaphoreType.DMA((94,)), pltpu.SemaphoreType.DMA((94,)), pltpu.SemaphoreType.DMA((4,))],
        compiler_params=pltpu.CompilerParams(collective_id=2, has_side_effects=True, vmem_limit_bytes=32 << 20),
        name="reduce_terms",
    )(*operands)


def gains_kernel(g_ref, gd_out, gu_out, parts, mine, send_sem, recv_sem):
    me = lax.axis_index("ctx")
    section = lax.axis_index("section")
    barrier = pltpu.get_barrier_semaphore()
    pl.semaphore_signal(barrier, inc=1, device_id={"section": 7 - section}, device_id_type=MESH_ID)
    for step in range(1, 16):
        pl.semaphore_signal(barrier, inc=1, device_id={"ctx": (me + step) % 16}, device_id_type=MESH_ID)
    pl.semaphore_wait(barrier, 16)
    copies = []
    for step in range(1, 16):
        to = (me + step) % 16
        copy = pltpu.make_async_remote_copy(
            src_ref=g_ref.at[to], dst_ref=parts.at[step], send_sem=send_sem.at[step], recv_sem=recv_sem.at[step],
            device_id={"ctx": to}, device_id_type=MESH_ID)
        copy.start()
        copies.append(copy)
    value = g_ref[me]
    for step in range(1, 16):
        copies[step - 1].wait_recv()
        value = value + parts[step]
    mine[...] = value
    gd_out[...] = value
    last = pltpu.make_async_remote_copy(src_ref=mine, dst_ref=gu_out, send_sem=send_sem.at[0], recv_sem=recv_sem.at[0],
                                        device_id={"section": 7 - section}, device_id_type=MESH_ID)
    last.start()
    for copy in copies:
        copy.wait_send()
    last.wait()


def sum_gains(gains):
    vmem = pl.BlockSpec(memory_space=pltpu.VMEM)
    small = jax.ShapeDtypeStruct((8, 256), F32)
    return pl.pallas_call(
        gains_kernel,
        in_specs=[vmem],
        out_specs=[vmem, vmem],
        out_shape=[small, small],
        scratch_shapes=[pltpu.VMEM((16, 8, 256), F32), pltpu.VMEM((8, 256), F32),
                        pltpu.SemaphoreType.DMA((16,)), pltpu.SemaphoreType.DMA((16,))],
        compiler_params=pltpu.CompilerParams(collective_id=3, has_side_effects=True),
        name="sum_gains",
    )(gains)


def by_head(kv):
    return kv.reshape(-1, 2, 4, 128).transpose(0, 2, 1, 3).reshape(-1, 1024)


def by_kind(kv):
    return kv.reshape(-1, 4, 2, 128).transpose(0, 2, 1, 3).reshape(-1, 1024)


def prepare(x, gain, weight):
    xf = x.astype(F32)
    recip = lax.rsqrt(jnp.mean(xf * xf, -1, keepdims=True) + EPS)
    normed = xf * recip
    act = (normed * gain[None, :]).astype(BF)
    kv = jnp.dot(act, weight, preferred_element_type=F32).astype(BF)
    return recip, act, by_head(kv)


def complete(x, recip, cot, gain, weight, dquery, dkv):
    normed = x.astype(F32) * recip
    dact = dquery.astype(F32) + lax.dot_general(by_kind(dkv), weight, NT, preferred_element_type=F32)
    gpart = jnp.sum(dact * normed, 0)
    dnormed = dact * gain[None, :]
    dx = cot.astype(F32) + recip * (dnormed - normed * jnp.mean(dnormed * normed, -1, keepdims=True))
    return dx.astype(BF), gpart


def halves_joined(core, mine, other):
    return jnp.where(core == 0, jnp.concatenate([mine, other], 1), jnp.concatenate([other, mine], 1))


def per_device(down_in, up_in, down_cot, up_cot, kv_weight, norm_gain, span_ids):
    own = lax.axis_index("ctx")
    core = own % 2
    x_d, x_u, cot_d, cot_u = down_in[0], up_in[0], down_cot[0], up_cot[0]
    gain_d, gain_u = norm_gain[0, 0], norm_gain[1, 0]
    weight_d, weight_u = kv_weight[0, 0], kv_weight[1, 0]
    scalars = jnp.stack([span_ids[own], span_ids[own + 1 - 2 * core], core]).astype(jnp.int32)
    inverse = jnp.argsort(span_ids).astype(jnp.int32)
    recip_u, act_u, kv_u = prepare(x_u, gain_u, weight_u)
    recip_d, act_d, kv_d = prepare(x_d, gain_d, weight_d)
    q_d, q_u, dy_d, dy_u, xh_d, xh_u, all_d, all_u = spread(act_d, act_u, cot_d, cot_u, x_d, x_u, kv_d, kv_u)
    features = jnp.stack([act_d, act_u]).reshape(2, 128, 16, 256).transpose(2, 0, 1, 3)
    features = lax.all_to_all(features, "ctx", 0, 0, tiled=False)
    yo_u, yg_u, dqo_u, dqg_u, terms_u = attention((act_u, q_u), (cot_u, dy_u), (x_u, xh_u), all_u, scalars, inverse)
    yo_d, yg_d, dqo_d, dqg_d, terms_d = attention((act_d, q_d), (cot_d, dy_d), (x_d, xh_d), all_d, scalars, inverse)
    down_out, up_out, dq_d, dq_u, dkv_d, dkv_u = reduce_terms(
        terms_d, terms_u, yo_d, yg_d, yo_u, yg_u, dqg_d, dqg_u)
    wgrad = lambda which, dkv: lax.dot_general(
        features[:, which].reshape(2048, 256), dkv.reshape(2048, 1024), TN, preferred_element_type=F32)
    sections = lax.axis_size("section")
    mirror_w = lax.ppermute(wgrad(1, dkv_u).astype(BF), "section", [(i, sections - 1 - i) for i in range(sections)])
    own_dkv = lambda dkv: lax.dynamic_index_in_dim(dkv, own, 0, False)
    grad_u, gpart_u = complete(x_u, recip_u, cot_u, gain_u, weight_u, halves_joined(core, dqo_u, dq_u), own_dkv(dkv_u))
    grad_d, gpart_d = complete(x_d, recip_d, cot_d, gain_d, weight_d, halves_joined(core, dqo_d, dq_d), own_dkv(dkv_d))
    gains = jnp.stack([gpart_d, gpart_u] + [jnp.zeros_like(gpart_d)] * 6).reshape(8, 16, 256).transpose(1, 0, 2)
    gain_here, gain_there = sum_gains(gains)
    kv_grad = by_kind(wgrad(0, dkv_d) + mirror_w.astype(F32))[None]
    gain_grad = (gain_here[0] + gain_there[1])[None]
    return (down_out[None], up_out[None], grad_d[None], grad_u[None], kv_grad, gain_grad)


def solution(mesh):
    row = P("section", "ctx", None)
    in_specs = (row, row, row, row, P(None, "section", None, None), P(None, "section", None), P())
    out_specs = (row, row, row, row, row, P("section", "ctx"))
    return jax.shard_map(per_device, mesh=mesh, in_specs=in_specs, out_specs=out_specs, check_vma=False)
```

```python
import functools

import jax
import jax.numpy as jnp
from jax import lax
from jax.experimental import pallas as pl
from jax.experimental.pallas import tpu as pltpu
from jax.sharding import PartitionSpec as P

LOG2E = 1.4426950408889634
NT = (((1,), (1,)), ((), ()))
TN = (((0,), (0,)), ((), ()))
F32 = jnp.float32
BF = jnp.bfloat16


def stack_heads(block):
    return jnp.concatenate([block[:, j * 128:(j + 1) * 128] for j in range(8)], 0)


def spread_heads(rows):
    return jnp.concatenate([rows[j * 128:(j + 1) * 128] for j in range(8)], 1)


def attention_kernel(kf, kb, tq_ref, inv_ref, q_own, q_got, dy_own, dy_got, x_own, x_got, kv_hbm,
                     y_own, y_got, dq_own, dq_got, terms_ref, kv_s, dk_s, dv_s, sems):
    head = pl.program_id(0)
    spans = kv_hbm.shape[0]
    scale = 128 ** -0.5
    c = scale * LOG2E

    @pl.when(head == 0)
    def _():
        copies = [pltpu.make_async_copy(kv_hbm.at[inv_ref[t]], kv_s.at[pl.ds(t * 128, 128)], sems.at[t])
                  for t in range(spans)]
        for cp in copies:
            cp.start()
        for cp in copies:
            cp.wait()

    dk_s[...] = jnp.zeros_like(dk_s)
    dv_s[...] = jnp.zeros_like(dv_s)
    kcol = pl.multiple_of(head * 256, 256)
    vcol = pl.multiple_of(head * 256 + 128, 128)

    def span(qi, q_ref, dy_ref, x_ref, y_ref, dq_ref):
        t = tq_ref[qi]
        q = stack_heads(q_ref[...])
        dy = stack_heads(dy_ref[...])
        rows = q.shape[0]

        def fwd(b, carry, masked):
            m, l, acc = carry
            at = pl.multiple_of(b * kf, kf)
            k = kv_s[pl.ds(at, kf), pl.ds(kcol, 128)]
            v = kv_s[pl.ds(at, kf), pl.ds(vcol, 128)]
            s = lax.dot_general(q, k, NT, preferred_element_type=F32) * c
            if masked:
                kpos = at + lax.broadcasted_iota(jnp.int32, (128, kf), 1)
                qpos = t * 128 + lax.broadcasted_iota(jnp.int32, (128, kf), 0)
                s = jnp.where((kpos <= qpos)[None], s.reshape(8, 128, kf), -1e30).reshape(rows, kf)
            m_new = jnp.maximum(m, jnp.max(s, 1, keepdims=True))
            e = jnp.exp2(s - m_new)
            fade = jnp.exp2(m - m_new)
            l = l * fade + jnp.sum(e, 1, keepdims=True)
            acc = acc * fade + lax.dot_general(e.astype(BF), v, (((1,), (0,)), ((), ())), preferred_element_type=F32)
            return m_new, l, acc

        nf = (t * 128) // kf
        carry = (jnp.full((rows, 1), -1e30, F32), jnp.zeros((rows, 1), F32), jnp.zeros((rows, 128), F32))
        carry = lax.fori_loop(0, nf, lambda b, cr: fwd(b, cr, False), carry)
        m, l, acc = fwd(nf, carry, True)
        mixed = acc / l
        y_ref[...] = (x_ref[...].astype(F32) + spread_heads(mixed)).astype(y_ref.dtype)
        lse = m + jnp.log2(l)
        delta = jnp.sum(dy.astype(F32) * mixed, 1, keepdims=True)
        lse_r = jnp.transpose(jnp.broadcast_to(lse, (rows, 128)))[0:1]
        delta_r = jnp.transpose(jnp.broadcast_to(delta, (rows, 128)))[0:1]

        def bwd(b, dq, masked):
            at = pl.multiple_of(b * kb, kb)
            k = kv_s[pl.ds(at, kb), pl.ds(kcol, 128)]
            v = kv_s[pl.ds(at, kb), pl.ds(vcol, 128)]
            s = lax.dot_general(k, q, NT, preferred_element_type=F32) * c
            p = jnp.exp2(s - lse_r)
            if masked:
                kpos = at + lax.broadcasted_iota(jnp.int32, (kb, 128), 0)
                qpos = t * 128 + lax.broadcasted_iota(jnp.int32, (kb, 128), 1)
                vis = kpos <= qpos
                p = jnp.concatenate([jnp.where(vis, p[:, j * 128:(j + 1) * 128], 0.0) for j in range(8)], 1)
            dp = lax.dot_general(v, dy, NT, preferred_element_type=F32)
            ds = (p * (dp - delta_r)).astype(BF)
            dv_s[pl.ds(at, kb)] += jnp.dot(p.astype(BF), dy, preferred_element_type=F32)
            dk_s[pl.ds(at, kb)] += jnp.dot(ds, q, preferred_element_type=F32)
            return dq + lax.dot_general(ds, k, TN, preferred_element_type=F32)

        nb = (t * 128) // kb
        dq = jnp.zeros((rows, 128), F32)
        dq = lax.fori_loop(0, nb, lambda b, cr: bwd(b, cr, False), dq)
        dq = bwd(nb, dq, True)
        dq_ref[...] = spread_heads(dq * scale).astype(dq_ref.dtype)

    span(0, q_own, dy_own, x_own, y_own, dq_own)
    span(1, q_got, dy_got, x_got, y_got, dq_got)
    for t in range(spans):
        at = pl.ds(pl.multiple_of(inv_ref[t] * 128, 128), 128)
        terms_ref[at, 0:128] = (dk_s[t * 128:(t + 1) * 128] * scale).astype(BF)
        terms_ref[at, 128:256] = dv_s[t * 128:(t + 1) * 128].astype(BF)


def attention(q, dy, x, kv, tq, inv, kf=1024, kb=512):
    spans = kv.shape[0]
    count = kv.shape[2] // 256
    own = pl.BlockSpec((128, 1024), lambda h, tq, inv: (0, tq[2] * count + h))
    got = pl.BlockSpec((128, 1024), lambda h, tq, inv: (0, h))
    flops = 2 * 7 * 2 * count * 1024 * spans * 128 * 128
    rows = jax.ShapeDtypeStruct((128, count * 1024), BF)
    return pl.pallas_call(
        functools.partial(attention_kernel, kf, kb),
        grid_spec=pltpu.PrefetchScalarGridSpec(
            num_scalar_prefetch=2,
            grid=(count,),
            in_specs=[own, got] * 3 + [pl.BlockSpec(memory_space=pl.ANY)],
            out_specs=[got] * 4 + [pl.BlockSpec((spans * 128, 256), lambda h, tq, inv: (0, h))],
            scratch_shapes=[pltpu.VMEM((spans * 128, count * 256), BF), pltpu.VMEM((spans * 128, 128), F32),
                            pltpu.VMEM((spans * 128, 128), F32), pltpu.SemaphoreType.DMA((spans,))],
        ),
        out_shape=[rows] * 4 + [jax.ShapeDtypeStruct((spans * 128, count * 256), BF)],
        compiler_params=pltpu.CompilerParams(vmem_limit_bytes=50 << 20),
        cost_estimate=pl.CostEstimate(flops=flops, bytes_accessed=16 << 20, transcendentals=0),
        name="attention",
    )(tq, inv, *q, *dy, *x, kv)


MESH_ID = pl.DeviceIdType.MESH
EPS = 1e-05
DOWN, UP = 0, 1
OWN, PAIR = 0, 1
UNITS = [(UP, OWN), (UP, PAIR), (DOWN, OWN), (DOWN, PAIR)]


class Place:
    def __init__(self):
        self.me = lax.axis_index("ctx")
        self.core = self.me % 2
        self.chip = self.me // 2
        beside = self.chip % 2
        self.partner = self.me + 1 - 2 * self.core
        self.across = self.me + 2 - 4 * beside
        self.above = (self.me + 4) % 16
        self.below = (self.me + 12) % 16
        self.chip_x = self.chip + 1 - 2 * beside

    def greet_all(self, barrier):
        for step in range(1, 16):
            pl.semaphore_signal(barrier, inc=1, device_id={"ctx": (self.me + step) % 16}, device_id_type=MESH_ID)
        mirrored = 7 - lax.axis_index("section")
        pl.semaphore_signal(barrier, inc=1, device_id={"section": mirrored}, device_id_type=MESH_ID)
        pl.semaphore_wait(barrier, 16)

    def greet(self, barrier):
        for dev in (self.partner, self.across, self.above, self.below):
            pl.semaphore_signal(barrier, inc=1, device_id={"ctx": dev}, device_id_type=MESH_ID)
        pl.semaphore_wait(barrier, 4)

    def span(self, chip, kind):
        return 2 * chip + (self.core if kind == OWN else 1 - self.core)

    def up(self, chip, by):
        return (chip + 2 * by) % 8


class Wires:
    def __init__(self, send_sem, recv_sem):
        self.send_sem, self.recv_sem, self.started = send_sem, recv_sem, []

    def copy(self, index, src, dst, dev):
        return pltpu.make_async_remote_copy(
            src_ref=src, dst_ref=dst, send_sem=self.send_sem.at[index], recv_sem=self.recv_sem.at[index],
            device_id={"ctx": dev}, device_id_type=MESH_ID)

    def send(self, index, src, dst, dev):
        copy = self.copy(index, src, dst, dev)
        copy.start()
        self.started.append(copy)

    def far_send(self, index, src, dst, section):
        copy = pltpu.make_async_remote_copy(
            src_ref=src, dst_ref=dst, send_sem=self.send_sem.at[index], recv_sem=self.recv_sem.at[index],
            device_id={"section": section}, device_id_type=MESH_ID)
        copy.start()
        self.started.append(copy)
        return copy

    def arrive(self, index, ref, dev):
        self.copy(index, ref, ref, dev).wait_recv()

    def finish(self):
        for copy in self.started:
            copy.wait_send()


X, ZM, ZP, XZM, XZP, AN, XA = range(7)


def gather_first(place, wires, base, unit, src, slot):
    kind = unit[1]
    at = base + 7 * UNITS.index(unit)
    here = slot(unit, place.chip)
    wires.send(at + X, src, here, place.across)
    wires.send(at + ZM, src, here, place.above)
    wires.send(at + ZP, src, here, place.below)


def gather_second(place, wires, base, unit, slot, landed):
    kind = unit[1]
    at = base + 7 * UNITS.index(unit)
    cx = slot(unit, place.chip_x)
    wires.arrive(at + X, cx, place.across)
    wires.send(at + XZM, cx, cx, place.above)
    wires.send(at + XZP, cx, cx, place.below)
    landed(unit, place.chip_x)
    lo, hi = slot(unit, place.up(place.chip, 3)), slot(unit, place.up(place.chip, 1))
    wires.arrive(at + ZM, lo, place.below)
    if kind == OWN:
        wires.send(at + AN, lo, lo, place.above)
    wires.arrive(at + ZP, hi, place.above)
    if kind == PAIR:
        wires.send(at + AN, hi, hi, place.below)
    landed(unit, place.up(place.chip, 3))
    landed(unit, place.up(place.chip, 1))


def gather_third(place, wires, base, unit, slot, landed):
    at = base + 7 * UNITS.index(unit)
    far = slot(unit, place.up(place.chip, 2))
    wires.arrive(at + AN, far, place.below if unit[1] == OWN else place.above)
    wires.send(at + XA, far, far, place.across)
    landed(unit, place.up(place.chip, 2))
    for kind, by, dev in ((XZM, 3, place.below), (XZP, 1, place.above)):
        chip = place.up(place.chip_x, by)
        wires.arrive(at + kind, slot(unit, chip), dev)
        landed(unit, chip)


def gather_last(place, wires, base, unit, slot, landed):
    at = base + 7 * UNITS.index(unit)
    chip = place.up(place.chip_x, 2)
    wires.arrive(at + XA, slot(unit, chip), place.across)
    landed(unit, chip)


def nothing(unit, chip):
    pass


def spread_kernel(act_d, act_u, cot_d, cot_u, x_d, x_u, kv_d, kv_u,
                  q_d, q_u, dy_d, dy_u, xh_d, xh_u, all_d, all_u, send_sem, recv_sem, local_sem):
    place = Place()
    wires = Wires(send_sem, recv_sem)
    place.greet(pltpu.get_barrier_semaphore())
    all_kv, kv = (all_d, all_u), (kv_d, kv_u)
    mine = pl.ds(pl.multiple_of(place.core * 512, 512), 512)
    other = lambda width: pl.ds(pl.multiple_of((1 - place.core) * width, width), width)
    slot = lambda unit, chip: all_kv[unit[0]].at[place.span(chip, unit[1])]
    local = []
    for layer in (UP, DOWN):
        wires.send(28 + layer, kv[layer].at[:, other(512)], all_kv[layer].at[place.me], place.partner)
    for layer in (UP, DOWN):
        gather_first(place, wires, 0, (layer, OWN), kv[layer].at[:, mine], slot)
        copy = pltpu.make_async_copy(kv[layer].at[:, mine], all_kv[layer].at[place.me], local_sem.at[layer])
        copy.start()
        local.append(copy)
    for layer in (UP, DOWN):
        wires.arrive(28 + layer, all_kv[layer].at[place.partner], place.partner)
        gather_first(place, wires, 0, (layer, PAIR), slot((layer, PAIR), place.chip), slot)
    halves = ((act_u, q_u), (cot_u, dy_u), (x_u, xh_u), (act_d, q_d), (cot_d, dy_d), (x_d, xh_d))
    for n, (src, dst) in enumerate(halves):
        wires.send(30 + n, src.at[:, other(2048)], dst, place.partner)
    for unit in UNITS:
        gather_second(place, wires, 0, unit, slot, nothing)
    for unit in UNITS:
        gather_third(place, wires, 0, unit, slot, nothing)
    for unit in UNITS:
        gather_last(place, wires, 0, unit, slot, nothing)
    for n, (src, dst) in enumerate(halves):
        wires.arrive(30 + n, dst, place.partner)
    for copy in local:
        copy.wait()
    wires.finish()


def spread(*operands):
    half = jax.ShapeDtypeStruct((128, 2048), BF)
    hbm = pl.BlockSpec(memory_space=pl.ANY)
    return pl.pallas_call(
        spread_kernel,
        in_specs=[hbm] * 6 + [pl.BlockSpec(memory_space=pltpu.VMEM)] * 2,
        out_specs=[hbm] * 8,
        out_shape=[half] * 6 + [jax.ShapeDtypeStruct((16, 128, 512), BF)] * 2,
        scratch_shapes=[pltpu.SemaphoreType.DMA((36,)), pltpu.SemaphoreType.DMA((36,)), pltpu.SemaphoreType.DMA((2,))],
        compiler_params=pltpu.CompilerParams(collective_id=1, has_side_effects=True),
        name="spread",
    )(*operands)


R0, RA, RB, R1, RU, RD, RX = range(7)


HANDED, DQ, GAINS, FAR = 56, 88, 90, 120


def finish_kernel(terms_d, terms_u, dqo_d, dqo_u, dqg_d, dqg_u, x_d, x_u, cot_d, cot_u, gains, features, w_d, w_u,
                  grad_d, grad_u, kv_grad, gain_grad,
                  slots, stage, total, all_kv, dquery, weight, dact, gparts, ggot, gsum, acc, wsend, wgot, ggot_far,
                  send_sem, recv_sem, local_sem):
    place = Place()
    wires = Wires(send_sem, recv_sem)
    mirrored = 7 - lax.axis_index("section")
    terms = (terms_d, terms_u)
    chip, chip_x = place.chip, place.chip_x
    wide = pl.ds(pl.multiple_of(place.core * 2048, 2048), 2048)
    local = []

    def keep(src, dst):
        copy = pltpu.make_async_copy(src, dst, local_sem.at[len(local)])
        copy.start()
        local.append(copy)
        return copy

    loads = {UP: keep(w_u, weight.at[UP]), DOWN: keep(w_d, weight.at[DOWN])}
    place.greet_all(pltpu.get_barrier_semaphore())

    def term(unit, at):
        return terms[unit[0]].at[pl.ds(pl.multiple_of(place.span(at, unit[1]) * 128, 128), 128)]

    def plus(*refs):
        value = refs[0][...].astype(F32)
        for ref in refs[1:]:
            value = value + ref[...].astype(F32)
        return value.astype(BF)

    for n, unit in enumerate(UNITS):
        at = 7 * n
        wires.send(at + R0, term(unit, place.up(chip_x, 2)), slots.at[at + R0], place.across)
        wires.send(at + RA, term(unit, place.up(chip_x, 1)), slots.at[at + RA], place.above)
        wires.send(at + RB, term(unit, place.up(chip_x, 3)), slots.at[at + RB], place.below)
        if unit[1] == OWN:
            wires.send(at + RD, term(unit, place.up(chip, 1)), slots.at[at + RD], place.above)
        else:
            wires.send(at + RU, term(unit, place.up(chip, 3)), slots.at[at + RU], place.below)
    for layer, own_part, sent in ((UP, dqo_u, dqg_u), (DOWN, dqo_d, dqg_d)):
        wires.send(DQ + layer, sent, dquery.at[layer, :, wide], place.partner)
        loads[layer + 2] = keep(own_part, dquery.at[layer, :, wide])
    for n, unit in enumerate(UNITS):
        at = 7 * n
        wires.arrive(at + R0, slots.at[at + R0], place.across)
        stage[3 * n] = plus(slots.at[at + R0], term(unit, place.up(chip, 2)))
        wires.send(at + R1, stage.at[3 * n], slots.at[at + R1], place.below if unit[1] == OWN else place.above)
    for n, unit in enumerate(UNITS):
        at = 7 * n
        wires.arrive(at + RA, slots.at[at + RA], place.below)
        wires.arrive(at + RB, slots.at[at + RB], place.above)
        stage[3 * n + 1] = plus(slots.at[at + RA], slots.at[at + RB], term(unit, chip_x))
        wires.send(at + RX, stage.at[3 * n + 1], slots.at[at + RX], place.across)
        if unit[1] == OWN:
            wires.arrive(at + R1, slots.at[at + R1], place.above)
            stage[3 * n + 2] = plus(slots.at[at + R1], term(unit, place.up(chip, 3)))
            wires.send(at + RU, stage.at[3 * n + 2], slots.at[at + RU], place.below)
        else:
            wires.arrive(at + R1, slots.at[at + R1], place.below)
            stage[3 * n + 2] = plus(slots.at[at + R1], term(unit, place.up(chip, 1)))
            wires.send(at + RD, stage.at[3 * n + 2], slots.at[at + RD], place.above)

    slot = lambda unit, at: all_kv.at[unit[0], place.core, place.span(at, unit[1])]
    order = []

    def landed(unit, at):
        ref = slot(unit, at)
        wires.send(HANDED + len(order), ref, ref, place.partner)
        order.append((unit, at))

    for n, unit in enumerate(UNITS):
        at = 7 * n
        wires.arrive(at + RX, slots.at[at + RX], place.across)
        wires.arrive(at + RU, slots.at[at + RU], place.above)
        wires.arrive(at + RD, slots.at[at + RD], place.below)
        total[n] = plus(slots.at[at + RX], slots.at[at + RU], slots.at[at + RD], term(unit, chip))
        gather_first(place, wires, 28, unit, total.at[n], slot)
        loads[4 + n] = keep(total.at[n], slot(unit, chip))
        wires.send(HANDED + n, total.at[n], slot(unit, chip), place.partner)
        order.append((unit, chip))

    waited = set()

    def handed(chosen):
        for n, (unit, at) in enumerate(order):
            if chosen(unit, at) and n not in waited:
                waited.add(n)
                ref = all_kv.at[unit[0], 1 - place.core, place.span(at, 1 - unit[1])]
                wires.arrive(HANDED + n, ref, place.partner)

    def complete(layer, x_ref, cot_ref, grad_ref):
        for n, unit in enumerate(UNITS):
            if unit[0] == layer:
                loads[4 + n].wait()
        handed(lambda unit, at: unit[0] == layer and at is chip)
        loads[layer].wait()
        loads[layer + 2].wait()
        wires.arrive(DQ + layer, dquery.at[layer, :, pl.ds(pl.multiple_of((1 - place.core) * 2048, 2048), 2048)], place.partner)
        halves = [all_kv[layer, half, place.me] for half in range(2)]
        dkv = jnp.concatenate([halves[h // 2][:, (h % 2) * 256 + kind * 128:(h % 2) * 256 + kind * 128 + 128]
                               for kind in range(2) for h in range(4)], 1)
        total_sq = jnp.zeros((128, 1), F32)
        for tile in range(8):
            part = x_ref[:, tile * 512:(tile + 1) * 512].astype(F32)
            total_sq = total_sq + jnp.sum(part * part, 1, keepdims=True)
        recip = lax.rsqrt(total_sq / 4096 + EPS)

        def first(tile, dots):
            cols = pl.ds(pl.multiple_of(tile * 512, 512), 512)
            normed = x_ref[:, cols].astype(F32) * recip
            value = dquery[layer, :, cols].astype(F32) + lax.dot_general(
                dkv, weight[layer, cols, :], NT, preferred_element_type=F32)
            dact[:, cols] = value
            product = value * normed
            column = jnp.sum(product, 0, keepdims=True)
            for half in range(2):
                gparts[layer, 2 * tile + half] = jnp.broadcast_to(column[:, half * 256:(half + 1) * 256], (8, 256))
            return dots + jnp.sum(product * gains[layer:layer + 1, cols], 1, keepdims=True)

        dots = lax.fori_loop(0, 8, first, jnp.zeros((128, 1), F32))
        for step in range(1, 16):
            to = (place.me + step) % 16
            wires.send(GAINS + 15 * layer + step - 1, gparts.at[layer, to], ggot.at[layer, step], to)
        mean = dots / 4096

        def second(tile, _):
            cols = pl.ds(pl.multiple_of(tile * 512, 512), 512)
            normed = x_ref[:, cols].astype(F32) * recip
            dnormed = dact[:, cols] * gains[layer:layer + 1, cols]
            grad_ref[:, cols] = (cot_ref[:, cols].astype(F32) + recip * (dnormed - normed * mean)).astype(BF)
            return 0

        lax.fori_loop(0, 8, second, 0)

    def gain_total(layer):
        value = gparts[layer, place.me]
        for step in range(1, 16):
            wires.arrive(GAINS + 15 * layer + step - 1, ggot.at[layer, step], (place.me + step) % 16)
            value = value + ggot[layer, step]
        return value

    def weight_grad(layer):
        acc[...] = jnp.zeros_like(acc)

        def step(n, _):
            two = pl.ds(2 * n, 2)
            act = features[two, layer].reshape(256, 256)
            for half in range(2):
                dkv = all_kv[layer, half, two].reshape(256, 512)
                acc[:, half * 512:(half + 1) * 512] += lax.dot_general(act, dkv, TN, preferred_element_type=F32)
            return 0

        lax.fori_loop(0, 8, step, 0)

    up, down = UNITS[:2], UNITS[2:]
    complete(UP, x_u, cot_u, grad_u)
    for unit in UNITS:
        gather_second(place, wires, 28, unit, slot, landed)
    complete(DOWN, x_d, cot_d, grad_d)
    for unit in UNITS:
        gather_third(place, wires, 28, unit, slot, landed)
    for unit in up:
        gather_last(place, wires, 28, unit, slot, landed)
    handed(lambda unit, at: unit[0] == UP)
    weight_grad(UP)
    wsend[...] = acc[...].astype(BF)
    far_w = wires.far_send(FAR, wsend, wgot, mirrored)
    gsum[...] = gain_total(UP)
    far_g = wires.far_send(FAR + 1, gsum, ggot_far, mirrored)
    for unit in down:
        gather_last(place, wires, 28, unit, slot, landed)
    handed(lambda unit, at: True)
    weight_grad(DOWN)
    mine = gain_total(DOWN)
    far_g.wait_recv()
    gain_grad[...] = mine + ggot_far[...]
    far_w.wait_recv()
    for h in range(4):
        for kind in range(2):
            came = slice(h * 256 + kind * 128, h * 256 + kind * 128 + 128)
            goes = slice(kind * 512 + h * 128, kind * 512 + h * 128 + 128)
            kv_grad[:, goes] = acc[:, came] + wgot[:, came].astype(F32)
    wires.finish()


def finish(terms_d, terms_u, dqo_d, dqo_u, dqg_d, dqg_u, x_d, x_u, cot_d, cot_u, gains, features, w_d, w_u):
    hbm = pl.BlockSpec(memory_space=pl.ANY)
    vmem = pl.BlockSpec(memory_space=pltpu.VMEM)
    row = jax.ShapeDtypeStruct((128, 4096), BF)
    operands = (terms_d, terms_u, dqo_d, dqo_u, dqg_d, dqg_u, x_d, x_u, cot_d, cot_u, gains, features, w_d, w_u)
    unit = lambda count: pltpu.VMEM((count, 128, 512), BF)
    return pl.pallas_call(
        finish_kernel,
        in_specs=[vmem] * 12 + [hbm] * 2,
        out_specs=[vmem] * 4,
        out_shape=[row, row, jax.ShapeDtypeStruct((256, 1024), F32), jax.ShapeDtypeStruct((8, 256), F32)],
        scratch_shapes=[unit(28), unit(12), unit(4), pltpu.VMEM((2, 2, 16, 128, 512), BF), pltpu.VMEM((2, 128, 4096), BF),
                        pltpu.VMEM((2, 4096, 1024), BF), pltpu.VMEM((128, 4096), F32), pltpu.VMEM((2, 16, 8, 256), F32),
                        pltpu.VMEM((2, 16, 8, 256), F32), pltpu.VMEM((8, 256), F32), pltpu.VMEM((256, 1024), F32),
                        pltpu.VMEM((256, 1024), BF), pltpu.VMEM((256, 1024), BF), pltpu.VMEM((8, 256), F32),
                        pltpu.SemaphoreType.DMA((122,)), pltpu.SemaphoreType.DMA((122,)), pltpu.SemaphoreType.DMA((8,))],
        compiler_params=pltpu.CompilerParams(collective_id=2, has_side_effects=True, vmem_limit_bytes=60 << 20),
        name="finish",
    )(*operands)


def by_head(kv):
    return kv.reshape(-1, 2, 4, 128).transpose(0, 2, 1, 3).reshape(-1, 1024)


def prepare(x, gain, weight):
    xf = x.astype(F32)
    recip = lax.rsqrt(jnp.mean(xf * xf, -1, keepdims=True) + EPS)
    normed = xf * recip
    act = (normed * gain[None, :]).astype(BF)
    kv = jnp.dot(act, weight, preferred_element_type=F32).astype(BF)
    return act, by_head(kv)


def halves_joined(core, mine, other):
    return jnp.where(core == 0, jnp.concatenate([mine, other], 1), jnp.concatenate([other, mine], 1))


def relayed(own, got, core, by):
    sections, spans = lax.axis_size("section"), lax.axis_size("ctx")
    to = lambda flip: [(s * spans + i, (s + by) % sections * spans + (i ^ flip)) for s in range(sections) for i in range(spans)]
    mine = lax.ppermute(own, ("section", "ctx"), to(0))
    other = lax.ppermute(got, ("section", "ctx"), to(1))
    return halves_joined(core, mine, other)


def per_device(down_in, up_in, down_cot, up_cot, kv_weight, norm_gain, span_ids):
    own = lax.axis_index("ctx")
    core = own % 2
    x_d, x_u, cot_d, cot_u = down_in[0], up_in[0], down_cot[0], up_cot[0]
    gain_d, gain_u = norm_gain[0, 0], norm_gain[1, 0]
    weight_d, weight_u = kv_weight[0, 0], kv_weight[1, 0]
    scalars = jnp.stack([span_ids[own], span_ids[own + 1 - 2 * core], core]).astype(jnp.int32)
    order = jnp.arange(16, dtype=jnp.int32)
    inverse = jnp.sum(jnp.where(span_ids[:, None] == order[None, :], order[:, None], 0), 0).astype(jnp.int32)
    act_u, kv_u = prepare(x_u, gain_u, weight_u)
    act_d, kv_d = prepare(x_d, gain_d, weight_d)
    q_d, q_u, dy_d, dy_u, xh_d, xh_u, all_d, all_u = spread(act_d, act_u, cot_d, cot_u, x_d, x_u, kv_d, kv_u)
    after_d, after_u, _ = lax.optimization_barrier((act_d, act_u, q_d))
    features = jnp.stack([after_d, after_u]).reshape(2, 128, 16, 256).transpose(2, 0, 1, 3)
    features = lax.all_to_all(features, "ctx", 0, 0, tiled=False)
    yo_u, yg_u, dqo_u, dqg_u, terms_u = attention((act_u, q_u), (cot_u, dy_u), (x_u, xh_u), all_u, scalars, inverse)
    up_out = relayed(yo_u, yg_u, core, -1)
    yo_d, yg_d, dqo_d, dqg_d, terms_d = attention((act_d, q_d), (cot_d, dy_d), (x_d, xh_d), all_d, scalars, inverse)
    down_out = relayed(yo_d, yg_d, core, 1)
    grad_d, grad_u, kv_grad, gain_grad = finish(
        terms_d, terms_u, dqo_d, dqo_u, dqg_d, dqg_u, x_d, x_u, cot_d, cot_u, norm_gain[:, 0], features, weight_d, weight_u)
    return (down_out[None], up_out[None], grad_d[None], grad_u[None], kv_grad[None], gain_grad[:1])


def solution(mesh):
    row = P("section", "ctx", None)
    in_specs = (row, row, row, row, P(None, "section", None, None), P(None, "section", None), P())
    out_specs = (row, row, row, row, row, P("section", "ctx"))
    return jax.shard_map(per_device, mesh=mesh, in_specs=in_specs, out_specs=out_specs, check_vma=False)
```

```python
import functools

import jax
import jax.numpy as jnp
from jax import lax
from jax.experimental import pallas as pl
from jax.experimental.pallas import tpu as pltpu
from jax.sharding import PartitionSpec as P

LOG2E = 1.4426950408889634
NT = (((1,), (1,)), ((), ()))
TN = (((0,), (0,)), ((), ()))
F32 = jnp.float32
BF = jnp.bfloat16


def stack_heads(block):
    return jnp.concatenate([block[:, j * 128:(j + 1) * 128] for j in range(8)], 0)


def spread_heads(rows):
    return jnp.concatenate([rows[j * 128:(j + 1) * 128] for j in range(8)], 1)


def attention_kernel(kf, kb, tq_ref, inv_ref, q_own, q_got, dy_own, dy_got, x_own, x_got, kv_hbm,
                     y_own, y_got, dq_own, dq_got, terms_ref, kv_s, dk_s, dv_s, sems):
    head = pl.program_id(0)
    spans = kv_hbm.shape[0]
    scale = 128 ** -0.5
    c = scale * LOG2E

    @pl.when(head == 0)
    def _():
        copies = [pltpu.make_async_copy(kv_hbm.at[inv_ref[t]], kv_s.at[pl.ds(t * 128, 128)], sems.at[t])
                  for t in range(spans)]
        for cp in copies:
            cp.start()
        for cp in copies:
            cp.wait()

    dk_s[...] = jnp.zeros_like(dk_s)
    dv_s[...] = jnp.zeros_like(dv_s)
    kcol = pl.multiple_of(head * 256, 256)
    vcol = pl.multiple_of(head * 256 + 128, 128)

    def span(qi, q_ref, dy_ref, x_ref, y_ref, dq_ref):
        t = tq_ref[qi]
        q = stack_heads(q_ref[...])
        dy = stack_heads(dy_ref[...])
        rows = q.shape[0]

        def fwd(b, carry, masked):
            m, l, acc = carry
            at = pl.multiple_of(b * kf, kf)
            k = kv_s[pl.ds(at, kf), pl.ds(kcol, 128)]
            v = kv_s[pl.ds(at, kf), pl.ds(vcol, 128)]
            s = lax.dot_general(q, k, NT, preferred_element_type=F32) * c
            if masked:
                kpos = at + lax.broadcasted_iota(jnp.int32, (128, kf), 1)
                qpos = t * 128 + lax.broadcasted_iota(jnp.int32, (128, kf), 0)
                s = jnp.where((kpos <= qpos)[None], s.reshape(8, 128, kf), -1e30).reshape(rows, kf)
            m_new = jnp.maximum(m, jnp.max(s, 1, keepdims=True))
            e = jnp.exp2(s - m_new)
            fade = jnp.exp2(m - m_new)
            l = l * fade + jnp.sum(e, 1, keepdims=True)
            acc = acc * fade + lax.dot_general(e.astype(BF), v, (((1,), (0,)), ((), ())), preferred_element_type=F32)
            return m_new, l, acc

        nf = (t * 128) // kf
        carry = (jnp.full((rows, 1), -1e30, F32), jnp.zeros((rows, 1), F32), jnp.zeros((rows, 128), F32))
        carry = lax.fori_loop(0, nf, lambda b, cr: fwd(b, cr, False), carry)
        m, l, acc = fwd(nf, carry, True)
        mixed = acc / l
        y_ref[...] = (x_ref[...].astype(F32) + spread_heads(mixed)).astype(y_ref.dtype)
        lse = m + jnp.log2(l)
        delta = jnp.sum(dy.astype(F32) * mixed, 1, keepdims=True)
        lse_r = jnp.transpose(jnp.broadcast_to(lse, (rows, 128)))[0:1]
        delta_r = jnp.transpose(jnp.broadcast_to(delta, (rows, 128)))[0:1]

        def bwd(b, dq, masked):
            at = pl.multiple_of(b * kb, kb)
            k = kv_s[pl.ds(at, kb), pl.ds(kcol, 128)]
            v = kv_s[pl.ds(at, kb), pl.ds(vcol, 128)]
            s = lax.dot_general(k, q, NT, preferred_element_type=F32) * c
            p = jnp.exp2(s - lse_r)
            if masked:
                kpos = at + lax.broadcasted_iota(jnp.int32, (kb, 128), 0)
                qpos = t * 128 + lax.broadcasted_iota(jnp.int32, (kb, 128), 1)
                vis = kpos <= qpos
                p = jnp.concatenate([jnp.where(vis, p[:, j * 128:(j + 1) * 128], 0.0) for j in range(8)], 1)
            dp = lax.dot_general(v, dy, NT, preferred_element_type=F32)
            ds = (p * (dp - delta_r)).astype(BF)
            dv_s[pl.ds(at, kb)] += jnp.dot(p.astype(BF), dy, preferred_element_type=F32)
            dk_s[pl.ds(at, kb)] += jnp.dot(ds, q, preferred_element_type=F32)
            return dq + lax.dot_general(ds, k, TN, preferred_element_type=F32)

        nb = (t * 128) // kb
        dq = jnp.zeros((rows, 128), F32)
        dq = lax.fori_loop(0, nb, lambda b, cr: bwd(b, cr, False), dq)
        dq = bwd(nb, dq, True)
        dq_ref[...] = spread_heads(dq * scale).astype(dq_ref.dtype)

    span(0, q_own, dy_own, x_own, y_own, dq_own)
    span(1, q_got, dy_got, x_got, y_got, dq_got)
    for t in range(spans):
        at = pl.ds(pl.multiple_of(inv_ref[t] * 128, 128), 128)
        terms_ref[at, 0:128] = (dk_s[t * 128:(t + 1) * 128] * scale).astype(BF)
        terms_ref[at, 128:256] = dv_s[t * 128:(t + 1) * 128].astype(BF)


def attention(q, dy, x, kv, tq, inv, kf=1024, kb=512):
    spans = kv.shape[0]
    count = kv.shape[2] // 256
    own = pl.BlockSpec((128, 1024), lambda h, tq, inv: (0, tq[2] * count + h))
    got = pl.BlockSpec((128, 1024), lambda h, tq, inv: (0, h))
    flops = 2 * 7 * 2 * count * 1024 * spans * 128 * 128
    rows = jax.ShapeDtypeStruct((128, count * 1024), BF)
    return pl.pallas_call(
        functools.partial(attention_kernel, kf, kb),
        grid_spec=pltpu.PrefetchScalarGridSpec(
            num_scalar_prefetch=2,
            grid=(count,),
            in_specs=[own, got] * 3 + [pl.BlockSpec(memory_space=pl.ANY)],
            out_specs=[got] * 4 + [pl.BlockSpec((spans * 128, 256), lambda h, tq, inv: (0, h))],
            scratch_shapes=[pltpu.VMEM((spans * 128, count * 256), BF), pltpu.VMEM((spans * 128, 128), F32),
                            pltpu.VMEM((spans * 128, 128), F32), pltpu.SemaphoreType.DMA((spans,))],
        ),
        out_shape=[rows] * 4 + [jax.ShapeDtypeStruct((spans * 128, count * 256), BF)],
        compiler_params=pltpu.CompilerParams(vmem_limit_bytes=50 << 20),
        cost_estimate=pl.CostEstimate(flops=flops, bytes_accessed=16 << 20, transcendentals=0),
        name="attention",
    )(tq, inv, *q, *dy, *x, kv)


MESH_ID = pl.DeviceIdType.MESH
EPS = 1e-05
DOWN, UP = 0, 1
OWN, PAIR = 0, 1
UNITS = [(UP, OWN), (UP, PAIR), (DOWN, OWN), (DOWN, PAIR)]


class Place:
    def __init__(self):
        self.me = lax.axis_index("ctx")
        self.core = self.me % 2
        self.chip = self.me // 2
        beside = self.chip % 2
        self.partner = self.me + 1 - 2 * self.core
        self.across = self.me + 2 - 4 * beside
        self.above = (self.me + 4) % 16
        self.below = (self.me + 12) % 16
        self.chip_x = self.chip + 1 - 2 * beside

    def greet_all(self, barrier):
        for step in range(1, 16):
            pl.semaphore_signal(barrier, inc=1, device_id={"ctx": (self.me + step) % 16}, device_id_type=MESH_ID)
        mirrored = 7 - lax.axis_index("section")
        pl.semaphore_signal(barrier, inc=1, device_id={"section": mirrored}, device_id_type=MESH_ID)
        pl.semaphore_wait(barrier, 16)

    def greet(self, barrier):
        for dev in (self.partner, self.across, self.above, self.below):
            pl.semaphore_signal(barrier, inc=1, device_id={"ctx": dev}, device_id_type=MESH_ID)
        pl.semaphore_wait(barrier, 4)

    def span(self, chip, kind):
        return 2 * chip + (self.core if kind == OWN else 1 - self.core)

    def up(self, chip, by):
        return (chip + 2 * by) % 8


class Wires:
    def __init__(self, send_sem, recv_sem):
        self.send_sem, self.recv_sem, self.started = send_sem, recv_sem, []

    def copy(self, index, src, dst, dev):
        return pltpu.make_async_remote_copy(
            src_ref=src, dst_ref=dst, send_sem=self.send_sem.at[index], recv_sem=self.recv_sem.at[index],
            device_id={"ctx": dev}, device_id_type=MESH_ID)

    def send(self, index, src, dst, dev):
        copy = self.copy(index, src, dst, dev)
        copy.start()
        self.started.append(copy)

    def far_send(self, index, src, dst, section):
        copy = pltpu.make_async_remote_copy(
            src_ref=src, dst_ref=dst, send_sem=self.send_sem.at[index], recv_sem=self.recv_sem.at[index],
            device_id={"section": section}, device_id_type=MESH_ID)
        copy.start()
        self.started.append(copy)
        return copy

    def arrive(self, index, ref, dev):
        self.copy(index, ref, ref, dev).wait_recv()

    def finish(self):
        for copy in self.started:
            copy.wait_send()


X, ZM, ZP, XZM, XZP, AN, XA = range(7)


def gather_first(place, wires, base, unit, src, slot):
    kind = unit[1]
    at = base + 7 * UNITS.index(unit)
    here = slot(unit, place.chip)
    wires.send(at + X, src, here, place.across)
    wires.send(at + ZM, src, here, place.above)
    wires.send(at + ZP, src, here, place.below)


def gather_second(place, wires, base, unit, slot, landed):
    at = base + 7 * UNITS.index(unit)
    lo, hi = slot(unit, place.up(place.chip, 3)), slot(unit, place.up(place.chip, 1))
    wires.arrive(at + ZM, lo, place.below)
    if unit[1] == OWN:
        wires.send(at + AN, lo, lo, place.above)
    wires.arrive(at + ZP, hi, place.above)
    if unit[1] == PAIR:
        wires.send(at + AN, hi, hi, place.below)
    landed(unit, place.up(place.chip, 3))
    landed(unit, place.up(place.chip, 1))


def gather_third(place, wires, base, unit, slot, landed):
    at = base + 7 * UNITS.index(unit)
    far = slot(unit, place.up(place.chip, 2))
    wires.arrive(at + AN, far, place.below if unit[1] == OWN else place.above)
    wires.send(at + XA, far, far, place.across)
    cx = slot(unit, place.chip_x)
    wires.arrive(at + X, cx, place.across)
    wires.send(at + XZM, cx, cx, place.above)
    wires.send(at + XZP, cx, cx, place.below)
    landed(unit, place.up(place.chip, 2))
    landed(unit, place.chip_x)


def gather_last(place, wires, base, unit, slot, landed):
    at = base + 7 * UNITS.index(unit)
    for kind, by, dev in ((XZM, 3, place.below), (XZP, 1, place.above), (XA, 2, place.across)):
        chip = place.up(place.chip_x, by)
        wires.arrive(at + kind, slot(unit, chip), dev)
        landed(unit, chip)


def nothing(unit, chip):
    pass


def spread_kernel(act_d, act_u, cot_d, cot_u, x_d, x_u, kv_d, kv_u,
                  q_d, q_u, dy_d, dy_u, xh_d, xh_u, all_d, all_u, send_sem, recv_sem, local_sem):
    place = Place()
    wires = Wires(send_sem, recv_sem)
    place.greet(pltpu.get_barrier_semaphore())
    all_kv, kv = (all_d, all_u), (kv_d, kv_u)
    mine = pl.ds(pl.multiple_of(place.core * 512, 512), 512)
    other = lambda width: pl.ds(pl.multiple_of((1 - place.core) * width, width), width)
    slot = lambda unit, chip: all_kv[unit[0]].at[place.span(chip, unit[1])]
    local = []
    for layer in (UP, DOWN):
        wires.send(28 + layer, kv[layer].at[:, other(512)], all_kv[layer].at[place.me], place.partner)
    for layer in (UP, DOWN):
        gather_first(place, wires, 0, (layer, OWN), kv[layer].at[:, mine], slot)
        copy = pltpu.make_async_copy(kv[layer].at[:, mine], all_kv[layer].at[place.me], local_sem.at[layer])
        copy.start()
        local.append(copy)
    for layer in (UP, DOWN):
        wires.arrive(28 + layer, all_kv[layer].at[place.partner], place.partner)
        gather_first(place, wires, 0, (layer, PAIR), slot((layer, PAIR), place.chip), slot)
    halves = ((act_u, q_u), (cot_u, dy_u), (x_u, xh_u), (act_d, q_d), (cot_d, dy_d), (x_d, xh_d))
    for n, (src, dst) in enumerate(halves):
        wires.send(30 + n, src.at[:, other(2048)], dst, place.partner)
    for unit in UNITS:
        gather_second(place, wires, 0, unit, slot, nothing)
    for unit in UNITS:
        gather_third(place, wires, 0, unit, slot, nothing)
    for unit in UNITS:
        gather_last(place, wires, 0, unit, slot, nothing)
    for n, (src, dst) in enumerate(halves):
        wires.arrive(30 + n, dst, place.partner)
    for copy in local:
        copy.wait()
    wires.finish()


def spread(*operands):
    half = jax.ShapeDtypeStruct((128, 2048), BF)
    hbm = pl.BlockSpec(memory_space=pl.ANY)
    return pl.pallas_call(
        spread_kernel,
        in_specs=[hbm] * 6 + [pl.BlockSpec(memory_space=pltpu.VMEM)] * 2,
        out_specs=[hbm] * 8,
        out_shape=[half] * 6 + [jax.ShapeDtypeStruct((16, 128, 512), BF)] * 2,
        scratch_shapes=[pltpu.SemaphoreType.DMA((36,)), pltpu.SemaphoreType.DMA((36,)), pltpu.SemaphoreType.DMA((2,))],
        compiler_params=pltpu.CompilerParams(collective_id=1, has_side_effects=True),
        name="spread",
    )(*operands)


R0, RA, RB, R1, RU, RD, RX = range(7)


HANDED, DQ, GAINS, FAR = 56, 88, 90, 120


def finish_kernel(terms_d, terms_u, dqo_d, dqo_u, dqg_d, dqg_u, x_d, x_u, cot_d, cot_u, act_hbm, weights, gains,
                  grad_d, grad_u, kv_grad, gain_grad,
                  slots, stage, total, all_kv, dquery, weight, dact, gparts, ggot, gsum, acc, wsend, wgot, ggot_far,
                  kept, x_s, cot_s, features, grad_s, send_sem, recv_sem, local_sem):
    place = Place()
    wires = Wires(send_sem, recv_sem)
    mirrored = 7 - lax.axis_index("section")
    terms = (terms_d, terms_u)
    chip, chip_x = place.chip, place.chip_x
    local = []

    def keep(src, dst):
        copy = pltpu.make_async_copy(src, dst, local_sem.at[len(local)])
        copy.start()
        local.append(copy)
        return copy

    loads = {}
    for layer, source in ((UP, terms_u), (DOWN, terms_d)):
        loads["terms", layer] = keep(source, kept.at[layer])
    place.greet_all(pltpu.get_barrier_semaphore())

    def rows(unit, at):
        return pl.ds(pl.multiple_of(place.span(at, unit[1]) * 128, 128), 128)

    def sent(unit, at):
        return terms[unit[0]].at[rows(unit, at)]

    def term(unit, at):
        return kept.at[unit[0], rows(unit, at)]

    def plus(*refs):
        value = refs[0][...].astype(F32)
        for ref in refs[1:]:
            value = value + ref[...].astype(F32)
        return value.astype(BF)

    def reduce_first(layer):
        for n, unit in enumerate(UNITS):
            if unit[0] == layer:
                at = 7 * n
                wires.send(at + R0, sent(unit, place.up(chip_x, 2)), slots.at[at + R0], place.across)
                wires.send(at + RA, sent(unit, place.up(chip_x, 1)), slots.at[at + RA], place.above)
                wires.send(at + RB, sent(unit, place.up(chip_x, 3)), slots.at[at + RB], place.below)

    def reduce_second(layer):
        for n, unit in enumerate(UNITS):
            if unit[0] == layer:
                at = 7 * n
                wires.arrive(at + R0, slots.at[at + R0], place.across)
                stage[3 * n] = plus(slots.at[at + R0], term(unit, place.up(chip, 2)))
                wires.send(at + R1, stage.at[3 * n], slots.at[at + R1], place.below if unit[1] == OWN else place.above)

    def reduce_direct(layer):
        for n, unit in enumerate(UNITS):
            if unit[0] == layer:
                at = 7 * n
                if unit[1] == OWN:
                    wires.send(at + RD, sent(unit, place.up(chip, 1)), slots.at[at + RD], place.above)
                else:
                    wires.send(at + RU, sent(unit, place.up(chip, 3)), slots.at[at + RU], place.below)

    def reduce_third(layer):
        for n, unit in enumerate(UNITS):
            if unit[0] == layer:
                at = 7 * n
                wires.arrive(at + RA, slots.at[at + RA], place.below)
                wires.arrive(at + RB, slots.at[at + RB], place.above)
                stage[3 * n + 1] = plus(slots.at[at + RA], slots.at[at + RB], term(unit, chip_x))
                wires.send(at + RX, stage.at[3 * n + 1], slots.at[at + RX], place.across)
        for n, unit in enumerate(UNITS):
            if unit[0] == layer:
                at = 7 * n
                if unit[1] == OWN:
                    wires.arrive(at + R1, slots.at[at + R1], place.above)
                    stage[3 * n + 2] = plus(slots.at[at + R1], term(unit, place.up(chip, 3)))
                    wires.send(at + RU, stage.at[3 * n + 2], slots.at[at + RU], place.below)
                else:
                    wires.arrive(at + R1, slots.at[at + R1], place.below)
                    stage[3 * n + 2] = plus(slots.at[at + R1], term(unit, place.up(chip, 1)))
                    wires.send(at + RD, stage.at[3 * n + 2], slots.at[at + RD], place.above)

    def load_rest(layer, own_part, other_part, x_ref, cot_ref):
        wires.send(DQ + layer, other_part, dquery.at[layer, place.core], place.partner)
        loads["rest", layer] = [
            keep(own_part, dquery.at[layer, place.core]), keep(x_ref, x_s.at[layer]), keep(cot_ref, cot_s.at[layer]),
            keep(weights.at[1 if layer == UP else 0, 0], weight.at[layer])]

    slot = lambda unit, at: all_kv.at[unit[0], place.core, place.span(at, unit[1])]
    order = []

    def landed(unit, at):
        ref = slot(unit, at)
        wires.send(HANDED + len(order), ref, ref, place.partner)
        order.append((unit, at))

    def reduce_last(layer):
        for n, unit in enumerate(UNITS):
            if unit[0] == layer:
                at = 7 * n
                wires.arrive(at + RX, slots.at[at + RX], place.across)
                wires.arrive(at + RU, slots.at[at + RU], place.above)
                wires.arrive(at + RD, slots.at[at + RD], place.below)
                total[n] = plus(slots.at[at + RX], slots.at[at + RU], slots.at[at + RD], term(unit, chip))
                gather_first(place, wires, 28, unit, total.at[n], slot)
                all_kv[layer, place.core, place.span(chip, unit[1])] = total[n]
                wires.send(HANDED + len(order), total.at[n], slot(unit, chip), place.partner)
                order.append((unit, chip))

    waited = set()

    def handed(chosen):
        for n, (unit, at) in enumerate(order):
            if chosen(unit, at) and n not in waited:
                waited.add(n)
                ref = all_kv.at[unit[0], 1 - place.core, place.span(at, 1 - unit[1])]
                wires.arrive(HANDED + n, ref, place.partner)

    def complete(layer, grad_ref):
        handed(lambda unit, at: unit[0] == layer and at is chip)
        for copy in loads["rest", layer]:
            copy.wait()
        wires.arrive(DQ + layer, dquery.at[layer, 1 - place.core], place.partner)
        halves = [all_kv[layer, half, place.me] for half in range(2)]
        dkv = jnp.concatenate([halves[h // 2][:, (h % 2) * 256 + kind * 128:(h % 2) * 256 + kind * 128 + 128]
                               for kind in range(2) for h in range(4)], 1)
        total_sq = jnp.zeros((128, 1), F32)
        for tile in range(8):
            part = x_s[layer, :, tile * 512:(tile + 1) * 512].astype(F32)
            total_sq = total_sq + jnp.sum(part * part, 1, keepdims=True)
        recip = lax.rsqrt(total_sq / 4096 + EPS)

        def first(tile, dots):
            cols = pl.ds(pl.multiple_of(tile * 512, 512), 512)
            normed = x_s[layer, :, cols].astype(F32) * recip
            within = pl.ds(pl.multiple_of(tile % 4 * 512, 512), 512)
            value = dquery[layer, tile // 4, :, within].astype(F32) + lax.dot_general(
                dkv, weight[layer, cols, :], NT, preferred_element_type=F32)
            dact[:, cols] = value
            product = value * normed
            column = jnp.sum(product, 0, keepdims=True)
            for half in range(2):
                gparts[layer, 2 * tile + half] = jnp.broadcast_to(column[:, half * 256:(half + 1) * 256], (8, 256))
            return dots + jnp.sum(product * gains[layer:layer + 1, cols], 1, keepdims=True)

        dots = lax.fori_loop(0, 8, first, jnp.zeros((128, 1), F32))
        for step in range(1, 16):
            to = (place.me + step) % 16
            wires.send(GAINS + 15 * layer + step - 1, gparts.at[layer, to], ggot.at[layer, step], to)
        mean = dots / 4096

        def second(tile, _):
            cols = pl.ds(pl.multiple_of(tile * 512, 512), 512)
            normed = x_s[layer, :, cols].astype(F32) * recip
            dnormed = dact[:, cols] * gains[layer:layer + 1, cols]
            grad_s[layer, :, cols] = (cot_s[layer, :, cols].astype(F32) + recip * (dnormed - normed * mean)).astype(BF)
            return 0

        lax.fori_loop(0, 8, second, 0)
        loads["grad", layer] = keep(grad_s.at[layer], grad_ref)

    def gain_total(layer):
        value = gparts[layer, place.me]
        for step in range(1, 16):
            wires.arrive(GAINS + 15 * layer + step - 1, ggot.at[layer, step], (place.me + step) % 16)
            value = value + ggot[layer, step]
        return value

    def weight_grad(layer):
        acc[...] = jnp.zeros_like(acc)

        def step(n, _):
            two = pl.ds(2 * n, 2)
            act = features[two, layer].reshape(256, 256)
            for half in range(2):
                dkv = all_kv[layer, half, two].reshape(256, 512)
                acc[:, half * 512:(half + 1) * 512] += lax.dot_general(act, dkv, TN, preferred_element_type=F32)
            return 0

        lax.fori_loop(0, 8, step, 0)

    def stage_of(step, layer):
        for unit in UNITS:
            if unit[0] == layer:
                step(place, wires, 28, unit, slot, landed)

    reduce_first(UP)
    for layer in (UP, DOWN):
        loads["terms", layer].wait()
    reduce_second(UP)
    reduce_first(DOWN)
    load_rest(UP, dqo_u, dqg_u, x_u, cot_u)
    reduce_third(UP)
    reduce_direct(UP)
    reduce_second(DOWN)
    load_rest(DOWN, dqo_d, dqg_d, x_d, cot_d)
    loads["act"] = keep(act_hbm, features)
    reduce_last(UP)
    reduce_third(DOWN)
    reduce_direct(DOWN)
    stage_of(gather_second, UP)
    reduce_last(DOWN)
    stage_of(gather_third, UP)
    stage_of(gather_second, DOWN)
    complete(UP, grad_u)
    stage_of(gather_third, DOWN)
    stage_of(gather_last, UP)
    handed(lambda unit, at: unit[0] == UP)
    loads["act"].wait()
    weight_grad(UP)
    wsend[...] = acc[...].astype(BF)
    far_w = wires.far_send(FAR, wsend, wgot, mirrored)
    complete(DOWN, grad_d)
    gsum[...] = gain_total(UP)
    far_g = wires.far_send(FAR + 1, gsum, ggot_far, mirrored)
    stage_of(gather_last, DOWN)
    handed(lambda unit, at: True)
    weight_grad(DOWN)
    mine = gain_total(DOWN)
    far_g.wait_recv()
    gain_grad[...] = mine + ggot_far[...]
    far_w.wait_recv()
    for h in range(4):
        for kind in range(2):
            came = slice(h * 256 + kind * 128, h * 256 + kind * 128 + 128)
            goes = slice(kind * 512 + h * 128, kind * 512 + h * 128 + 128)
            kv_grad[:, goes] = acc[:, came] + wgot[:, came].astype(F32)
    for layer in (UP, DOWN):
        loads["grad", layer].wait()
    wires.finish()


def finish(*operands):
    hbm = pl.BlockSpec(memory_space=pl.ANY)
    vmem = pl.BlockSpec(memory_space=pltpu.VMEM)
    row = jax.ShapeDtypeStruct((128, 4096), BF)
    unit = lambda count: pltpu.VMEM((count, 128, 512), BF)
    return pl.pallas_call(
        finish_kernel,
        in_specs=[hbm] * 12 + [vmem],
        out_specs=[hbm] * 2 + [vmem] * 2,
        out_shape=[row, row, jax.ShapeDtypeStruct((256, 1024), F32), jax.ShapeDtypeStruct((8, 256), F32)],
        scratch_shapes=[unit(28), unit(12), unit(4), pltpu.VMEM((2, 2, 16, 128, 512), BF), pltpu.VMEM((2, 2, 128, 2048), BF),
                        pltpu.VMEM((2, 4096, 1024), BF), pltpu.VMEM((128, 4096), F32), pltpu.VMEM((2, 16, 8, 256), F32),
                        pltpu.VMEM((2, 16, 8, 256), F32), pltpu.VMEM((8, 256), F32), pltpu.VMEM((256, 1024), F32),
                        pltpu.VMEM((256, 1024), BF), pltpu.VMEM((256, 1024), BF), pltpu.VMEM((8, 256), F32),
                        pltpu.VMEM((2, 2048, 512), BF), pltpu.VMEM((2, 128, 4096), BF), pltpu.VMEM((2, 128, 4096), BF),
                        pltpu.VMEM((16, 2, 128, 256), BF), pltpu.VMEM((2, 128, 4096), BF),
                        pltpu.SemaphoreType.DMA((122,)), pltpu.SemaphoreType.DMA((122,)), pltpu.SemaphoreType.DMA((13,))],
        compiler_params=pltpu.CompilerParams(collective_id=2, has_side_effects=True, vmem_limit_bytes=60 << 20),
        name="finish",
    )(*operands)


def by_head(kv):
    return kv.reshape(-1, 2, 4, 128).transpose(0, 2, 1, 3).reshape(-1, 1024)


def prepare(x, gain, weight):
    xf = x.astype(F32)
    recip = lax.rsqrt(jnp.mean(xf * xf, -1, keepdims=True) + EPS)
    normed = xf * recip
    act = (normed * gain[None, :]).astype(BF)
    kv = jnp.dot(act, weight, preferred_element_type=F32).astype(BF)
    return act, by_head(kv)


def halves_joined(core, mine, other):
    both = jnp.concatenate([other, other], 1)
    return lax.dynamic_update_slice(both, mine, (0, core * mine.shape[1]))


def relayed(own, got, by):
    sections, spans = lax.axis_size("section"), lax.axis_size("ctx")
    to = lambda flip: [(s * spans + i, (s + by) % sections * spans + (i ^ flip)) for s in range(sections) for i in range(spans)]
    mine = lax.ppermute(own, ("section", "ctx"), to(0))
    other = lax.ppermute(got, ("section", "ctx"), to(1))
    return mine, other


def per_device(down_in, up_in, down_cot, up_cot, kv_weight, norm_gain, span_ids):
    own = lax.axis_index("ctx")
    core = own % 2
    x_d, x_u, cot_d, cot_u = down_in[0], up_in[0], down_cot[0], up_cot[0]
    gain_d, gain_u = norm_gain[0, 0], norm_gain[1, 0]
    weight_d, weight_u = kv_weight[0, 0], kv_weight[1, 0]
    scalars = jnp.stack([span_ids[own], span_ids[own + 1 - 2 * core], core]).astype(jnp.int32)
    order = jnp.arange(16, dtype=jnp.int32)
    inverse = jnp.sum(jnp.where(span_ids[:, None] == order[None, :], order[:, None], 0), 0).astype(jnp.int32)
    act_u, kv_u = prepare(x_u, gain_u, weight_u)
    act_d, kv_d = prepare(x_d, gain_d, weight_d)
    q_d, q_u, dy_d, dy_u, xh_d, xh_u, all_d, all_u = spread(act_d, act_u, cot_d, cot_u, x_d, x_u, kv_d, kv_u)
    after_d, after_u, _ = lax.optimization_barrier((act_d, act_u, q_d))
    features = jnp.stack([after_d, after_u]).reshape(2, 128, 16, 256).transpose(2, 0, 1, 3)
    features = lax.all_to_all(features, "ctx", 0, 0, tiled=False)
    yo_u, yg_u, dqo_u, dqg_u, terms_u = attention((act_u, q_u), (cot_u, dy_u), (x_u, xh_u), all_u, scalars, inverse)
    up_halves = relayed(yo_u, yg_u, -1)
    yo_d, yg_d, dqo_d, dqg_d, terms_d = attention((act_d, q_d), (cot_d, dy_d), (x_d, xh_d), all_d, scalars, inverse)
    down_halves = relayed(yo_d, yg_d, 1)
    grad_d, grad_u, kv_grad, gain_grad = finish(
        terms_d, terms_u, dqo_d, dqo_u, dqg_d, dqg_u, x_d, x_u, cot_d, cot_u, features, kv_weight, norm_gain[:, 0])
    down_halves, up_halves, gain_grad = lax.optimization_barrier((down_halves, up_halves, gain_grad))
    down_out, up_out = halves_joined(core, *down_halves), halves_joined(core, *up_halves)
    return (down_out[None], up_out[None], grad_d[None], grad_u[None], kv_grad[None], gain_grad[:1])


def solution(mesh):
    row = P("section", "ctx", None)
    in_specs = (row, row, row, row, P(None, "section", None, None), P(None, "section", None), P())
    out_specs = (row, row, row, row, row, P("section", "ctx"))
    return jax.shard_map(per_device, mesh=mesh, in_specs=in_specs, out_specs=out_specs, check_vma=False)
```

```python
import functools

import jax
import jax.numpy as jnp
from jax import lax
from jax.experimental import pallas as pl
from jax.experimental.pallas import tpu as pltpu
from jax.sharding import PartitionSpec as P

LOG2E = 1.4426950408889634
NT = (((1,), (1,)), ((), ()))
TN = (((0,), (0,)), ((), ()))
F32 = jnp.float32
BF = jnp.bfloat16


def stack_heads(block):
    return jnp.concatenate([block[:, j * 128:(j + 1) * 128] for j in range(8)], 0)


def spread_heads(rows):
    return jnp.concatenate([rows[j * 128:(j + 1) * 128] for j in range(8)], 1)


def attention_kernel(block, small, tq_ref, inv_ref, q_own, q_got, dy_own, dy_got, x_own, x_got, kv_hbm,
                     y_own, y_got, dq_own, dq_got, terms_ref, kv_s, dk_s, dv_s, e_s, top_s, sems):
    head = pl.program_id(0)
    spans = kv_hbm.shape[0]
    heads = kv_hbm.shape[2] // 256
    scale = 128 ** -0.5
    c = scale * LOG2E

    def load(h, t):
        return pltpu.make_async_copy(kv_hbm.at[inv_ref[t], :, pl.ds(h * 256, 256)],
                                     kv_s.at[h, pl.ds(t * 128, 128)], sems.at[h, t])

    @pl.when(head == 0)
    def _():
        for h in range(heads):
            for t in range(spans):
                load(h, t).start()

    for h in range(heads):
        @pl.when(head == h)
        def _():
            for t in range(spans):
                load(h, t).wait()

    dk_s[...] = jnp.zeros_like(dk_s)
    dv_s[...] = jnp.zeros_like(dv_s)

    def span(qi, q_ref, dy_ref, x_ref, y_ref, dq_ref):
        t = tq_ref[qi]
        q = stack_heads(q_ref[...])
        dy = stack_heads(dy_ref[...])
        rows = q.shape[0]
        blocks = (t * 128) // block
        short = t * 128 + 128 - blocks * block <= small

        def forward(b, size, masked, carry):
            m, l, acc = carry
            at = pl.multiple_of(b * block, block)
            k = kv_s[head, pl.ds(at, size), 0:128]
            v = kv_s[head, pl.ds(at, size), 128:256]
            s = lax.dot_general(k, q, NT, preferred_element_type=F32)
            if masked:
                kpos = at + lax.broadcasted_iota(jnp.int32, (size, 128), 0)
                qpos = t * 128 + lax.broadcasted_iota(jnp.int32, (size, 128), 1)
                visible = kpos <= qpos
                s = jnp.concatenate([jnp.where(visible, s[:, j * 128:(j + 1) * 128], -1e30) for j in range(8)], 1)
            m_new = jnp.maximum(m, jnp.max(s, 0, keepdims=True))
            e = jnp.exp2((s - m_new) * c)
            fade = jnp.exp2((m - m_new) * c)
            rounded = e.astype(BF)
            e_s[pl.ds(at, size), :] = rounded
            top_s[b] = jnp.broadcast_to(m_new, (8, rows))
            l = l * fade + jnp.sum(e, 0, keepdims=True)
            acc = acc * fade + lax.dot_general(v, rounded, TN, preferred_element_type=F32)
            return m_new, l, acc

        def over_blocks(step, carry):
            carry = lax.fori_loop(0, blocks, lambda b, cr: step(b, block, False, cr), carry)
            return lax.cond(short, lambda cr: step(blocks, small, True, cr), lambda cr: step(blocks, block, True, cr), carry)

        start = (jnp.full((1, rows), -1e30, F32), jnp.zeros((1, rows), F32), jnp.zeros((128, rows), F32))
        m, l, acc = over_blocks(forward, start)
        mixed = acc / l
        delta = jnp.sum(jnp.transpose(dy.astype(F32)) * mixed, 0, keepdims=True)
        y_ref[...] = (x_ref[...].astype(F32) + spread_heads(jnp.transpose(mixed))).astype(y_ref.dtype)

        def backward(b, size, masked, dq):
            at = pl.multiple_of(b * block, block)
            k = kv_s[head, pl.ds(at, size), 0:128]
            v = kv_s[head, pl.ds(at, size), 128:256]
            p = e_s[pl.ds(at, size), :].astype(F32) * (jnp.exp2((top_s[b, 0:1] - m) * c) / l)
            dp = lax.dot_general(v, dy, NT, preferred_element_type=F32)
            ds = (p * (dp - delta)).astype(BF)
            dv_s[pl.ds(at, size)] += jnp.dot(p.astype(BF), dy, preferred_element_type=F32)
            dk_s[pl.ds(at, size)] += jnp.dot(ds, q, preferred_element_type=F32)
            return dq + lax.dot_general(k, ds, TN, preferred_element_type=F32)

        dq = over_blocks(backward, jnp.zeros((128, rows), F32))
        dq_ref[...] = spread_heads(jnp.transpose(dq * scale)).astype(dq_ref.dtype)

    span(0, q_own, dy_own, x_own, y_own, dq_own)
    span(1, q_got, dy_got, x_got, y_got, dq_got)
    for t in range(spans):
        at = pl.ds(pl.multiple_of(inv_ref[t] * 128, 128), 128)
        terms_ref[at, 0:128] = (dk_s[t * 128:(t + 1) * 128] * scale).astype(BF)
        terms_ref[at, 128:256] = dv_s[t * 128:(t + 1) * 128].astype(BF)


def attention(q, dy, x, kv, tq, inv, block=1024, small=512):
    spans = kv.shape[0]
    count = kv.shape[2] // 256
    own = pl.BlockSpec((128, 1024), lambda h, tq, inv: (0, tq[2] * count + h))
    got = pl.BlockSpec((128, 1024), lambda h, tq, inv: (0, h))
    flops = 2 * 7 * 2 * count * 1024 * spans * 128 * 128
    rows = jax.ShapeDtypeStruct((128, count * 1024), BF)
    return pl.pallas_call(
        functools.partial(attention_kernel, block, small),
        grid_spec=pltpu.PrefetchScalarGridSpec(
            num_scalar_prefetch=2,
            grid=(count,),
            in_specs=[own, got] * 3 + [pl.BlockSpec(memory_space=pl.ANY)],
            out_specs=[got] * 4 + [pl.BlockSpec((spans * 128, 256), lambda h, tq, inv: (0, h))],
            scratch_shapes=[pltpu.VMEM((count, spans * 128, 256), BF), pltpu.VMEM((spans * 128, 128), F32),
                            pltpu.VMEM((spans * 128, 128), F32), pltpu.VMEM((spans * 128, 1024), BF),
                            pltpu.VMEM((spans * 128 // block, 8, 1024), F32), pltpu.SemaphoreType.DMA((count, spans))],
        ),
        out_shape=[rows] * 4 + [jax.ShapeDtypeStruct((spans * 128, count * 256), BF)],
        compiler_params=pltpu.CompilerParams(vmem_limit_bytes=50 << 20),
        cost_estimate=pl.CostEstimate(flops=flops, bytes_accessed=16 << 20, transcendentals=0),
        name="attention",
    )(tq, inv, *q, *dy, *x, kv)


MESH_ID = pl.DeviceIdType.MESH
EPS = 1e-05
DOWN, UP = 0, 1
OWN, PAIR = 0, 1
UNITS = [(UP, OWN), (UP, PAIR), (DOWN, OWN), (DOWN, PAIR)]


class Place:
    def __init__(self):
        self.me = lax.axis_index("ctx")
        self.core = self.me % 2
        self.chip = self.me // 2
        beside = self.chip % 2
        self.partner = self.me + 1 - 2 * self.core
        self.across = self.me + 2 - 4 * beside
        self.above = (self.me + 4) % 16
        self.below = (self.me + 12) % 16
        self.chip_x = self.chip + 1 - 2 * beside

    def greet_all(self, barrier):
        for step in range(1, 16):
            pl.semaphore_signal(barrier, inc=1, device_id={"ctx": (self.me + step) % 16}, device_id_type=MESH_ID)
        mirrored = 7 - lax.axis_index("section")
        pl.semaphore_signal(barrier, inc=1, device_id={"section": mirrored}, device_id_type=MESH_ID)
        pl.semaphore_wait(barrier, 16)

    def greet(self, barrier):
        for dev in (self.partner, self.across, self.above, self.below):
            pl.semaphore_signal(barrier, inc=1, device_id={"ctx": dev}, device_id_type=MESH_ID)
        pl.semaphore_wait(barrier, 4)

    def span(self, chip, kind):
        return 2 * chip + (self.core if kind == OWN else 1 - self.core)

    def up(self, chip, by):
        return (chip + 2 * by) % 8


class Wires:
    def __init__(self, send_sem, recv_sem):
        self.send_sem, self.recv_sem, self.started = send_sem, recv_sem, []

    def copy(self, index, src, dst, dev):
        return pltpu.make_async_remote_copy(
            src_ref=src, dst_ref=dst, send_sem=self.send_sem.at[index], recv_sem=self.recv_sem.at[index],
            device_id={"ctx": dev}, device_id_type=MESH_ID)

    def send(self, index, src, dst, dev):
        copy = self.copy(index, src, dst, dev)
        copy.start()
        self.started.append(copy)

    def far_send(self, index, src, dst, section):
        copy = pltpu.make_async_remote_copy(
            src_ref=src, dst_ref=dst, send_sem=self.send_sem.at[index], recv_sem=self.recv_sem.at[index],
            device_id={"section": section}, device_id_type=MESH_ID)
        copy.start()
        self.started.append(copy)
        return copy

    def arrive(self, index, ref, dev):
        self.copy(index, ref, ref, dev).wait_recv()

    def finish(self):
        for copy in self.started:
            copy.wait_send()


X, ZM, ZP, XZM, XZP, AN, XA = range(7)


def gather_first(place, wires, base, unit, src, slot):
    kind = unit[1]
    at = base + 7 * UNITS.index(unit)
    here = slot(unit, place.chip)
    wires.send(at + X, src, here, place.across)
    wires.send(at + ZM, src, here, place.above)
    wires.send(at + ZP, src, here, place.below)


def gather_second(place, wires, base, unit, slot, landed):
    at = base + 7 * UNITS.index(unit)
    lo, hi = slot(unit, place.up(place.chip, 3)), slot(unit, place.up(place.chip, 1))
    wires.arrive(at + ZM, lo, place.below)
    if unit[1] == OWN:
        wires.send(at + AN, lo, lo, place.above)
    wires.arrive(at + ZP, hi, place.above)
    if unit[1] == PAIR:
        wires.send(at + AN, hi, hi, place.below)
    landed(unit, place.up(place.chip, 3))
    landed(unit, place.up(place.chip, 1))


def gather_third(place, wires, base, unit, slot, landed):
    at = base + 7 * UNITS.index(unit)
    far = slot(unit, place.up(place.chip, 2))
    wires.arrive(at + AN, far, place.below if unit[1] == OWN else place.above)
    wires.send(at + XA, far, far, place.across)
    cx = slot(unit, place.chip_x)
    wires.arrive(at + X, cx, place.across)
    wires.send(at + XZM, cx, cx, place.above)
    wires.send(at + XZP, cx, cx, place.below)
    landed(unit, place.up(place.chip, 2))
    landed(unit, place.chip_x)


def gather_last(place, wires, base, unit, slot, landed):
    at = base + 7 * UNITS.index(unit)
    for kind, by, dev in ((XZM, 3, place.below), (XZP, 1, place.above), (XA, 2, place.across)):
        chip = place.up(place.chip_x, by)
        wires.arrive(at + kind, slot(unit, chip), dev)
        landed(unit, chip)


def nothing(unit, chip):
    pass


def spread_kernel(act_d, act_u, cot_d, cot_u, x_d, x_u, kv_d, kv_u,
                  q_d, q_u, dy_d, dy_u, xh_d, xh_u, all_d, all_u, send_sem, recv_sem, local_sem):
    place = Place()
    wires = Wires(send_sem, recv_sem)
    place.greet(pltpu.get_barrier_semaphore())
    all_kv, kv = (all_d, all_u), (kv_d, kv_u)
    mine = pl.ds(pl.multiple_of(place.core * 512, 512), 512)
    other = lambda width: pl.ds(pl.multiple_of((1 - place.core) * width, width), width)
    slot = lambda unit, chip: all_kv[unit[0]].at[place.span(chip, unit[1])]
    local = []
    for layer in (UP, DOWN):
        wires.send(28 + layer, kv[layer].at[:, other(512)], all_kv[layer].at[place.me], place.partner)
    for layer in (UP, DOWN):
        gather_first(place, wires, 0, (layer, OWN), kv[layer].at[:, mine], slot)
        copy = pltpu.make_async_copy(kv[layer].at[:, mine], all_kv[layer].at[place.me], local_sem.at[layer])
        copy.start()
        local.append(copy)
    for layer in (UP, DOWN):
        wires.arrive(28 + layer, all_kv[layer].at[place.partner], place.partner)
        gather_first(place, wires, 0, (layer, PAIR), slot((layer, PAIR), place.chip), slot)
    halves = ((act_u, q_u), (cot_u, dy_u), (x_u, xh_u), (act_d, q_d), (cot_d, dy_d), (x_d, xh_d))
    for n, (src, dst) in enumerate(halves):
        wires.send(30 + n, src.at[:, other(2048)], dst, place.partner)
    for unit in UNITS:
        gather_second(place, wires, 0, unit, slot, nothing)
    for unit in UNITS:
        gather_third(place, wires, 0, unit, slot, nothing)
    for unit in UNITS:
        gather_last(place, wires, 0, unit, slot, nothing)
    for n, (src, dst) in enumerate(halves):
        wires.arrive(30 + n, dst, place.partner)
    for copy in local:
        copy.wait()
    wires.finish()


def spread(*operands):
    half = jax.ShapeDtypeStruct((128, 2048), BF)
    hbm = pl.BlockSpec(memory_space=pl.ANY)
    return pl.pallas_call(
        spread_kernel,
        in_specs=[hbm] * 6 + [pl.BlockSpec(memory_space=pltpu.VMEM)] * 2,
        out_specs=[hbm] * 8,
        out_shape=[half] * 6 + [jax.ShapeDtypeStruct((16, 128, 512), BF)] * 2,
        scratch_shapes=[pltpu.SemaphoreType.DMA((36,)), pltpu.SemaphoreType.DMA((36,)), pltpu.SemaphoreType.DMA((2,))],
        compiler_params=pltpu.CompilerParams(collective_id=1, has_side_effects=True),
        name="spread",
    )(*operands)


R0, RA, RB, R1, RU, RD, RX = range(7)


HANDED, DQ, GAINS, FAR = 56, 88, 90, 120


def finish_kernel(terms_d, parts_u, dqo_d, dqo_u, dqg_d, dqg_u, x_d, x_u, cot_d, cot_u, act_hbm, weights, gains,
                  grad_d, grad_u, kv_grad, gain_grad,
                  slots, stage, total, all_kv, dquery, weight, dact, gparts, ggot, gsum, acc, wsend, wgot, ggot_far,
                  kept, parts, x_s, cot_s, features, grad_s, send_sem, recv_sem, local_sem):
    place = Place()
    wires = Wires(send_sem, recv_sem)
    mirrored = 7 - lax.axis_index("section")
    chip, chip_x = place.chip, place.chip_x
    local = []

    def keep(src, dst):
        copy = pltpu.make_async_copy(src, dst, local_sem.at[len(local)])
        copy.start()
        local.append(copy)
        return copy

    loads = {}
    loads["terms"], loads["parts"] = keep(terms_d, kept), keep(parts_u, parts)
    place.greet_all(pltpu.get_barrier_semaphore())

    def rows(unit, at):
        return pl.ds(pl.multiple_of(place.span(at, unit[1]) * 128, 128), 128)

    def sent(unit, at):
        return terms_d.at[rows(unit, at)]

    def term(unit, at):
        return kept.at[rows(unit, at)]

    def plus(*refs):
        value = refs[0][...].astype(F32)
        for ref in refs[1:]:
            value = value + ref[...].astype(F32)
        return value.astype(BF)

    def reduce_first(layer):
        for n, unit in enumerate(UNITS):
            if unit[0] == layer:
                at = 7 * n
                wires.send(at + R0, sent(unit, place.up(chip_x, 2)), slots.at[at + R0], place.across)
                wires.send(at + RA, sent(unit, place.up(chip_x, 1)), slots.at[at + RA], place.above)
                wires.send(at + RB, sent(unit, place.up(chip_x, 3)), slots.at[at + RB], place.below)

    def reduce_second(layer):
        for n, unit in enumerate(UNITS):
            if unit[0] == layer:
                at = 7 * n
                wires.arrive(at + R0, slots.at[at + R0], place.across)
                stage[3 * n] = plus(slots.at[at + R0], term(unit, place.up(chip, 2)))
                wires.send(at + R1, stage.at[3 * n], slots.at[at + R1], place.below if unit[1] == OWN else place.above)

    def reduce_direct(layer):
        for n, unit in enumerate(UNITS):
            if unit[0] == layer:
                at = 7 * n
                if unit[1] == OWN:
                    wires.send(at + RD, sent(unit, place.up(chip, 1)), slots.at[at + RD], place.above)
                else:
                    wires.send(at + RU, sent(unit, place.up(chip, 3)), slots.at[at + RU], place.below)

    def reduce_third(layer):
        for n, unit in enumerate(UNITS):
            if unit[0] == layer:
                at = 7 * n
                wires.arrive(at + RA, slots.at[at + RA], place.below)
                wires.arrive(at + RB, slots.at[at + RB], place.above)
                stage[3 * n + 1] = plus(slots.at[at + RA], slots.at[at + RB], term(unit, chip_x))
                wires.send(at + RX, stage.at[3 * n + 1], slots.at[at + RX], place.across)
        for n, unit in enumerate(UNITS):
            if unit[0] == layer:
                at = 7 * n
                if unit[1] == OWN:
                    wires.arrive(at + R1, slots.at[at + R1], place.above)
                    stage[3 * n + 2] = plus(slots.at[at + R1], term(unit, place.up(chip, 3)))
                    wires.send(at + RU, stage.at[3 * n + 2], slots.at[at + RU], place.below)
                else:
                    wires.arrive(at + R1, slots.at[at + R1], place.below)
                    stage[3 * n + 2] = plus(slots.at[at + R1], term(unit, place.up(chip, 1)))
                    wires.send(at + RD, stage.at[3 * n + 2], slots.at[at + RD], place.above)

    def load_rest(layer, own_part, other_part, x_ref, cot_ref):
        wires.send(DQ + layer, other_part, dquery.at[layer, place.core], place.partner)
        loads["rest", layer] = [
            keep(own_part, dquery.at[layer, place.core]), keep(x_ref, x_s.at[layer]), keep(cot_ref, cot_s.at[layer]),
            keep(weights.at[1 if layer == UP else 0, 0], weight.at[layer])]

    slot = lambda unit, at: all_kv.at[unit[0], place.core, place.span(at, unit[1])]
    order = []

    def landed(unit, at):
        ref = slot(unit, at)
        wires.send(HANDED + len(order), ref, ref, place.partner)
        order.append((unit, at))

    def spread_total(n, unit):
        gather_first(place, wires, 28, unit, total.at[n], slot)
        all_kv[unit[0], place.core, place.span(chip, unit[1])] = total[n]
        wires.send(HANDED + len(order), total.at[n], slot(unit, chip), place.partner)
        order.append((unit, chip))

    def reduce_last(layer):
        for n, unit in enumerate(UNITS):
            if unit[0] == layer:
                at = 7 * n
                wires.arrive(at + RX, slots.at[at + RX], place.across)
                wires.arrive(at + RU, slots.at[at + RU], place.above)
                wires.arrive(at + RD, slots.at[at + RD], place.below)
                total[n] = plus(slots.at[at + RX], slots.at[at + RU], slots.at[at + RD], term(unit, chip))
                spread_total(n, unit)

    def add_parts(layer):
        for n, unit in enumerate(UNITS):
            if unit[0] == layer:
                here = pl.ds(pl.multiple_of((place.core if unit[1] == OWN else 1 - place.core) * 128, 128), 128)
                total[n] = plus(*[parts.at[came, here] for came in range(8)])
                spread_total(n, unit)

    waited = set()

    def handed(chosen):
        for n, (unit, at) in enumerate(order):
            if chosen(unit, at) and n not in waited:
                waited.add(n)
                ref = all_kv.at[unit[0], 1 - place.core, place.span(at, 1 - unit[1])]
                wires.arrive(HANDED + n, ref, place.partner)

    def complete(layer, grad_ref):
        handed(lambda unit, at: unit[0] == layer and at is chip)
        for copy in loads["rest", layer]:
            copy.wait()
        wires.arrive(DQ + layer, dquery.at[layer, 1 - place.core], place.partner)
        halves = [all_kv[layer, half, place.me] for half in range(2)]
        dkv = jnp.concatenate([halves[h // 2][:, (h % 2) * 256 + kind * 128:(h % 2) * 256 + kind * 128 + 128]
                               for kind in range(2) for h in range(4)], 1)
        total_sq = jnp.zeros((128, 1), F32)
        for tile in range(8):
            part = x_s[layer, :, tile * 512:(tile + 1) * 512].astype(F32)
            total_sq = total_sq + jnp.sum(part * part, 1, keepdims=True)
        recip = lax.rsqrt(total_sq / 4096 + EPS)

        def first(tile, dots):
            cols = pl.ds(pl.multiple_of(tile * 512, 512), 512)
            normed = x_s[layer, :, cols].astype(F32) * recip
            within = pl.ds(pl.multiple_of(tile % 4 * 512, 512), 512)
            value = dquery[layer, tile // 4, :, within].astype(F32) + lax.dot_general(
                dkv, weight[layer, cols, :], NT, preferred_element_type=F32)
            dact[:, cols] = value
            product = value * normed
            column = jnp.sum(product, 0, keepdims=True)
            for half in range(2):
                gparts[layer, 2 * tile + half] = jnp.broadcast_to(column[:, half * 256:(half + 1) * 256], (8, 256))
            return dots + jnp.sum(product * gains[layer:layer + 1, cols], 1, keepdims=True)

        dots = lax.fori_loop(0, 8, first, jnp.zeros((128, 1), F32))
        for step in range(1, 16):
            to = (place.me + step) % 16
            wires.send(GAINS + 15 * layer + step - 1, gparts.at[layer, to], ggot.at[layer, step], to)
        mean = dots / 4096

        def second(tile, _):
            cols = pl.ds(pl.multiple_of(tile * 512, 512), 512)
            normed = x_s[layer, :, cols].astype(F32) * recip
            dnormed = dact[:, cols] * gains[layer:layer + 1, cols]
            grad_s[layer, :, cols] = (cot_s[layer, :, cols].astype(F32) + recip * (dnormed - normed * mean)).astype(BF)
            return 0

        lax.fori_loop(0, 8, second, 0)
        loads["grad", layer] = keep(grad_s.at[layer], grad_ref)

    def gain_total(layer):
        value = gparts[layer, place.me]
        for step in range(1, 16):
            wires.arrive(GAINS + 15 * layer + step - 1, ggot.at[layer, step], (place.me + step) % 16)
            value = value + ggot[layer, step]
        return value

    def weight_grad(layer):
        acc[...] = jnp.zeros_like(acc)

        def step(n, _):
            two = pl.ds(2 * n, 2)
            act = features[two, layer].reshape(256, 256)
            for half in range(2):
                dkv = all_kv[layer, half, two].reshape(256, 512)
                acc[:, half * 512:(half + 1) * 512] += lax.dot_general(act, dkv, TN, preferred_element_type=F32)
            return 0

        lax.fori_loop(0, 8, step, 0)

    def stage_of(step, layer):
        for unit in UNITS:
            if unit[0] == layer:
                step(place, wires, 28, unit, slot, landed)

    reduce_first(DOWN)
    loads["parts"].wait()
    add_parts(UP)
    loads["terms"].wait()
    load_rest(UP, dqo_u, dqg_u, x_u, cot_u)
    reduce_second(DOWN)
    load_rest(DOWN, dqo_d, dqg_d, x_d, cot_d)
    loads["act"] = keep(act_hbm, features)
    reduce_third(DOWN)
    reduce_direct(DOWN)
    stage_of(gather_second, UP)
    reduce_last(DOWN)
    stage_of(gather_third, UP)
    stage_of(gather_second, DOWN)
    complete(UP, grad_u)
    stage_of(gather_third, DOWN)
    stage_of(gather_last, UP)
    handed(lambda unit, at: unit[0] == UP)
    loads["act"].wait()
    weight_grad(UP)
    wsend[...] = acc[...].astype(BF)
    far_w = wires.far_send(FAR, wsend, wgot, mirrored)
    complete(DOWN, grad_d)
    gsum[...] = gain_total(UP)
    far_g = wires.far_send(FAR + 1, gsum, ggot_far, mirrored)
    stage_of(gather_last, DOWN)
    handed(lambda unit, at: True)
    weight_grad(DOWN)
    mine = gain_total(DOWN)
    far_g.wait_recv()
    gain_grad[...] = mine + ggot_far[...]
    far_w.wait_recv()
    for h in range(4):
        for kind in range(2):
            came = slice(h * 256 + kind * 128, h * 256 + kind * 128 + 128)
            goes = slice(kind * 512 + h * 128, kind * 512 + h * 128 + 128)
            kv_grad[:, goes] = acc[:, came] + wgot[:, came].astype(F32)
    for layer in (UP, DOWN):
        loads["grad", layer].wait()
    wires.finish()


def finish(*operands):
    hbm = pl.BlockSpec(memory_space=pl.ANY)
    vmem = pl.BlockSpec(memory_space=pltpu.VMEM)
    row = jax.ShapeDtypeStruct((128, 4096), BF)
    unit = lambda count: pltpu.VMEM((count, 128, 512), BF)
    return pl.pallas_call(
        finish_kernel,
        in_specs=[hbm] * 12 + [vmem],
        out_specs=[hbm] * 2 + [vmem] * 2,
        out_shape=[row, row, jax.ShapeDtypeStruct((256, 1024), F32), jax.ShapeDtypeStruct((8, 256), F32)],
        scratch_shapes=[unit(28), unit(12), unit(4), pltpu.VMEM((2, 2, 16, 128, 512), BF), pltpu.VMEM((2, 2, 128, 2048), BF),
                        pltpu.VMEM((2, 4096, 1024), BF), pltpu.VMEM((128, 4096), F32), pltpu.VMEM((2, 16, 8, 256), F32),
                        pltpu.VMEM((2, 16, 8, 256), F32), pltpu.VMEM((8, 256), F32), pltpu.VMEM((256, 1024), F32),
                        pltpu.VMEM((256, 1024), BF), pltpu.VMEM((256, 1024), BF), pltpu.VMEM((8, 256), F32),
                        pltpu.VMEM((2048, 512), BF), pltpu.VMEM((8, 256, 512), BF), pltpu.VMEM((2, 128, 4096), BF), pltpu.VMEM((2, 128, 4096), BF),
                        pltpu.VMEM((16, 2, 128, 256), BF), pltpu.VMEM((2, 128, 4096), BF),
                        pltpu.SemaphoreType.DMA((122,)), pltpu.SemaphoreType.DMA((122,)), pltpu.SemaphoreType.DMA((13,))],
        compiler_params=pltpu.CompilerParams(collective_id=2, has_side_effects=True, vmem_limit_bytes=60 << 20),
        name="finish",
    )(*operands)


def by_head(kv):
    return kv.reshape(-1, 2, 4, 128).transpose(0, 2, 1, 3).reshape(-1, 1024)


def prepare(x, gain, weight):
    xf = x.astype(F32)
    recip = lax.rsqrt(jnp.mean(xf * xf, -1, keepdims=True) + EPS)
    normed = xf * recip
    act = (normed * gain[None, :]).astype(BF)
    kv = jnp.dot(act, weight, preferred_element_type=F32).astype(BF)
    return act, by_head(kv)


def halves_joined(core, mine, other):
    both = jnp.concatenate([other, other], 1)
    return lax.dynamic_update_slice(both, mine, (0, core * mine.shape[1]))


def relayed(own, got, by):
    sections, spans = lax.axis_size("section"), lax.axis_size("ctx")
    to = lambda flip: [(s * spans + i, (s + by) % sections * spans + (i ^ flip)) for s in range(sections) for i in range(spans)]
    mine = lax.ppermute(own, ("section", "ctx"), to(0))
    other = lax.ppermute(got, ("section", "ctx"), to(1))
    return mine, other


def per_device(down_in, up_in, down_cot, up_cot, kv_weight, norm_gain, span_ids):
    own = lax.axis_index("ctx")
    core = own % 2
    x_d, x_u, cot_d, cot_u = down_in[0], up_in[0], down_cot[0], up_cot[0]
    gain_d, gain_u = norm_gain[0, 0], norm_gain[1, 0]
    weight_d, weight_u = kv_weight[0, 0], kv_weight[1, 0]
    scalars = jnp.stack([span_ids[own], span_ids[own + 1 - 2 * core], core]).astype(jnp.int32)
    order = jnp.arange(16, dtype=jnp.int32)
    inverse = jnp.sum(jnp.where(span_ids[:, None] == order[None, :], order[:, None], 0), 0).astype(jnp.int32)
    act_u, kv_u = prepare(x_u, gain_u, weight_u)
    act_d, kv_d = prepare(x_d, gain_d, weight_d)
    q_d, q_u, dy_d, dy_u, xh_d, xh_u, all_d, all_u = spread(act_d, act_u, cot_d, cot_u, x_d, x_u, kv_d, kv_u)
    after_d, after_u, _ = lax.optimization_barrier((act_d, act_u, q_d))
    features = jnp.stack([after_d, after_u]).reshape(2, 128, 16, 256).transpose(2, 0, 1, 3)
    features = lax.all_to_all(features, "ctx", 0, 0, tiled=False)
    yo_u, yg_u, dqo_u, dqg_u, terms_u = attention((act_u, q_u), (cot_u, dy_u), (x_u, xh_u), all_u, scalars, inverse)
    same_core = [list(range(c, 16, 2)) for c in range(2)]
    parts_u = lax.all_to_all(terms_u.reshape(8, 256, 512), "ctx", 0, 0, axis_index_groups=same_core, tiled=False)
    up_halves = relayed(yo_u, yg_u, -1)
    yo_d, yg_d, dqo_d, dqg_d, terms_d = attention((act_d, q_d), (cot_d, dy_d), (x_d, xh_d), all_d, scalars, inverse)
    down_halves = relayed(yo_d, yg_d, 1)
    grad_d, grad_u, kv_grad, gain_grad = finish(
        terms_d, parts_u, dqo_d, dqo_u, dqg_d, dqg_u, x_d, x_u, cot_d, cot_u, features, kv_weight, norm_gain[:, 0])
    down_halves, up_halves, gain_grad = lax.optimization_barrier((down_halves, up_halves, gain_grad))
    down_out, up_out = halves_joined(core, *down_halves), halves_joined(core, *up_halves)
    return (down_out[None], up_out[None], grad_d[None], grad_u[None], kv_grad[None], gain_grad[:1])


def solution(mesh):
    row = P("section", "ctx", None)
    in_specs = (row, row, row, row, P(None, "section", None, None), P(None, "section", None), P())
    out_specs = (row, row, row, row, row, P("section", "ctx"))
    return jax.shard_map(per_device, mesh=mesh, in_specs=in_specs, out_specs=out_specs, check_vma=False)
```

```python
import functools

import jax
import jax.numpy as jnp
from jax import lax
from jax.experimental import pallas as pl
from jax.experimental.pallas import tpu as pltpu
from jax.sharding import PartitionSpec as P

LOG2E = 1.4426950408889634
NT = (((1,), (1,)), ((), ()))
TN = (((0,), (0,)), ((), ()))
F32 = jnp.float32
BF = jnp.bfloat16


def stack_heads(block):
    return jnp.concatenate([block[:, j * 128:(j + 1) * 128] for j in range(8)], 0)


def spread_heads(rows):
    return jnp.concatenate([rows[j * 128:(j + 1) * 128] for j in range(8)], 1)


def attention_kernel(block, small, tq_ref, inv_ref, q_own, q_got, dy_own, dy_got, x_own, x_got, kv_hbm,
                     y_own, y_got, dq_own, dq_got, terms_ref, kv_s, dk_s, dv_s, e_s, top_s, sems):
    head = pl.program_id(0)
    spans = kv_hbm.shape[0]
    heads = kv_hbm.shape[2] // 256
    scale = 128 ** -0.5
    c = scale * LOG2E

    def load(h, t):
        return pltpu.make_async_copy(kv_hbm.at[inv_ref[t], :, pl.ds(h * 256, 256)],
                                     kv_s.at[h, pl.ds(t * 128, 128)], sems.at[h, t])

    @pl.when(head == 0)
    def _():
        for h in range(heads):
            for t in range(spans):
                load(h, t).start()

    for h in range(heads):
        @pl.when(head == h)
        def _():
            for t in range(spans):
                load(h, t).wait()

    dk_s[...] = jnp.zeros_like(dk_s)
    dv_s[...] = jnp.zeros_like(dv_s)

    def span(qi, q_ref, dy_ref, x_ref, y_ref, dq_ref):
        t = tq_ref[qi]
        q = stack_heads(q_ref[...])
        dy = stack_heads(dy_ref[...])
        rows = q.shape[0]
        blocks = (t * 128) // block
        short = t * 128 + 128 - blocks * block <= small

        def forward(b, size, masked, carry):
            m, l, acc = carry
            at = pl.multiple_of(b * block, block)
            k = kv_s[head, pl.ds(at, size), 0:128]
            v = kv_s[head, pl.ds(at, size), 128:256]
            s = lax.dot_general(k, q, NT, preferred_element_type=F32)
            if masked:
                kpos = at + lax.broadcasted_iota(jnp.int32, (size, 128), 0)
                qpos = t * 128 + lax.broadcasted_iota(jnp.int32, (size, 128), 1)
                visible = kpos <= qpos
                s = jnp.concatenate([jnp.where(visible, s[:, j * 128:(j + 1) * 128], -1e30) for j in range(8)], 1)
            m_new = jnp.maximum(m, jnp.max(s, 0, keepdims=True))
            e = jnp.exp2((s - m_new) * c)
            fade = jnp.exp2((m - m_new) * c)
            rounded = e.astype(BF)
            e_s[pl.ds(at, size), :] = rounded
            top_s[b] = jnp.broadcast_to(m_new, (8, rows))
            l = l * fade + jnp.sum(e, 0, keepdims=True)
            acc = acc * fade + lax.dot_general(v, rounded, TN, preferred_element_type=F32)
            return m_new, l, acc

        def over_blocks(step, carry):
            carry = lax.fori_loop(0, blocks, lambda b, cr: step(b, block, False, cr), carry)
            return lax.cond(short, lambda cr: step(blocks, small, True, cr), lambda cr: step(blocks, block, True, cr), carry)

        start = (jnp.full((1, rows), -1e30, F32), jnp.zeros((1, rows), F32), jnp.zeros((128, rows), F32))
        m, l, acc = over_blocks(forward, start)
        mixed = acc / l
        delta = jnp.sum(jnp.transpose(dy.astype(F32)) * mixed, 0, keepdims=True)
        y_ref[...] = (x_ref[...].astype(F32) + spread_heads(jnp.transpose(mixed))).astype(y_ref.dtype)

        def backward(b, size, masked, dq):
            at = pl.multiple_of(b * block, block)
            k = kv_s[head, pl.ds(at, size), 0:128]
            v = kv_s[head, pl.ds(at, size), 128:256]
            p = e_s[pl.ds(at, size), :].astype(F32) * (jnp.exp2((top_s[b, 0:1] - m) * c) / l)
            dp = lax.dot_general(v, dy, NT, preferred_element_type=F32)
            ds = (p * (dp - delta)).astype(BF)
            dv_s[pl.ds(at, size)] += jnp.dot(p.astype(BF), dy, preferred_element_type=F32)
            dk_s[pl.ds(at, size)] += jnp.dot(ds, q, preferred_element_type=F32)
            return dq + lax.dot_general(k, ds, TN, preferred_element_type=F32)

        dq = over_blocks(backward, jnp.zeros((128, rows), F32))
        dq_ref[...] = spread_heads(jnp.transpose(dq * scale)).astype(dq_ref.dtype)

    span(0, q_own, dy_own, x_own, y_own, dq_own)
    span(1, q_got, dy_got, x_got, y_got, dq_got)
    for t in range(spans):
        at = pl.ds(pl.multiple_of(inv_ref[t] * 128, 128), 128)
        terms_ref[at, 0:128] = (dk_s[t * 128:(t + 1) * 128] * scale).astype(BF)
        terms_ref[at, 128:256] = dv_s[t * 128:(t + 1) * 128].astype(BF)


def attention(q, dy, x, kv, tq, inv, block=1024, small=512):
    spans = kv.shape[0]
    count = kv.shape[2] // 256
    own = pl.BlockSpec((128, 1024), lambda h, tq, inv: (0, tq[2] * count + h))
    got = pl.BlockSpec((128, 1024), lambda h, tq, inv: (0, h))
    flops = 2 * 7 * 2 * count * 1024 * spans * 128 * 128
    rows = jax.ShapeDtypeStruct((128, count * 1024), BF)
    return pl.pallas_call(
        functools.partial(attention_kernel, block, small),
        grid_spec=pltpu.PrefetchScalarGridSpec(
            num_scalar_prefetch=2,
            grid=(count,),
            in_specs=[own, got] * 3 + [pl.BlockSpec(memory_space=pl.ANY)],
            out_specs=[got] * 4 + [pl.BlockSpec((spans * 128, 256), lambda h, tq, inv: (0, h))],
            scratch_shapes=[pltpu.VMEM((count, spans * 128, 256), BF), pltpu.VMEM((spans * 128, 128), F32),
                            pltpu.VMEM((spans * 128, 128), F32), pltpu.VMEM((spans * 128, 1024), BF),
                            pltpu.VMEM((spans * 128 // block, 8, 1024), F32), pltpu.SemaphoreType.DMA((count, spans))],
        ),
        out_shape=[rows] * 4 + [jax.ShapeDtypeStruct((spans * 128, count * 256), BF)],
        compiler_params=pltpu.CompilerParams(vmem_limit_bytes=60 << 20),
        cost_estimate=pl.CostEstimate(flops=flops, bytes_accessed=16 << 20, transcendentals=0),
        name="attention",
    )(tq, inv, *q, *dy, *x, kv)


MESH_ID = pl.DeviceIdType.MESH
EPS = 1e-05
DOWN, UP = 0, 1
OWN, PAIR = 0, 1
UNITS = [(UP, OWN), (UP, PAIR), (DOWN, OWN), (DOWN, PAIR)]


class Place:
    def __init__(self):
        self.me = lax.axis_index("ctx")
        self.core = self.me % 2
        self.chip = self.me // 2
        beside = self.chip % 2
        self.partner = self.me + 1 - 2 * self.core
        self.across = self.me + 2 - 4 * beside
        self.above = (self.me + 4) % 16
        self.below = (self.me + 12) % 16
        self.chip_x = self.chip + 1 - 2 * beside

    def greet_all(self, barrier):
        for step in range(1, 16):
            pl.semaphore_signal(barrier, inc=1, device_id={"ctx": (self.me + step) % 16}, device_id_type=MESH_ID)
        mirrored = 7 - lax.axis_index("section")
        pl.semaphore_signal(barrier, inc=1, device_id={"section": mirrored}, device_id_type=MESH_ID)
        pl.semaphore_wait(barrier, 16)

    def greet(self, barrier):
        for dev in (self.partner, self.across, self.above, self.below):
            pl.semaphore_signal(barrier, inc=1, device_id={"ctx": dev}, device_id_type=MESH_ID)
        pl.semaphore_wait(barrier, 4)

    def span(self, chip, kind):
        return 2 * chip + (self.core if kind == OWN else 1 - self.core)

    def up(self, chip, by):
        return (chip + 2 * by) % 8


class Wires:
    def __init__(self, send_sem, recv_sem):
        self.send_sem, self.recv_sem, self.started = send_sem, recv_sem, []

    def copy(self, index, src, dst, dev):
        return pltpu.make_async_remote_copy(
            src_ref=src, dst_ref=dst, send_sem=self.send_sem.at[index], recv_sem=self.recv_sem.at[index],
            device_id={"ctx": dev}, device_id_type=MESH_ID)

    def send(self, index, src, dst, dev):
        copy = self.copy(index, src, dst, dev)
        copy.start()
        self.started.append(copy)

    def far_send(self, index, src, dst, section):
        copy = pltpu.make_async_remote_copy(
            src_ref=src, dst_ref=dst, send_sem=self.send_sem.at[index], recv_sem=self.recv_sem.at[index],
            device_id={"section": section}, device_id_type=MESH_ID)
        copy.start()
        self.started.append(copy)
        return copy

    def arrive(self, index, ref, dev):
        self.copy(index, ref, ref, dev).wait_recv()

    def finish(self):
        for copy in self.started:
            copy.wait_send()


X, ZM, ZP, XZM, XZP, AN, XA = range(7)


def gather_first(place, wires, base, unit, src, slot):
    kind = unit[1]
    at = base + 7 * UNITS.index(unit)
    here = slot(unit, place.chip)
    wires.send(at + X, src, here, place.across)
    wires.send(at + ZM, src, here, place.above)
    wires.send(at + ZP, src, here, place.below)


def gather_second(place, wires, base, unit, slot, landed):
    at = base + 7 * UNITS.index(unit)
    lo, hi = slot(unit, place.up(place.chip, 3)), slot(unit, place.up(place.chip, 1))
    wires.arrive(at + ZM, lo, place.below)
    if unit[1] == OWN:
        wires.send(at + AN, lo, lo, place.above)
    wires.arrive(at + ZP, hi, place.above)
    if unit[1] == PAIR:
        wires.send(at + AN, hi, hi, place.below)
    landed(unit, place.up(place.chip, 3))
    landed(unit, place.up(place.chip, 1))


def gather_third(place, wires, base, unit, slot, landed):
    at = base + 7 * UNITS.index(unit)
    far = slot(unit, place.up(place.chip, 2))
    wires.arrive(at + AN, far, place.below if unit[1] == OWN else place.above)
    wires.send(at + XA, far, far, place.across)
    cx = slot(unit, place.chip_x)
    wires.arrive(at + X, cx, place.across)
    wires.send(at + XZM, cx, cx, place.above)
    wires.send(at + XZP, cx, cx, place.below)
    landed(unit, place.up(place.chip, 2))
    landed(unit, place.chip_x)


def gather_last(place, wires, base, unit, slot, landed):
    at = base + 7 * UNITS.index(unit)
    for kind, by, dev in ((XZM, 3, place.below), (XZP, 1, place.above), (XA, 2, place.across)):
        chip = place.up(place.chip_x, by)
        wires.arrive(at + kind, slot(unit, chip), dev)
        landed(unit, chip)


def nothing(unit, chip):
    pass


def spread_kernel(act_d, act_u, cot_d, cot_u, x_d, x_u, kv_d, kv_u,
                  q_d, q_u, dy_d, dy_u, xh_d, xh_u, all_d, all_u, kv, send_sem, recv_sem, local_sem):
    place = Place()
    wires = Wires(send_sem, recv_sem)
    for layer, source in ((UP, kv_u), (DOWN, kv_d)):
        for h in range(4):
            for kind in range(2):
                kv[layer, :, (2 * h + kind) * 128:(2 * h + kind + 1) * 128] = (
                    source[:, kind * 512 + h * 128:kind * 512 + (h + 1) * 128])
    place.greet(pltpu.get_barrier_semaphore())
    all_kv = (all_d, all_u)
    mine = pl.ds(pl.multiple_of(place.core * 512, 512), 512)
    other = lambda width: pl.ds(pl.multiple_of((1 - place.core) * width, width), width)
    slot = lambda unit, chip: all_kv[unit[0]].at[place.span(chip, unit[1])]
    local = []
    for layer in (UP, DOWN):
        wires.send(28 + layer, kv.at[layer, :, other(512)], all_kv[layer].at[place.me], place.partner)
    for layer in (UP, DOWN):
        gather_first(place, wires, 0, (layer, OWN), kv.at[layer, :, mine], slot)
        copy = pltpu.make_async_copy(kv.at[layer, :, mine], all_kv[layer].at[place.me], local_sem.at[layer])
        copy.start()
        local.append(copy)
    for layer in (UP, DOWN):
        wires.arrive(28 + layer, all_kv[layer].at[place.partner], place.partner)
        gather_first(place, wires, 0, (layer, PAIR), slot((layer, PAIR), place.chip), slot)
    halves = ((act_u, q_u), (cot_u, dy_u), (x_u, xh_u), (act_d, q_d), (cot_d, dy_d), (x_d, xh_d))
    for n, (src, dst) in enumerate(halves):
        wires.send(30 + n, src.at[:, other(2048)], dst, place.partner)
    for unit in UNITS:
        gather_second(place, wires, 0, unit, slot, nothing)
    for unit in UNITS:
        gather_third(place, wires, 0, unit, slot, nothing)
    for unit in UNITS:
        gather_last(place, wires, 0, unit, slot, nothing)
    for n, (src, dst) in enumerate(halves):
        wires.arrive(30 + n, dst, place.partner)
    for copy in local:
        copy.wait()
    wires.finish()


def spread(*operands):
    half = jax.ShapeDtypeStruct((128, 2048), BF)
    hbm = pl.BlockSpec(memory_space=pl.ANY)
    return pl.pallas_call(
        spread_kernel,
        in_specs=[hbm] * 6 + [pl.BlockSpec(memory_space=pltpu.VMEM)] * 2,
        out_specs=[hbm] * 8,
        out_shape=[half] * 6 + [jax.ShapeDtypeStruct((16, 128, 512), BF)] * 2,
        scratch_shapes=[pltpu.VMEM((2, 128, 1024), BF), pltpu.SemaphoreType.DMA((36,)), pltpu.SemaphoreType.DMA((36,)), pltpu.SemaphoreType.DMA((2,))],
        compiler_params=pltpu.CompilerParams(collective_id=1, has_side_effects=True),
        name="spread",
    )(*operands)


R0, RA, RB, R1, RU, RD, RX = range(7)


HANDED, DQ, GAINS, FAR = 56, 88, 90, 120


def finish_kernel(terms_d, parts_u, dqo_d, dqo_u, dqg_d, dqg_u, x_d, x_u, cot_d, cot_u, act_hbm, weights, gains,
                  grad_d, grad_u, kv_grad, gain_grad,
                  slots, stage, total, all_kv, dquery, weight, dact, gparts, ggot, gsum, acc, wsend, wgot, ggot_far,
                  kept, parts, x_s, cot_s, features, grad_s, send_sem, recv_sem, local_sem):
    place = Place()
    wires = Wires(send_sem, recv_sem)
    mirrored = 7 - lax.axis_index("section")
    chip, chip_x = place.chip, place.chip_x
    local = []

    def keep(src, dst):
        copy = pltpu.make_async_copy(src, dst, local_sem.at[len(local)])
        copy.start()
        local.append(copy)
        return copy

    loads = {}
    loads["terms"], loads["parts"] = keep(terms_d, kept), keep(parts_u, parts)
    place.greet_all(pltpu.get_barrier_semaphore())

    def rows(unit, at):
        return pl.ds(pl.multiple_of(place.span(at, unit[1]) * 128, 128), 128)

    def sent(unit, at):
        return terms_d.at[rows(unit, at)]

    def term(unit, at):
        return kept.at[rows(unit, at)]

    def plus(*refs):
        value = refs[0][...].astype(F32)
        for ref in refs[1:]:
            value = value + ref[...].astype(F32)
        return value.astype(BF)

    def reduce_first(layer):
        for n, unit in enumerate(UNITS):
            if unit[0] == layer:
                at = 7 * n
                wires.send(at + R0, sent(unit, place.up(chip_x, 2)), slots.at[at + R0], place.across)
                wires.send(at + RA, sent(unit, place.up(chip_x, 1)), slots.at[at + RA], place.above)
                wires.send(at + RB, sent(unit, place.up(chip_x, 3)), slots.at[at + RB], place.below)

    def reduce_second(layer):
        for n, unit in enumerate(UNITS):
            if unit[0] == layer:
                at = 7 * n
                wires.arrive(at + R0, slots.at[at + R0], place.across)
                stage[3 * n] = plus(slots.at[at + R0], term(unit, place.up(chip, 2)))
                wires.send(at + R1, stage.at[3 * n], slots.at[at + R1], place.below if unit[1] == OWN else place.above)

    def reduce_direct(layer):
        for n, unit in enumerate(UNITS):
            if unit[0] == layer:
                at = 7 * n
                if unit[1] == OWN:
                    wires.send(at + RD, sent(unit, place.up(chip, 1)), slots.at[at + RD], place.above)
                else:
                    wires.send(at + RU, sent(unit, place.up(chip, 3)), slots.at[at + RU], place.below)

    def reduce_third(layer):
        for n, unit in enumerate(UNITS):
            if unit[0] == layer:
                at = 7 * n
                wires.arrive(at + RA, slots.at[at + RA], place.below)
                wires.arrive(at + RB, slots.at[at + RB], place.above)
                stage[3 * n + 1] = plus(slots.at[at + RA], slots.at[at + RB], term(unit, chip_x))
                wires.send(at + RX, stage.at[3 * n + 1], slots.at[at + RX], place.across)
        for n, unit in enumerate(UNITS):
            if unit[0] == layer:
                at = 7 * n
                if unit[1] == OWN:
                    wires.arrive(at + R1, slots.at[at + R1], place.above)
                    stage[3 * n + 2] = plus(slots.at[at + R1], term(unit, place.up(chip, 3)))
                    wires.send(at + RU, stage.at[3 * n + 2], slots.at[at + RU], place.below)
                else:
                    wires.arrive(at + R1, slots.at[at + R1], place.below)
                    stage[3 * n + 2] = plus(slots.at[at + R1], term(unit, place.up(chip, 1)))
                    wires.send(at + RD, stage.at[3 * n + 2], slots.at[at + RD], place.above)

    def load_rest(layer, own_part, other_part, x_ref, cot_ref):
        wires.send(DQ + layer, other_part, dquery.at[layer, place.core], place.partner)
        loads["rest", layer] = [
            keep(own_part, dquery.at[layer, place.core]), keep(x_ref, x_s.at[layer]), keep(cot_ref, cot_s.at[layer]),
            keep(weights.at[1 if layer == UP else 0, 0], weight.at[layer])]

    slot = lambda unit, at: all_kv.at[unit[0], place.core, place.span(at, unit[1])]
    order = []

    def landed(unit, at):
        ref = slot(unit, at)
        wires.send(HANDED + len(order), ref, ref, place.partner)
        order.append((unit, at))

    def spread_total(n, unit):
        gather_first(place, wires, 28, unit, total.at[n], slot)
        all_kv[unit[0], place.core, place.span(chip, unit[1])] = total[n]
        wires.send(HANDED + len(order), total.at[n], slot(unit, chip), place.partner)
        order.append((unit, chip))

    def reduce_last(layer):
        for n, unit in enumerate(UNITS):
            if unit[0] == layer:
                at = 7 * n
                wires.arrive(at + RX, slots.at[at + RX], place.across)
                wires.arrive(at + RU, slots.at[at + RU], place.above)
                wires.arrive(at + RD, slots.at[at + RD], place.below)
                total[n] = plus(slots.at[at + RX], slots.at[at + RU], slots.at[at + RD], term(unit, chip))
                spread_total(n, unit)

    def add_parts(layer):
        for n, unit in enumerate(UNITS):
            if unit[0] == layer:
                here = pl.ds(pl.multiple_of((place.core if unit[1] == OWN else 1 - place.core) * 128, 128), 128)
                total[n] = plus(*[parts.at[came, here] for came in range(8)])
                spread_total(n, unit)

    waited = set()

    def handed(chosen):
        for n, (unit, at) in enumerate(order):
            if chosen(unit, at) and n not in waited:
                waited.add(n)
                ref = all_kv.at[unit[0], 1 - place.core, place.span(at, 1 - unit[1])]
                wires.arrive(HANDED + n, ref, place.partner)

    def complete(layer, grad_ref):
        handed(lambda unit, at: unit[0] == layer and at is chip)
        for copy in loads["rest", layer]:
            copy.wait()
        wires.arrive(DQ + layer, dquery.at[layer, 1 - place.core], place.partner)
        halves = [all_kv[layer, half, place.me] for half in range(2)]
        dkv = jnp.concatenate([halves[h // 2][:, (h % 2) * 256 + kind * 128:(h % 2) * 256 + kind * 128 + 128]
                               for kind in range(2) for h in range(4)], 1)
        total_sq = jnp.zeros((128, 1), F32)
        for tile in range(8):
            part = x_s[layer, :, tile * 512:(tile + 1) * 512].astype(F32)
            total_sq = total_sq + jnp.sum(part * part, 1, keepdims=True)
        recip = lax.rsqrt(total_sq / 4096 + EPS)

        def first(tile, dots):
            cols = pl.ds(pl.multiple_of(tile * 512, 512), 512)
            normed = x_s[layer, :, cols].astype(F32) * recip
            within = pl.ds(pl.multiple_of(tile % 4 * 512, 512), 512)
            value = dquery[layer, tile // 4, :, within].astype(F32) + lax.dot_general(
                dkv, weight[layer, cols, :], NT, preferred_element_type=F32)
            dact[:, cols] = value
            product = value * normed
            column = jnp.sum(product, 0, keepdims=True)
            for half in range(2):
                gparts[layer, 2 * tile + half] = jnp.broadcast_to(column[:, half * 256:(half + 1) * 256], (8, 256))
            return dots + jnp.sum(product * gains[layer:layer + 1, cols], 1, keepdims=True)

        dots = lax.fori_loop(0, 8, first, jnp.zeros((128, 1), F32))
        for step in range(1, 16):
            to = (place.me + step) % 16
            wires.send(GAINS + 15 * layer + step - 1, gparts.at[layer, to], ggot.at[layer, step], to)
        mean = dots / 4096

        def second(tile, _):
            cols = pl.ds(pl.multiple_of(tile * 512, 512), 512)
            normed = x_s[layer, :, cols].astype(F32) * recip
            dnormed = dact[:, cols] * gains[layer:layer + 1, cols]
            grad_s[layer, :, cols] = (cot_s[layer, :, cols].astype(F32) + recip * (dnormed - normed * mean)).astype(BF)
            return 0

        lax.fori_loop(0, 8, second, 0)
        loads["grad", layer] = keep(grad_s.at[layer], grad_ref)

    def gain_total(layer):
        value = gparts[layer, place.me]
        for step in range(1, 16):
            wires.arrive(GAINS + 15 * layer + step - 1, ggot.at[layer, step], (place.me + step) % 16)
            value = value + ggot[layer, step]
        return value

    def weight_grad(layer):
        acc[...] = jnp.zeros_like(acc)

        def step(n, _):
            two = pl.ds(2 * n, 2)
            act = features[two, layer].reshape(256, 256)
            for half in range(2):
                dkv = all_kv[layer, half, two].reshape(256, 512)
                acc[:, half * 512:(half + 1) * 512] += lax.dot_general(act, dkv, TN, preferred_element_type=F32)
            return 0

        lax.fori_loop(0, 8, step, 0)

    def stage_of(step, layer):
        for unit in UNITS:
            if unit[0] == layer:
                step(place, wires, 28, unit, slot, landed)

    reduce_first(DOWN)
    loads["parts"].wait()
    add_parts(UP)
    loads["terms"].wait()
    load_rest(UP, dqo_u, dqg_u, x_u, cot_u)
    reduce_second(DOWN)
    load_rest(DOWN, dqo_d, dqg_d, x_d, cot_d)
    loads["act"] = keep(act_hbm, features)
    reduce_third(DOWN)
    reduce_direct(DOWN)
    stage_of(gather_second, UP)
    reduce_last(DOWN)
    stage_of(gather_third, UP)
    stage_of(gather_second, DOWN)
    complete(UP, grad_u)
    stage_of(gather_third, DOWN)
    stage_of(gather_last, UP)
    handed(lambda unit, at: unit[0] == UP)
    loads["act"].wait()
    weight_grad(UP)
    wsend[...] = acc[...].astype(BF)
    far_w = wires.far_send(FAR, wsend, wgot, mirrored)
    complete(DOWN, grad_d)
    gsum[...] = gain_total(UP)
    far_g = wires.far_send(FAR + 1, gsum, ggot_far, mirrored)
    stage_of(gather_last, DOWN)
    handed(lambda unit, at: True)
    weight_grad(DOWN)
    mine = gain_total(DOWN)
    far_g.wait_recv()
    gain_grad[...] = (mine + ggot_far[...])[0:1]
    far_w.wait_recv()
    for h in range(4):
        for kind in range(2):
            came = slice(h * 256 + kind * 128, h * 256 + kind * 128 + 128)
            goes = slice(kind * 512 + h * 128, kind * 512 + h * 128 + 128)
            kv_grad[:, goes] = acc[:, came] + wgot[:, came].astype(F32)
    for layer in (UP, DOWN):
        loads["grad", layer].wait()
    wires.finish()


def finish(*operands):
    hbm = pl.BlockSpec(memory_space=pl.ANY)
    vmem = pl.BlockSpec(memory_space=pltpu.VMEM)
    row = jax.ShapeDtypeStruct((128, 4096), BF)
    unit = lambda count: pltpu.VMEM((count, 128, 512), BF)
    return pl.pallas_call(
        finish_kernel,
        in_specs=[hbm] * 12 + [vmem],
        out_specs=[hbm] * 2 + [vmem] * 2,
        out_shape=[row, row, jax.ShapeDtypeStruct((256, 1024), F32), jax.ShapeDtypeStruct((1, 256), F32)],
        scratch_shapes=[unit(28), unit(12), unit(4), pltpu.VMEM((2, 2, 16, 128, 512), BF), pltpu.VMEM((2, 2, 128, 2048), BF),
                        pltpu.VMEM((2, 4096, 1024), BF), pltpu.VMEM((128, 4096), F32), pltpu.VMEM((2, 16, 8, 256), F32),
                        pltpu.VMEM((2, 16, 8, 256), F32), pltpu.VMEM((8, 256), F32), pltpu.VMEM((256, 1024), F32),
                        pltpu.VMEM((256, 1024), BF), pltpu.VMEM((256, 1024), BF), pltpu.VMEM((8, 256), F32),
                        pltpu.VMEM((2048, 512), BF), pltpu.VMEM((8, 256, 512), BF), pltpu.VMEM((2, 128, 4096), BF), pltpu.VMEM((2, 128, 4096), BF),
                        pltpu.VMEM((16, 2, 128, 256), BF), pltpu.VMEM((2, 128, 4096), BF),
                        pltpu.SemaphoreType.DMA((122,)), pltpu.SemaphoreType.DMA((122,)), pltpu.SemaphoreType.DMA((13,))],
        compiler_params=pltpu.CompilerParams(collective_id=2, has_side_effects=True, vmem_limit_bytes=60 << 20),
        name="finish",
    )(*operands)


def prepare(x, gain, weight):
    xf = x.astype(F32)
    recip = lax.rsqrt(jnp.mean(xf * xf, -1, keepdims=True) + EPS)
    normed = xf * recip
    act = (normed * gain[None, :]).astype(BF)
    kv = jnp.dot(act, weight, preferred_element_type=F32).astype(BF)
    return act, kv


def halves_joined(core, mine, other):
    both = jnp.concatenate([other, other], 1)
    return lax.dynamic_update_slice(both, mine, (0, core * mine.shape[1]))


def relayed(own, got, by):
    sections, spans = lax.axis_size("section"), lax.axis_size("ctx")
    to = lambda flip: [(s * spans + i, (s + by) % sections * spans + (i ^ flip)) for s in range(sections) for i in range(spans)]
    mine = lax.ppermute(own, ("section", "ctx"), to(0))
    other = lax.ppermute(got, ("section", "ctx"), to(1))
    return mine, other


def per_device(down_in, up_in, down_cot, up_cot, kv_weight, norm_gain, span_ids):
    own = lax.axis_index("ctx")
    core = own % 2
    x_d, x_u, cot_d, cot_u = down_in[0], up_in[0], down_cot[0], up_cot[0]
    gain_d, gain_u = norm_gain[0, 0], norm_gain[1, 0]
    weight_d, weight_u = kv_weight[0, 0], kv_weight[1, 0]
    scalars = jnp.stack([span_ids[own], span_ids[own + 1 - 2 * core], core]).astype(jnp.int32)
    order = jnp.arange(16, dtype=jnp.int32)
    inverse = jnp.sum(jnp.where(span_ids[:, None] == order[None, :], order[:, None], 0), 0).astype(jnp.int32)
    act_u, kv_u = prepare(x_u, gain_u, weight_u)
    act_d, kv_d = prepare(x_d, gain_d, weight_d)
    gains, act_d, act_u = lax.optimization_barrier((jnp.stack([gain_d, gain_u]), act_d, act_u))
    q_d, q_u, dy_d, dy_u, xh_d, xh_u, all_d, all_u = spread(act_d, act_u, cot_d, cot_u, x_d, x_u, kv_d, kv_u)
    after_d, after_u, _ = lax.optimization_barrier((act_d, act_u, q_d))
    features = jnp.stack([after_d, after_u]).reshape(2, 128, 16, 256).transpose(2, 0, 1, 3)
    features = lax.all_to_all(features, "ctx", 0, 0, tiled=False)
    yo_u, yg_u, dqo_u, dqg_u, terms_u = attention((act_u, q_u), (cot_u, dy_u), (x_u, xh_u), all_u, scalars, inverse)
    features, terms_u = lax.optimization_barrier((features, terms_u))
    same_core = [list(range(c, 16, 2)) for c in range(2)]
    parts_u = lax.all_to_all(terms_u.reshape(8, 256, 512), "ctx", 0, 0, axis_index_groups=same_core, tiled=False)
    up_halves = relayed(yo_u, yg_u, -1)
    yo_d, yg_d, dqo_d, dqg_d, terms_d = attention((act_d, q_d), (cot_d, dy_d), (x_d, xh_d), all_d, scalars, inverse)
    down_halves = relayed(yo_d, yg_d, 1)
    grad_d, grad_u, kv_grad, gain_grad = finish(
        terms_d, parts_u, dqo_d, dqo_u, dqg_d, dqg_u, x_d, x_u, cot_d, cot_u, features, kv_weight, gains)
    down_halves, up_halves, gain_grad = lax.optimization_barrier((down_halves, up_halves, gain_grad))
    down_out, up_out = halves_joined(core, *down_halves), halves_joined(core, *up_halves)
    return (down_out[None], up_out[None], grad_d[None], grad_u[None], kv_grad[None], gain_grad)


def solution(mesh):
    row = P("section", "ctx", None)
    in_specs = (row, row, row, row, P(None, "section", None, None), P(None, "section", None), P())
    out_specs = (row, row, row, row, row, P("section", "ctx"))
    return jax.shard_map(per_device, mesh=mesh, in_specs=in_specs, out_specs=out_specs, check_vma=False)
```
